256 devices in a mesh: dp: 64 (over y, z, core), mp: 4 (over x).
Axes of the slice: x: 4, y: 4, z: 8, core: 2. Of those that a mesh axis runs over, the one named last changes fastest.
Arguments:
- cand_item: int32 [512, 128], P(('dp', 'mp')), may hold values from 0 to 131071, as said below
- list_place: int32 [512], replicated, may hold values from 0 to 511, as said below
- item_table: bfloat16 [131072, 768], P('dp', 'mp'), may hold values from -6 to 6
- query_vec: bfloat16 [512, 768], P(('dp', 'mp')), may hold values from -1.796875 to 1.796875
- labels: int32 [512, 128], P(('dp', 'mp')), may hold values from 0 to 4
- query_weight: bfloat16 [768, 768], replicated, may hold values from -0.75 to 0.75
- key_weight: bfloat16 [768, 768], replicated, may hold values from -0.75 to 0.75
- value_weight: bfloat16 [768, 768], replicated, may hold values from -0.21875 to 0.21875
- output_weight: bfloat16 [768, 768], replicated, may hold values from -0.21875 to 0.21875
- gain_attn: float32 [768], replicated, may hold values from 0.1 to 1.9
- gain_score: float32 [768], replicated, may hold values from 0.1 to 1.9
- w_score: float32 [768], replicated, may hold values from -0.6 to 0.6
Outputs:
- losses: float32 [512], P(('dp', 'mp'))
- table_grad: float32 [131072, 768], P('dp', 'mp')
- query_grad: float32 [512, 768], P(('dp', 'mp'))
- query_weight_gradient: float32 [768, 768], P('dp')
- key_weight_gradient: float32 [768, 768], P('dp')
- value_weight_gradient: float32 [768, 768], P('dp')
- output_weight_gradient: float32 [768, 768], P('dp')
- grad_gain_attn: float32 [768], replicated
- grad_gain_score: float32 [768], replicated
- grad_w_score: float32 [768], replicated
The draws below stay inside these ranges and needn't reach their ends.
Inputs may be any that keep to these rules, and one draw needn't show every extreme that they name: `cand_item`: item i lies in list i // 256 at place i % 256. Of the 1024 candidates of the queries of one index of dp (aligned blocks of rows), at most 32 lie in lists stored on one index of dp; one index of dp, the same for every block, holds exactly 32 of the candidates of every block. A permutation: list l is stored as rows list_place[l] * 256 to list_place[l] * 256 + 255 of item_table.
All inputs are finite; a program needn't handle non-finite values.
Results may differ from the reference program's by a relative error of at most 0.025.
Values may be sent and summed in bfloat16 or wider, within the bound.
No kernel may reach another device: no remote copies, remote signals or barrier semaphores. Data moves between devices by JAX's collectives and lax.ppermute only.
A program may use at most 128 MiB of HBM per device.

```python
import jax
import jax.numpy as jnp
from jax import lax

D = 768
HEADS = 12
HEAD = 64
K = 128
Q_DEV = 2
LIST_DEV = 8
LIST_LEN = 256
CAP = 32
LISTS = 512
ITEMS = 131072
QUERIES = 512
N_DP = 64
N_MP = 4


def place_and_items(key):
    streams = jax.random.split(key, 6)
    place = jax.random.permutation(streams[0], LISTS).astype(jnp.int32)
    stored_at = jnp.argsort(place).astype(jnp.int32)
    group_rows = N_MP * Q_DEV * K
    busiest = jax.random.randint(streams[1], (), 0, N_DP).astype(jnp.int32)
    others = jnp.arange(N_DP - 1, dtype=jnp.int32)
    others = others + (others >= busiest).astype(jnp.int32)
    spares = jnp.repeat(others, CAP)

    def take_spares(stream):
        return jax.random.permutation(stream, spares)[:group_rows - CAP]
    chosen = jax.vmap(take_spares)(jax.random.split(streams[2], N_DP))
    owners = jnp.concatenate([jnp.full((N_DP, CAP), busiest, jnp.int32), chosen], 1)

    def shuffle(stream, values):
        return jax.random.permutation(stream, values)
    owners = jax.vmap(shuffle)(jax.random.split(streams[3], N_DP), owners)
    list_pick = jax.random.randint(streams[4], (N_DP, group_rows), 0, LIST_DEV).astype(jnp.int32)
    list_ids = stored_at[owners * LIST_DEV + list_pick]
    positions = jax.random.randint(streams[5], (N_DP, group_rows), 0, LIST_LEN).astype(jnp.int32)
    items = (list_ids * LIST_LEN + positions).reshape(QUERIES, K)
    return (place, items)


def draw_list_place(key, part):
    place, items = place_and_items(key)
    return place


def draw_cand_item(key, part):
    place, items = place_and_items(key)
    return items


def set_ends(entries, rng, smallest, top_value):
    longest = entries.shape.index(max(entries.shape))
    spots = []
    for shift in (0, 1):
        where = [jax.random.randint(jax.random.fold_in(rng, axis), (), 0, length) for axis, length in enumerate(entries.shape)]
        where[longest] = (where[longest] + shift) % entries.shape[longest]
        spots.append(tuple(where))
    return entries.at[spots[0]].set(smallest).at[spots[1]].set(top_value)


def block_levels(stream_key, extent, pieces, smallest, top_value):
    def one(dim, blocks):
        draws = jax.random.uniform(jax.random.fold_in(jax.random.fold_in(stream_key, 6), dim), (blocks,), jnp.float32, smallest / len(pieces), top_value / len(pieces))
        return jnp.repeat(jnp.exp(draws), extent[dim] // blocks).reshape((-1,) + (1,) * (len(extent) - dim - 1))

    loudness = one(*pieces[0])
    for cut in pieces[1:]:
        loudness = loudness * one(*cut)
    return loudness


def noise(rng, dims, width, limit, shards=(), kind=jnp.bfloat16):
    array = jax.random.normal(rng, dims, jnp.float32) * width
    if len(shards) > 0:
        array = block_levels(rng, dims, shards, -0.22, 0.18) * array
    return jnp.clip(array, min=-limit, max=limit).astype(kind)


def setup_inputs(seed: int = 0) -> dict:
    streams_of = jax.random.split(jax.random.key(seed), 13)
    cand_item = draw_cand_item(jax.random.fold_in(streams_of[12], 71), 0)
    list_place = draw_list_place(jax.random.fold_in(streams_of[12], 71), 0)
    item_table = noise(streams_of[2], (ITEMS, D), 1.0, 6.0, ((0, 64), (1, 4)))
    query_vec = noise(streams_of[3], (QUERIES, D), 0.3, 1.796875, ((0, 256),))
    labels = set_ends(jax.random.randint(streams_of[4], (QUERIES, K), 0, 5), jax.random.fold_in(streams_of[4], 1), 0, 4).astype(jnp.int32)
    query_weight = noise(streams_of[5], (D, D), HEAD ** -0.5, 0.75)
    key_weight = noise(streams_of[6], (D, D), HEAD ** -0.5, 0.75)
    value_weight = noise(streams_of[7], (D, D), D ** -0.5, 0.21875)
    output_weight = noise(streams_of[8], (D, D), D ** -0.5, 0.21875)
    gain_attn = jnp.clip(1.0 + 0.18 * jax.random.normal(streams_of[9], (D,), jnp.float32), 0.1, 1.9)
    gain_score = jnp.clip(1.0 + 0.18 * jax.random.normal(streams_of[10], (D,), jnp.float32), 0.1, 1.9)
    w_score = noise(streams_of[11], (D,), 0.1, 0.6, (), jnp.float32)
    return {"cand_item": cand_item, "list_place": list_place, "item_table": item_table, "query_vec": query_vec, "labels": labels, "query_weight": query_weight, "key_weight": key_weight, "value_weight": value_weight, "output_weight": output_weight, "gain_attn": gain_attn, "gain_score": gain_score, "w_score": w_score}


EPSILON = 1e-06
SCORE_CAP = 20.0
RANK_CAP = 30.0

def mixing_weights(form, left, right):
    return jnp.einsum(form, left.astype(jnp.float32), right.astype(jnp.float32), precision=lax.Precision.HIGHEST)

def layer_step(rows_in, query_vec, labels, query_weight, key_weight, value_weight, output_weight, gain_attn, gain_score, w_score):
    batch_size, set_size, width_all = rows_in.shape
    head_size = width_all // HEADS
    shrink = head_size ** (-0.5)
    base_scores = rows_in.astype(jnp.float32) + query_vec.astype(jnp.float32)[:, None, :]
    scale_one = jnp.sqrt(lax.optimization_barrier(jnp.mean(base_scores * base_scores, -1, keepdims=True)) + EPSILON)
    normed_one = base_scores / scale_one
    first_input = (normed_one * gain_attn).astype(jnp.bfloat16)
    projected_queries = mixing_weights('uvy,ym->uvm', first_input, query_weight).astype(jnp.bfloat16)
    projected_keys = mixing_weights('uvy,ym->uvm', first_input, key_weight).astype(jnp.bfloat16)
    projected_values = mixing_weights('uvy,ym->uvm', first_input, value_weight).astype(jnp.bfloat16)
    head_split_shape = (batch_size, set_size, HEADS, head_size)
    query_heads = projected_queries.reshape(head_split_shape)
    key_heads = projected_keys.reshape(head_split_shape)
    value_heads = projected_values.reshape(head_split_shape)
    logits = mixing_weights('bqhe,bkhe->bhqk', query_heads, key_heads) * shrink
    capped = SCORE_CAP * jnp.tanh(logits / SCORE_CAP)
    raised = jnp.exp(capped)
    attend = raised / lax.optimization_barrier(jnp.sum(raised, -1, keepdims=True))
    attend_low = attend.astype(jnp.bfloat16)
    context_rows = mixing_weights('bhqk,bkhe->bqhe', attend_low, value_heads).astype(jnp.bfloat16).reshape(batch_size, set_size, width_all)
    mixed_output = base_scores + mixing_weights('uvy,ym->uvm', context_rows, output_weight)
    scale_two = jnp.sqrt(lax.optimization_barrier(jnp.mean(mixed_output * mixed_output, -1, keepdims=True)) + EPSILON)
    normed_two = mixed_output / scale_two
    scaled_two = normed_two * gain_score
    scores = RANK_CAP * jnp.tanh(lax.optimization_barrier(jnp.sum(scaled_two * w_score, -1)) / RANK_CAP)
    raised_scores = jnp.exp(scores)
    totals = lax.optimization_barrier(jnp.sum(raised_scores, -1, keepdims=True))
    relevance = jnp.exp(labels.astype(jnp.float32))
    target = relevance / lax.optimization_barrier(jnp.sum(relevance, -1, keepdims=True))
    losses = jnp.log(totals[:, 0]) - lax.optimization_barrier(jnp.sum(target * scores, -1))
    diff_raw = (raised_scores / totals - target) * (1.0 - (scores / RANK_CAP) ** 2)
    grad_w_score = lax.optimization_barrier(jnp.sum(scaled_two * diff_raw[..., None], (0, 1)))
    diff_scaled = diff_raw[..., None] * w_score
    grad_gain_score = lax.optimization_barrier(jnp.sum(normed_two * diff_scaled, (0, 1)))
    diff_normed = diff_scaled * gain_score
    diff_mixed = (diff_normed - normed_two * lax.optimization_barrier(jnp.mean(diff_normed * normed_two, -1, keepdims=True))) / scale_two
    lower_gradient = diff_mixed.astype(jnp.bfloat16)
    output_weight_gradient = mixing_weights('fpg,fpi->gi', context_rows, lower_gradient)
    context_gradient = mixing_weights('ifm,gm->ifg', lower_gradient, output_weight).astype(jnp.bfloat16).reshape(head_split_shape)
    diff_attend = mixing_weights('bqhe,bkhe->bhqk', context_gradient, value_heads)
    value_gradient = mixing_weights('bhqk,bqhe->bkhe', attend_low, context_gradient).astype(jnp.bfloat16)
    diff_capped = attend * (diff_attend - lax.optimization_barrier(jnp.sum(attend * diff_attend, -1, keepdims=True)))
    diff_logits = (diff_capped * (1.0 - (capped / SCORE_CAP) ** 2) * shrink).astype(jnp.bfloat16)
    query_gradient = mixing_weights('bhqk,bkhe->bqhe', diff_logits, key_heads).astype(jnp.bfloat16)
    key_gradient = mixing_weights('bhqk,bqhe->bkhe', diff_logits, query_heads).astype(jnp.bfloat16)
    flat_shape = (batch_size, set_size, width_all)
    query_gradient = query_gradient.reshape(flat_shape)
    key_gradient = key_gradient.reshape(flat_shape)
    value_gradient = value_gradient.reshape(flat_shape)
    query_weight_gradient = mixing_weights('fpg,fpi->gi', first_input, query_gradient)
    key_weight_gradient = mixing_weights('fpg,fpi->gi', first_input, key_gradient)
    value_weight_gradient = mixing_weights('fpg,fpi->gi', first_input, value_gradient)
    input_gradient = mixing_weights('ifm,gm->ifg', query_gradient, query_weight) + mixing_weights('ifm,gm->ifg', key_gradient, key_weight) + mixing_weights('ifm,gm->ifg', value_gradient, value_weight)
    grad_gain_attn = lax.optimization_barrier(jnp.sum(normed_one * input_gradient, (0, 1)))
    diff_first = input_gradient * gain_attn
    diff_base = diff_mixed + (diff_first - normed_one * lax.optimization_barrier(jnp.mean(diff_first * normed_one, -1, keepdims=True))) / scale_one
    query_grad = lax.optimization_barrier(jnp.sum(diff_base, 1))
    return (losses, diff_base, query_grad, (query_weight_gradient, key_weight_gradient, value_weight_gradient, output_weight_gradient), (grad_gain_attn, grad_gain_score, grad_w_score))

def reference(cand_item, list_place, item_table, query_vec, labels, query_weight, key_weight, value_weight, output_weight, gain_attn, gain_score, w_score):
    table_rows = (list_place[cand_item // LIST_LEN] * LIST_LEN + cand_item % LIST_LEN).astype(jnp.int32)
    per_group = N_MP * Q_DEV
    row_groups = table_rows.reshape(N_DP, per_group, K)
    query_groups = query_vec.reshape(N_DP, per_group, D)
    label_groups = labels.reshape(N_DP, per_group, K)

    def visit(carry, inputs):
        table_grad, matrices, vectors = carry
        where_rows, group_query, group_labels = inputs
        rows_in = item_table[where_rows]
        losses, diff_base, query_grad, new_matrices, new_vectors = layer_step(rows_in, group_query, group_labels, query_weight, key_weight, value_weight, output_weight, gain_attn, gain_score, w_score)
        table_grad = table_grad.at[where_rows.reshape(-1)].add(diff_base.reshape(-1, D))
        matrices = jax.tree.map(jnp.add, matrices, new_matrices)
        vectors = jax.tree.map(jnp.add, vectors, new_vectors)
        return ((table_grad, matrices, vectors), (losses, query_grad))
    zero_matrix = jnp.zeros((D, D), jnp.float32)
    zero_vector = jnp.zeros((D,), jnp.float32)
    start = (jnp.zeros((ITEMS, D), jnp.float32), (zero_matrix, zero_matrix, zero_matrix, zero_matrix), (zero_vector, zero_vector, zero_vector))
    (table_grad, matrices, vectors), (losses, query_grad) = lax.scan(visit, start, (row_groups, query_groups, label_groups))
    return (losses.reshape(QUERIES), table_grad, query_grad.reshape(QUERIES, D), matrices[0], matrices[1], matrices[2], matrices[3], vectors[0], vectors[1], vectors[2])
```

```python
import jax
import jax.numpy as jnp
from jax import lax
from jax.experimental import pallas as pl
from jax.experimental.pallas import tpu as pltpu
from jax.sharding import Mesh
from jax.sharding import PartitionSpec as P

HEADS = 12
LIST_LEN = 256
EPSILON = 1e-06
SCORE_CAP = 20.0
RANK_CAP = 30.0

ROWS = ("y", "z", "c")
CAP = 32
SLAB = 192
BF = jnp.bfloat16
F32 = jnp.float32
MIB = 1024 * 1024


def dot(a, b, ca=1, cb=0):
    return lax.dot_general(a, b, (((ca,), (cb,)), ((), ())), preferred_element_type=F32)


def iota(shape, dim):
    return lax.broadcasted_iota(jnp.int32, shape, dim)


def whole(n):
    return [pl.BlockSpec(memory_space=pltpu.VMEM)] * n


def call(kernel, out_shape, args, mib, flops, size, scratch=()):
    outs = out_shape if isinstance(out_shape, (list, tuple)) else [out_shape]
    specs = whole(len(outs))
    return pl.pallas_call(
        kernel,
        out_shape=out_shape,
        in_specs=whole(len(args)),
        out_specs=specs if isinstance(out_shape, (list, tuple)) else specs[0],
        scratch_shapes=list(scratch),
        compiler_params=pltpu.CompilerParams(vmem_limit_bytes=mib * MIB),
        cost_estimate=pl.CostEstimate(flops=flops, bytes_accessed=size, transcendentals=0),
    )(*args)


def low_half(shape):
    return iota(shape, len(shape) - 1) < 64


def swap_halves(t):
    return jnp.concatenate([t[..., 64:], t[..., :64]], axis=-1)


def spread_tail(t):
    t = t.astype(F32)
    other = swap_halves(t)
    low = low_half(t.shape)
    return jnp.concatenate([jnp.where(low, t, other), jnp.where(low, other, t)], axis=1)


def unpack(block):
    b, rows, _ = block.shape
    n = rows // 3
    main = block[:, : 2 * n, :].reshape(b * 2 * n, 128)
    tail = spread_tail(block[:, 2 * n :, :]).astype(BF).reshape(b * 2 * n, 128)
    return jnp.concatenate([main, tail], axis=1)


def pack(full, n):
    tail = full[:, 128:]
    tail = jnp.where(low_half((n, 128)), tail[:n], tail[n:])
    return jnp.concatenate([full[:, :128], tail], axis=0).astype(BF)


def as_column(row):
    return jnp.transpose(jnp.broadcast_to(row, (128, 128)))


def routing_kernel(ids_ref, place_ref, request_ref, slot_ref):
    place = place_ref[...]
    lists = place.shape[1]
    lane = iota((128, 128), 1)
    owner_of_list = jnp.broadcast_to(place >> 3, (128, lists))
    row = iota((128, lists), 0)
    lookup = jnp.where(owner_of_list == row, 1.0, 0.0)
    lookup = jnp.where(row == 64, jnp.broadcast_to(place & 7, (128, lists)).astype(F32), lookup)
    lookup = lookup.astype(BF)
    before = (iota((128, 128), 1) < iota((128, 128), 0)).astype(F32).astype(BF)
    carry = jnp.zeros((1, 128), F32)
    request = jnp.zeros((128, 128), F32)
    for q in range(ids_ref.shape[0]):
        ids = as_column(ids_ref[q : q + 1, :])
        list_id = ids >> 8
        chosen = jnp.concatenate(
            [(list_id == lane + 128 * t).astype(F32).astype(BF) for t in range(lists // 128)], axis=1
        )
        found = dot(chosen, lookup, 1, 1)
        sub = jnp.sum(jnp.where(lane == 64, found, 0.0), 1, keepdims=True)
        onehot = jnp.where(lane < 64, found, 0.0)
        onehot_low = onehot.astype(BF)
        ahead = dot(before, onehot_low) + carry
        carry = carry + jnp.sum(onehot, 0, keepdims=True)
        rank = jnp.sum(onehot * ahead, 1, keepdims=True)
        owner = jnp.sum(onehot * lane.astype(F32), 1, keepdims=True)
        slot = jnp.broadcast_to(owner * CAP + rank, (128, 128))
        slot_ref[q : q + 1, :] = jnp.transpose(slot)[0:1, :].astype(jnp.int32)
        rank = rank.astype(jnp.int32)
        place_in = (ids & 255).astype(F32)
        entry = jnp.where(rank == lane, sub + 1.0, jnp.where(rank == lane - CAP, place_in, 0.0))
        request = request + dot(onehot_low, entry.astype(BF), 0, 0)
    high = request[:64, :CAP]
    low = request[:64, CAP : 2 * CAP]
    asked = (high - 1.0) * LIST_LEN + low
    request_ref[...] = jnp.where(high > 0.5, asked, -1.0).astype(jnp.int32)


def owner_kernel(asked_ref, table_ref, out_ref):
    groups = asked_ref.shape[0]
    part = groups // 4
    asked = asked_ref[...]
    asked = jnp.concatenate([asked[part * k : part * (k + 1)] for k in range(4)], axis=1)
    table = table_ref[...]
    stored = table.shape[0]
    tail = table[:, 128:].astype(F32)
    table = jnp.concatenate([table[:, :128], jnp.concatenate([tail, tail], 1).astype(BF)], axis=1)
    step = 4
    for r in range(0, part, step):
        column = jnp.concatenate([as_column(asked[r + i : r + i + 1]) for i in range(step)], axis=0)
        lane = iota((128 * step, 128), 1)
        chosen = jnp.concatenate(
            [(column == lane + 128 * t).astype(F32).astype(BF) for t in range(stored // 128)], axis=1
        )
        rows = dot(chosen, table)
        for i in range(step):
            for k in range(4):
                at = 128 * i + CAP * k
                out_ref[part * k + r + i] = pack(rows[at : at + CAP], CAP // 2)


def pieces_kernel(slot_ref, fetched_ref, out_ref):
    fetched = unpack(fetched_ref[...])
    slots = fetched.shape[0]
    for m in range(out_ref.shape[0]):
        column = jnp.concatenate([as_column(slot_ref[2 * m + i : 2 * m + i + 1, :]) for i in (0, 1)], axis=0)
        lane = iota((256, 128), 1)
        chosen = jnp.concatenate(
            [(column == lane + 128 * t).astype(F32).astype(BF) for t in range(slots // 128)], axis=1
        )
        out_ref[m] = pack(dot(chosen, fetched), 128)


def slots_kernel(slot_ref, grads_ref, out_ref):
    grads = unpack(grads_ref[...])
    groups = out_ref.shape[0]
    step = 16 * CAP
    for r in range(0, groups * CAP, step):
        row = iota((step, 128), 0) + r
        chosen = jnp.concatenate(
            [
                (jnp.broadcast_to(slot_ref[q : q + 1, :], (step, 128)) == row).astype(F32).astype(BF)
                for q in range(slot_ref.shape[0])
            ],
            axis=1,
        )
        rows = dot(chosen, grads)
        for i in range(16):
            out_ref[r // CAP + i] = pack(rows[CAP * i : CAP * (i + 1)], CAP // 2)


def landing_kernel(asked_ref, arrived_ref, out_ref):
    arrived = unpack(arrived_ref[...])
    stored = out_ref.shape[0]
    step = 512
    for r in range(0, stored, step):
        row = iota((step, 128), 0) + r
        chosen = jnp.concatenate(
            [
                (jnp.broadcast_to(asked_ref[q : q + 1, :], (step, 128)) == row).astype(F32).astype(BF)
                for q in range(asked_ref.shape[0])
            ],
            axis=1,
        )
        out_ref[r : r + step, :] = dot(chosen, arrived)[:, :SLAB]


def lane_mean(x):
    return jnp.sum(x, 1, keepdims=True) * (1.0 / x.shape[1])


def step_kernel(
    core_ref,
    rows_ref,
    query_ref,
    labels_ref,
    wq_ref,
    wk_ref,
    wv_ref,
    wo_ref,
    gain_attn_ref,
    gain_score_ref,
    w_score_ref,
    losses_ref,
    base_ref,
    query_grad_ref,
    keep_ref,
    send_ref,
    scores_t,
    attend_t,
    grads,
):
    queries, width = query_ref.shape
    size = 128
    head = width // HEADS
    pairs = HEADS // 2
    shrink = head ** (-0.5)
    low = low_half((size, 128))

    parts = []
    for m in range(rows_ref.shape[0]):
        main = rows_ref[m, :256, :].astype(F32)
        tail = rows_ref[m, 256:, :].astype(F32)
        parts += [main, jnp.concatenate([tail[:, :64], tail[:, 64:]], axis=0)]
    rows_in = jnp.concatenate(parts, axis=1)
    vecs = query_ref[...].astype(F32)
    vecs = jnp.concatenate([jnp.broadcast_to(vecs[q : q + 1], (size, width)) for q in range(queries)], axis=0)
    base = rows_in + vecs
    inv_one = 1.0 / jnp.sqrt(lane_mean(base * base) + EPSILON)
    normed_one = base * inv_one
    gain_attn = gain_attn_ref[...]
    first_input = (normed_one * gain_attn).astype(BF)
    q_all = dot(first_input, wq_ref[...]).astype(BF)
    k_all = dot(first_input, wk_ref[...]).astype(BF)
    v_all = dot(first_input, wv_ref[...]).astype(BF)

    def cut(x, q, p):
        return x[size * q : size * (q + 1), 128 * p : 128 * (p + 1)]

    zero = jnp.zeros((size, 128), BF)

    def heads_apart(x):
        return jnp.concatenate([jnp.where(low, x, zero), jnp.where(low, zero, x)], axis=0)

    def heads_joined(x):
        return jnp.where(low, x[:size], x[size:])

    context = []
    for q in range(queries):
        line = []
        for p in range(pairs):
            logits = dot(cut(k_all, q, p), heads_apart(cut(q_all, q, p)), 1, 1)
            th = jnp.tanh(logits * (shrink / SCORE_CAP))
            raised = jnp.exp(SCORE_CAP * th)
            attend = raised * (1.0 / jnp.sum(raised, 0, keepdims=True))
            scores_t[q * pairs + p] = th
            attend_t[q * pairs + p] = attend
            line.append(heads_joined(dot(attend.astype(BF), cut(v_all, q, p), 0, 0)))
        context.append(jnp.concatenate(line, axis=1))
    context = jnp.concatenate(context, axis=0).astype(BF)

    mixed = base + dot(context, wo_ref[...])
    inv_two = 1.0 / jnp.sqrt(lane_mean(mixed * mixed) + EPSILON)
    normed_two = mixed * inv_two
    gain_score = gain_score_ref[...]
    w_score = w_score_ref[...]
    scaled_two = normed_two * gain_score
    capped_scores = jnp.tanh(jnp.sum(scaled_two * w_score, 1, keepdims=True) * (1.0 / RANK_CAP))
    scores = RANK_CAP * capped_scores
    raised = jnp.exp(scores)
    relevance = jnp.exp(labels_ref[...].astype(F32))
    target = relevance / jnp.sum(relevance, 1, keepdims=True)
    diffs = []
    for q in range(queries):
        at = slice(size * q, size * (q + 1))
        total = jnp.sum(raised[at], 0, keepdims=True)
        wanted = as_column(target[q : q + 1])[:, 0:1]
        loss = jnp.log(total) - jnp.sum(wanted * scores[at], 0, keepdims=True)
        losses_ref[q : q + 1, :] = jnp.broadcast_to(loss, (1, 128))
        diffs.append(raised[at] / total - wanted)
    diff_raw = jnp.concatenate(diffs, axis=0) * (1.0 - capped_scores * capped_scores)
    grad_w_score = jnp.sum(scaled_two * diff_raw, 0, keepdims=True)
    diff_scaled = diff_raw * w_score
    grad_gain_score = jnp.sum(normed_two * diff_scaled, 0, keepdims=True)
    diff_normed = diff_scaled * gain_score
    diff_mixed = (diff_normed - normed_two * lane_mean(diff_normed * normed_two)) * inv_two
    diff_low = diff_mixed.astype(BF)
    diff_context = dot(diff_low, wo_ref[...], 1, 1).astype(BF)

    diff_q, diff_k, diff_v = [], [], []
    for q in range(queries):
        line_q, line_k, line_v = [], [], []
        for p in range(pairs):
            th = scores_t[q * pairs + p]
            attend = attend_t[q * pairs + p]
            split = heads_apart(cut(diff_context, q, p))
            diff_attend = dot(cut(v_all, q, p), split, 1, 1)
            line_v.append(dot(attend.astype(BF), split))
            inner = diff_attend - jnp.sum(attend * diff_attend, 0, keepdims=True)
            diff_logits = (attend * inner * (1.0 - th * th) * shrink).astype(BF)
            line_q.append(heads_joined(dot(diff_logits, cut(k_all, q, p), 0, 0)))
            line_k.append(dot(diff_logits, heads_apart(cut(q_all, q, p))))
        diff_q.append(jnp.concatenate(line_q, axis=1))
        diff_k.append(jnp.concatenate(line_k, axis=1))
        diff_v.append(jnp.concatenate(line_v, axis=1))
    diff_q = jnp.concatenate(diff_q, axis=0).astype(BF)
    diff_k = jnp.concatenate(diff_k, axis=0).astype(BF)
    diff_v = jnp.concatenate(diff_v, axis=0).astype(BF)

    diff_input = dot(diff_q, wq_ref[...], 1, 1) + dot(diff_k, wk_ref[...], 1, 1) + dot(diff_v, wv_ref[...], 1, 1)
    grad_gain_attn = jnp.sum(normed_one * diff_input, 0, keepdims=True)
    diff_first = diff_input * gain_attn
    diff_base = diff_mixed + (diff_first - normed_one * lane_mean(diff_first * normed_one)) * inv_one
    for q in range(queries):
        query_grad_ref[q : q + 1, :] = jnp.sum(diff_base[size * q : size * (q + 1)], 0, keepdims=True)
    for m in range(base_ref.shape[0]):
        slab = diff_base[:, SLAB * m : SLAB * (m + 1)]
        base_ref[m, :256, :] = slab[:, :128].astype(BF)
        base_ref[m, 256:, :] = jnp.concatenate([slab[:128, 128:], slab[128:, 128:]], axis=1).astype(BF)

    grads[0] = dot(first_input, diff_q, 0, 0)
    grads[1] = dot(first_input, diff_k, 0, 0)
    grads[2] = dot(first_input, diff_v, 0, 0)
    grads[3] = dot(context, diff_low, 0, 0)
    vectors = [
        v[:, 128 * t : 128 * (t + 1)]
        for v in (grad_gain_attn, grad_gain_score, grad_w_score)
        for t in range(width // 128)
    ]
    vectors = jnp.concatenate(vectors + [jnp.zeros((32 - len(vectors), 128), F32)], axis=0)
    first_core = core_ref[0] == 0

    def assemble(at, carry):
        chunk = [grads[i, pl.ds(pl.multiple_of(24 * at, 8), 24), :] for i in range(4)]
        halves = [jnp.concatenate([g[12 * c : 12 * (c + 1)] for g in chunk], axis=0) for c in (0, 1)]
        for m in range(4):
            blocks = []
            for rows48 in halves:
                tiles = []
                for h in range(9 * m, 9 * m + 9):
                    rb, t = h // 6, h % 6
                    tiles.append(rows48[8 * rb : 8 * rb + 8, 128 * t : 128 * (t + 1)])
                blocks.append(jnp.concatenate(tiles + [vectors[8 * m : 8 * m + 8]], axis=0).astype(BF))
            keep_ref[m, at] = jnp.where(first_core, blocks[0], blocks[1])
            send_ref[m, at] = jnp.where(first_core, blocks[1], blocks[0])
        return carry

    lax.fori_loop(0, keep_ref.shape[1], assemble, 0)


def finish_kernel(blocks_ref, q_ref, k_ref, v_ref, o_ref, vec_ref):
    blocks = blocks_ref[...].astype(F32)
    tiles = [blocks[m, 8 * i : 8 * i + 8] for m in range(4) for i in range(9)]
    rows48 = jnp.concatenate([jnp.concatenate(tiles[6 * rb : 6 * rb + 6], axis=1) for rb in range(6)], axis=0)
    for i, ref in enumerate((q_ref, k_ref, v_ref, o_ref)):
        ref[...] = rows48[12 * i : 12 * (i + 1)]
    vec_ref[...] = jnp.concatenate([blocks[m, 72:] for m in range(4)], axis=0)


def shape(dims, kind=BF):
    return jax.ShapeDtypeStruct(dims, kind)


def swap(x, axes):
    return lax.all_to_all(x, axes, split_axis=0, concat_axis=0, tiled=True)


def body(
    cand_item,
    list_place,
    item_table,
    query_vec,
    labels,
    query_weight,
    key_weight,
    value_weight,
    output_weight,
    gain_attn,
    gain_score,
    w_score,
):
    queries, size = cand_item.shape
    stored, slab = item_table.shape
    width = query_vec.shape[1]
    n_dp = lax.axis_size(ROWS)
    n_mp = lax.axis_size("x")
    n_yz = lax.axis_size(("y", "z"))
    slots = n_dp * CAP

    ids = lax.all_gather(cand_item, "x", axis=0, tiled=True)
    request, slot = call(
        routing_kernel,
        [shape((n_dp, CAP), jnp.int32), shape((n_mp * queries, size), jnp.int32)],
        (ids, list_place.reshape(1, -1)),
        24, 3 * 10**8, 10**6,
    )
    asked = swap(request, ROWS)
    found = call(
        owner_kernel, shape((n_dp, 48, 128)), (asked, item_table), 40, 2 * 10**9, 2 * 10**6
    )
    fetched = swap(found, ROWS)
    pieces = call(pieces_kernel, shape((n_mp, 384, 128)), (slot, fetched), 40, 10**9, 2 * 10**6)
    rows_in = swap(pieces, "x")
    core = lax.axis_index("c").astype(jnp.int32).reshape(1)
    args = (
        core, rows_in, query_vec, labels,
        query_weight, key_weight, value_weight, output_weight,
        gain_attn.reshape(1, -1), gain_score.reshape(1, -1), w_score.reshape(1, -1),
    )
    outs = [
        shape((queries, 128), F32),
        shape((n_mp, 384, 128)),
        shape((queries, width), F32),
        shape((n_mp, n_yz, 80, 128)),
        shape((n_mp, n_yz, 80, 128)),
    ]
    losses, diff_base, query_grad, keep, send = pl.pallas_call(
        step_kernel,
        out_shape=outs,
        in_specs=[pl.BlockSpec(memory_space=pltpu.SMEM)] + whole(len(args) - 1),
        out_specs=whole(len(outs)),
        scratch_shapes=[
            pltpu.VMEM((HEADS * queries // 2, 128, 256), F32),
            pltpu.VMEM((HEADS * queries // 2, 128, 256), F32),
            pltpu.VMEM((4, width, width), F32),
        ],
        compiler_params=pltpu.CompilerParams(vmem_limit_bytes=56 * MIB),
        cost_estimate=pl.CostEstimate(flops=5 * 10**9, bytes_accessed=12 * 10**6, transcendentals=0),
    )(*args)

    column_grads = swap(diff_base, "x")
    outgoing = call(
        slots_kernel, shape((n_dp, 48, 128)), (slot, column_grads), 40, 10**9, 2 * 10**6
    )
    arrived = swap(outgoing, ROWS)
    table_grad = call(
        landing_kernel,
        shape((stored, slab), F32),
        (asked.reshape(slots // 128, 128), arrived),
        40, 2 * 10**9, 4 * 10**6,
    )

    other = lax.ppermute(send, "c", [(0, 1), (1, 0)])
    both = (keep.astype(F32) + other.astype(F32)).astype(BF)

    def summed(x):
        return jnp.sum(x.astype(F32), 0).astype(BF)

    over_x = summed(swap(both, "x"))
    over_all = summed(swap(over_x, ("y", "z")))
    blocks = lax.all_gather(over_all, "x", axis=0, tiled=False)
    rows = width // n_dp
    finished = call(
        finish_kernel,
        [shape((rows, width), F32)] * 4 + [shape((32, 128), F32)],
        (blocks,), 8, 10**6, 10**6,
    )
    vectors = finished[4].reshape(-1)
    return (
        losses[:, 0],
        table_grad,
        query_grad,
        finished[0],
        finished[1],
        finished[2],
        finished[3],
        vectors[:width],
        vectors[width : 2 * width],
        vectors[2 * width : 3 * width],
    )


def solution(mesh):
    grid = Mesh(mesh.devices.reshape(4, 8, 2, 4), ("y", "z", "c", "x"))
    each = P(("y", "z", "c", "x"), None)
    placed = (each, P(), P(ROWS, "x"), each, each, P(), P(), P(), P(), P(), P(), P())
    return jax.shard_map(
        body,
        mesh=grid,
        in_specs=placed,
        out_specs=(
            P(("y", "z", "c", "x")),
            P(ROWS, "x"),
            each,
            P(ROWS, None),
            P(ROWS, None),
            P(ROWS, None),
            P(ROWS, None),
            P(),
            P(),
            P(),
        ),
        check_vma=False,
    )
```

```python
import jax
import jax.numpy as jnp
from jax import lax
from jax.experimental import pallas as pl
from jax.experimental.pallas import tpu as pltpu
from jax.sharding import Mesh
from jax.sharding import PartitionSpec as P

HEADS = 12
LIST_LEN = 256
EPSILON = 1e-06
SCORE_CAP = 20.0
RANK_CAP = 30.0

ROWS = ("y", "z", "c")
CAP = 32
SLAB = 192
BF = jnp.bfloat16
F32 = jnp.float32
MIB = 1024 * 1024


def dot(a, b, ca=1, cb=0):
    return lax.dot_general(a, b, (((ca,), (cb,)), ((), ())), preferred_element_type=F32)


def iota(shape, dim):
    return lax.broadcasted_iota(jnp.int32, shape, dim)


def whole(n):
    return [pl.BlockSpec(memory_space=pltpu.VMEM)] * n


def call(kernel, out_shape, args, mib, flops, size, scratch=(), scalar=False):
    outs = out_shape if isinstance(out_shape, (list, tuple)) else [out_shape]
    specs = whole(len(outs))
    in_specs = whole(len(args))
    if scalar:
        in_specs[0] = pl.BlockSpec(memory_space=pltpu.SMEM)
    return pl.pallas_call(
        kernel,
        out_shape=out_shape,
        in_specs=in_specs,
        out_specs=specs if isinstance(out_shape, (list, tuple)) else specs[0],
        scratch_shapes=list(scratch),
        compiler_params=pltpu.CompilerParams(vmem_limit_bytes=mib * MIB),
        cost_estimate=pl.CostEstimate(flops=flops, bytes_accessed=size, transcendentals=0),
    )(*args)


def shift(x, axis, by):
    return lax.ppermute(x, axis, [(i, (i + by) % 4) for i in range(4)])


def exchange(blocks, axis):
    return [blocks[0]] + [shift(blocks[k], axis, k) for k in (1, 2, 3)]


def collect(me, refs, held):
    for k, ref in enumerate(refs):
        held[(me - k) & 3] = ref[...]


def low_half(shape):
    return iota(shape, len(shape) - 1) < 64


def swap_halves(t):
    return jnp.concatenate([t[..., 64:], t[..., :64]], axis=-1)


def spread_tail(t):
    t = t.astype(F32)
    other = swap_halves(t)
    low = low_half(t.shape)
    return jnp.concatenate([jnp.where(low, t, other), jnp.where(low, other, t)], axis=1)


def unpack(block):
    b, rows, _ = block.shape
    n = rows // 3
    main = block[:, : 2 * n, :].reshape(b * 2 * n, 128)
    tail = spread_tail(block[:, 2 * n :, :]).astype(BF).reshape(b * 2 * n, 128)
    return jnp.concatenate([main, tail], axis=1)


def pack(full, n):
    tail = full[:, 128:]
    tail = jnp.where(low_half((n, 128)), tail[:n], tail[n:])
    return jnp.concatenate([full[:, :128], tail], axis=0).astype(BF)


def as_column(row):
    return jnp.transpose(jnp.broadcast_to(row, (128, 128)))


def routing_kernel(me_ref, a_ref, b_ref, c_ref, d_ref, place_ref, request_ref, slot_ref, held):
    collect(me_ref[0], (a_ref, b_ref, c_ref, d_ref), held)
    place = place_ref[...]
    lists = place.shape[1]
    lane = iota((128, 128), 1)
    owner_of_list = jnp.broadcast_to(place >> 3, (128, lists))
    row = iota((128, lists), 0)
    lookup = jnp.where(owner_of_list == row, 1.0, 0.0)
    lookup = jnp.where(row == 64, jnp.broadcast_to(place & 7, (128, lists)).astype(F32), lookup)
    lookup = lookup.astype(BF)
    before = (iota((128, 128), 1) < iota((128, 128), 0)).astype(F32).astype(BF)
    carry = jnp.zeros((1, 128), F32)
    request = jnp.zeros((128, 128), F32)
    for q in range(slot_ref.shape[0]):
        ids = as_column(held[q // 2, q % 2 : q % 2 + 1, :])
        list_id = ids >> 8
        chosen = jnp.concatenate(
            [(list_id == lane + 128 * t).astype(F32).astype(BF) for t in range(lists // 128)], axis=1
        )
        found = dot(chosen, lookup, 1, 1)
        sub = jnp.sum(jnp.where(lane == 64, found, 0.0), 1, keepdims=True)
        onehot = jnp.where(lane < 64, found, 0.0)
        onehot_low = onehot.astype(BF)
        ahead = dot(before, onehot_low) + carry
        carry = carry + jnp.sum(onehot, 0, keepdims=True)
        rank = jnp.sum(onehot * ahead, 1, keepdims=True)
        owner = jnp.sum(onehot * lane.astype(F32), 1, keepdims=True)
        slot = jnp.broadcast_to(owner * CAP + rank, (128, 128))
        slot_ref[q : q + 1, :] = jnp.transpose(slot)[0:1, :].astype(jnp.int32)
        rank = rank.astype(jnp.int32)
        place_in = (ids & 255).astype(F32)
        entry = jnp.where(rank == lane, sub + 1.0, jnp.where(rank == lane - CAP, place_in, 0.0))
        request = request + dot(onehot_low, entry.astype(BF), 0, 0)
    high = request[:64, :CAP]
    low = request[:64, CAP : 2 * CAP]
    asked = (high - 1.0) * LIST_LEN + low
    request_ref[...] = jnp.where(high > 0.5, asked, -1.0).astype(jnp.int32)


def owner_kernel(asked_ref, table_ref, out_ref):
    groups = asked_ref.shape[0]
    part = groups // 4
    asked = asked_ref[...]
    asked = jnp.concatenate([asked[part * k : part * (k + 1)] for k in range(4)], axis=1)
    table = table_ref[...]
    stored = table.shape[0]
    tail = table[:, 128:].astype(F32)
    table = jnp.concatenate([table[:, :128], jnp.concatenate([tail, tail], 1).astype(BF)], axis=1)
    step = 4
    for r in range(0, part, step):
        column = jnp.concatenate([as_column(asked[r + i : r + i + 1]) for i in range(step)], axis=0)
        lane = iota((128 * step, 128), 1)
        chosen = jnp.concatenate(
            [(column == lane + 128 * t).astype(F32).astype(BF) for t in range(stored // 128)], axis=1
        )
        rows = dot(chosen, table)
        for i in range(step):
            for k in range(4):
                at = 128 * i + CAP * k
                out_ref[part * k + r + i] = pack(rows[at : at + CAP], CAP // 2)


def pieces_kernel(me_ref, slot_ref, fetched_ref, *out_refs):
    fetched = unpack(fetched_ref[...])
    slots = fetched.shape[0]
    for k, out_ref in enumerate(out_refs):
        m = (me_ref[0] + k) & 3
        column = jnp.concatenate([as_column(slot_ref[pl.ds(2 * m + i, 1), :]) for i in (0, 1)], axis=0)
        lane = iota((256, 128), 1)
        chosen = jnp.concatenate(
            [(column == lane + 128 * t).astype(F32).astype(BF) for t in range(slots // 128)], axis=1
        )
        out_ref[...] = pack(dot(chosen, fetched), 128)


def slots_kernel(me_ref, slot_ref, a_ref, b_ref, c_ref, d_ref, out_ref, held):
    collect(me_ref[0], (a_ref, b_ref, c_ref, d_ref), held)
    grads = unpack(held[...])
    groups = out_ref.shape[0]
    step = 16 * CAP
    for r in range(0, groups * CAP, step):
        row = iota((step, 128), 0) + r
        chosen = jnp.concatenate(
            [
                (jnp.broadcast_to(slot_ref[q : q + 1, :], (step, 128)) == row).astype(F32).astype(BF)
                for q in range(slot_ref.shape[0])
            ],
            axis=1,
        )
        rows = dot(chosen, grads)
        for i in range(16):
            out_ref[r // CAP + i] = pack(rows[CAP * i : CAP * (i + 1)], CAP // 2)


def landing_kernel(asked_ref, arrived_ref, out_ref):
    arrived = unpack(arrived_ref[...])
    stored = out_ref.shape[0]
    step = 512
    for r in range(0, stored, step):
        row = iota((step, 128), 0) + r
        chosen = jnp.concatenate(
            [
                (jnp.broadcast_to(asked_ref[q : q + 1, :], (step, 128)) == row).astype(F32).astype(BF)
                for q in range(asked_ref.shape[0])
            ],
            axis=1,
        )
        out_ref[r : r + step, :] = dot(chosen, arrived)[:, :SLAB]


def lane_mean(x):
    return jnp.sum(x, 1, keepdims=True) * (1.0 / x.shape[1])


def step_kernel(
    me_ref,
    a_ref,
    b_ref,
    c_ref,
    d_ref,
    query_ref,
    labels_ref,
    wq_ref,
    wk_ref,
    wv_ref,
    wo_ref,
    gain_attn_ref,
    gain_score_ref,
    w_score_ref,
    losses_ref,
    query_grad_ref,
    base_0_ref,
    base_1_ref,
    base_2_ref,
    base_3_ref,
    input_ref,
    diff_q_ref,
    diff_k_ref,
    diff_v_ref,
    context_ref,
    diff_low_ref,
    vectors_ref,
    held,
    scores_t,
    attend_t,
):
    me = me_ref[0]
    collect(me, (a_ref, b_ref, c_ref, d_ref), held)
    queries, width = query_ref.shape
    size = 128
    head = width // HEADS
    pairs = HEADS // 2
    shrink = head ** (-0.5)
    low = low_half((size, 128))

    parts = []
    for m in range(4):
        main = held[m, :256, :].astype(F32)
        tail = held[m, 256:, :].astype(F32)
        parts += [main, jnp.concatenate([tail[:, :64], tail[:, 64:]], axis=0)]
    rows_in = jnp.concatenate(parts, axis=1)
    vecs = query_ref[...].astype(F32)
    vecs = jnp.concatenate([jnp.broadcast_to(vecs[q : q + 1], (size, width)) for q in range(queries)], axis=0)
    base = rows_in + vecs
    inv_one = 1.0 / jnp.sqrt(lane_mean(base * base) + EPSILON)
    normed_one = base * inv_one
    gain_attn = gain_attn_ref[...]
    first_input = (normed_one * gain_attn).astype(BF)
    q_all = dot(first_input, wq_ref[...]).astype(BF)
    k_all = dot(first_input, wk_ref[...]).astype(BF)
    v_all = dot(first_input, wv_ref[...]).astype(BF)

    def cut(x, q, p):
        return x[size * q : size * (q + 1), 128 * p : 128 * (p + 1)]

    zero = jnp.zeros((size, 128), BF)

    def heads_apart(x):
        return jnp.concatenate([jnp.where(low, x, zero), jnp.where(low, zero, x)], axis=0)

    def heads_joined(x):
        return jnp.where(low, x[:size], x[size:])

    context = []
    for q in range(queries):
        line = []
        for p in range(pairs):
            logits = dot(cut(k_all, q, p), heads_apart(cut(q_all, q, p)), 1, 1)
            th = jnp.tanh(logits * (shrink / SCORE_CAP))
            raised = jnp.exp(SCORE_CAP * th)
            attend = raised * (1.0 / jnp.sum(raised, 0, keepdims=True))
            scores_t[q * pairs + p] = th
            attend_t[q * pairs + p] = attend
            line.append(heads_joined(dot(attend.astype(BF), cut(v_all, q, p), 0, 0)))
        context.append(jnp.concatenate(line, axis=1))
    context = jnp.concatenate(context, axis=0).astype(BF)

    mixed = base + dot(context, wo_ref[...])
    inv_two = 1.0 / jnp.sqrt(lane_mean(mixed * mixed) + EPSILON)
    normed_two = mixed * inv_two
    gain_score = gain_score_ref[...]
    w_score = w_score_ref[...]
    scaled_two = normed_two * gain_score
    capped_scores = jnp.tanh(jnp.sum(scaled_two * w_score, 1, keepdims=True) * (1.0 / RANK_CAP))
    scores = RANK_CAP * capped_scores
    raised = jnp.exp(scores)
    relevance = jnp.exp(labels_ref[...].astype(F32))
    target = relevance / jnp.sum(relevance, 1, keepdims=True)
    diffs = []
    for q in range(queries):
        at = slice(size * q, size * (q + 1))
        total = jnp.sum(raised[at], 0, keepdims=True)
        wanted = as_column(target[q : q + 1])[:, 0:1]
        loss = jnp.log(total) - jnp.sum(wanted * scores[at], 0, keepdims=True)
        losses_ref[q : q + 1, :] = jnp.broadcast_to(loss, (1, 128))
        diffs.append(raised[at] / total - wanted)
    diff_raw = jnp.concatenate(diffs, axis=0) * (1.0 - capped_scores * capped_scores)
    grad_w_score = jnp.sum(scaled_two * diff_raw, 0, keepdims=True)
    diff_scaled = diff_raw * w_score
    grad_gain_score = jnp.sum(normed_two * diff_scaled, 0, keepdims=True)
    diff_normed = diff_scaled * gain_score
    diff_mixed = (diff_normed - normed_two * lane_mean(diff_normed * normed_two)) * inv_two
    diff_low = diff_mixed.astype(BF)
    diff_context = dot(diff_low, wo_ref[...], 1, 1).astype(BF)

    diff_q, diff_k, diff_v = [], [], []
    for q in range(queries):
        line_q, line_k, line_v = [], [], []
        for p in range(pairs):
            th = scores_t[q * pairs + p]
            attend = attend_t[q * pairs + p]
            split = heads_apart(cut(diff_context, q, p))
            diff_attend = dot(cut(v_all, q, p), split, 1, 1)
            line_v.append(dot(attend.astype(BF), split))
            inner = diff_attend - jnp.sum(attend * diff_attend, 0, keepdims=True)
            diff_logits = (attend * inner * (1.0 - th * th) * shrink).astype(BF)
            line_q.append(heads_joined(dot(diff_logits, cut(k_all, q, p), 0, 0)))
            line_k.append(dot(diff_logits, heads_apart(cut(q_all, q, p))))
        diff_q.append(jnp.concatenate(line_q, axis=1))
        diff_k.append(jnp.concatenate(line_k, axis=1))
        diff_v.append(jnp.concatenate(line_v, axis=1))
    diff_q = jnp.concatenate(diff_q, axis=0).astype(BF)
    diff_k = jnp.concatenate(diff_k, axis=0).astype(BF)
    diff_v = jnp.concatenate(diff_v, axis=0).astype(BF)

    diff_input = dot(diff_q, wq_ref[...], 1, 1) + dot(diff_k, wk_ref[...], 1, 1) + dot(diff_v, wv_ref[...], 1, 1)
    grad_gain_attn = jnp.sum(normed_one * diff_input, 0, keepdims=True)
    diff_first = diff_input * gain_attn
    diff_base = diff_mixed + (diff_first - normed_one * lane_mean(diff_first * normed_one)) * inv_one
    for q in range(queries):
        query_grad_ref[q : q + 1, :] = jnp.sum(diff_base[size * q : size * (q + 1)], 0, keepdims=True)
    for m in range(4):
        slab = diff_base[:, SLAB * m : SLAB * (m + 1)]
        held[m, :256, :] = slab[:, :128].astype(BF)
        held[m, 256:, :] = jnp.concatenate([slab[:128, 128:], slab[128:, 128:]], axis=1).astype(BF)
    for k, ref in enumerate((base_0_ref, base_1_ref, base_2_ref, base_3_ref)):
        ref[...] = held[(me + k) & 3]
    input_ref[...] = first_input
    diff_q_ref[...] = diff_q
    diff_k_ref[...] = diff_k
    diff_v_ref[...] = diff_v
    context_ref[...] = context
    diff_low_ref[...] = diff_low
    vectors = [
        v[:, 128 * t : 128 * (t + 1)]
        for v in (grad_gain_attn, grad_gain_score, grad_w_score)
        for t in range(width // 128)
    ]
    vectors_ref[...] = jnp.concatenate(vectors + [jnp.zeros((32 - len(vectors), 128), F32)], axis=0)


FIRST = 48


def gradients_kernel(
    core_ref, input_ref, diff_q_ref, diff_k_ref, diff_v_ref, context_ref, diff_low_ref, vectors_ref,
    keep_x_ref, send_x_ref, keep_y_ref, send_y_ref, grads,
):
    first_input = input_ref[...]
    grads[0] = dot(first_input, diff_q_ref[...], 0, 0)
    grads[1] = dot(first_input, diff_k_ref[...], 0, 0)
    grads[2] = dot(first_input, diff_v_ref[...], 0, 0)
    grads[3] = dot(context_ref[...], diff_low_ref[...], 0, 0)
    first_core = core_ref[0] == 0

    def assemble(at, carry):
        chunk = [grads[i, pl.ds(pl.multiple_of(24 * at, 8), 24), :] for i in range(4)]
        halves = [jnp.concatenate([g[12 * c : 12 * (c + 1)] for g in chunk], axis=0) for c in (0, 1)]
        y, z = at >> 3, at & 7
        for m in range(4):
            blocks = []
            for rows48 in halves:
                tiles = []
                for h in range(9 * m, 9 * m + 9):
                    rb, t = h // 6, h % 6
                    tiles.append(rows48[8 * rb : 8 * rb + 8, 128 * t : 128 * (t + 1)])
                tiles.append(vectors_ref[8 * m : 8 * m + 8, :])
                blocks.append(jnp.concatenate(tiles, axis=0).astype(BF))
            keep = jnp.where(first_core, blocks[0], blocks[1])
            send = jnp.where(first_core, blocks[1], blocks[0])
            keep_x_ref[m, at] = keep[:FIRST]
            send_x_ref[m, at] = send[:FIRST]
            keep_y_ref[y, 8 * m + z] = keep[FIRST:]
            send_y_ref[y, 8 * m + z] = send[FIRST:]
        return carry

    lax.fori_loop(0, keep_x_ref.shape[1], assemble, 0)


def plus(*refs):
    total = refs[0].astype(F32)
    for r in refs[1:]:
        total = total + r.astype(F32)
    return total.astype(BF)


def cores_kernel(me_ref, keep_ref, other_ref, own_ref, right_ref, left_ref, far_a_ref, far_b_ref):
    me = me_ref[0]
    n = far_a_ref.shape[0]

    def add(i, carry):
        for k, ref in ((0, own_ref), (1, right_ref), (3, left_ref)):
            at = (me + k) & 3
            ref[i] = plus(keep_ref[at, i], other_ref[at, i])
            ref[i + n] = plus(keep_ref[at, i + n], other_ref[at, i + n])
        at = (me + 2) & 3
        far_a_ref[i] = plus(keep_ref[at, i], other_ref[at, i])
        far_b_ref[i] = plus(keep_ref[at, i + n], other_ref[at, i + n])
        return carry

    lax.fori_loop(0, n, add, 0)


def passing_kernel(right_ref, left_ref, far_a_ref, far_b_ref, right_out, left_out):
    n = far_a_ref.shape[0]
    right_out[:n] = plus(right_ref[:n], far_a_ref[...])
    right_out[n:] = right_ref[n:]
    left_out[:n] = left_ref[:n]
    left_out[n:] = plus(left_ref[n:], far_b_ref[...])


def three_kernel(a_ref, b_ref, c_ref, out_ref):
    out_ref[...] = plus(a_ref[...], b_ref[...], c_ref[...])


def last_kernel(a_ref, b_ref, out_ref):
    for ref, at in ((a_ref, 0), (b_ref, FIRST)):
        total = ref[0].astype(F32)
        for i in range(1, ref.shape[0]):
            total = total + ref[i].astype(F32)
        out_ref[at : at + ref.shape[1], :] = total.astype(BF)


def ring_sum(me, keep, other, axis):
    _, n, rows, _ = keep.shape
    block, half = shape((n, rows, 128)), shape((n // 2, rows, 128))
    size = n * rows * 128 * 2
    own, right, left, far_a, far_b = call(
        cores_kernel, [block, block, block, half, half], (me, keep, other), 24, size, 12 * size, scalar=True
    )
    far_a, far_b = shift(far_a, axis, 1), shift(far_b, axis, 3)
    right, left = call(passing_kernel, [block, block], (right, left, far_a, far_b), 16, size, 5 * size)
    right, left = shift(right, axis, 1), shift(left, axis, 3)
    return call(three_kernel, block, (own, right, left), 16, size, 4 * size)


def finish_kernel(me_ref, a_ref, b_ref, c_ref, d_ref, q_ref, k_ref, v_ref, o_ref, vec_ref, held):
    collect(me_ref[0], (a_ref, b_ref, c_ref, d_ref), held)
    blocks = held[...].astype(F32)
    tiles = [blocks[m, 8 * i : 8 * i + 8] for m in range(4) for i in range(9)]
    rows48 = jnp.concatenate([jnp.concatenate(tiles[6 * rb : 6 * rb + 6], axis=1) for rb in range(6)], axis=0)
    for i, ref in enumerate((q_ref, k_ref, v_ref, o_ref)):
        ref[...] = rows48[12 * i : 12 * (i + 1)]
    vec_ref[...] = jnp.concatenate([blocks[m, 72:] for m in range(4)], axis=0)


def shape(dims, kind=BF):
    return jax.ShapeDtypeStruct(dims, kind)


def swap(x, axes):
    return lax.all_to_all(x, axes, split_axis=0, concat_axis=0, tiled=True)


def body(
    cand_item,
    list_place,
    item_table,
    query_vec,
    labels,
    query_weight,
    key_weight,
    value_weight,
    output_weight,
    gain_attn,
    gain_score,
    w_score,
):
    queries, size = cand_item.shape
    stored, slab = item_table.shape
    width = query_vec.shape[1]
    n_dp = lax.axis_size(ROWS)
    n_mp = lax.axis_size("x")
    n_yz = lax.axis_size(("y", "z"))
    slots = n_dp * CAP

    along_x = lax.axis_index("x").astype(jnp.int32).reshape(1)
    along_y = lax.axis_index("y").astype(jnp.int32).reshape(1)
    core = lax.axis_index("c").astype(jnp.int32).reshape(1)

    ids = exchange([cand_item] * 4, "x")
    request, slot = call(
        routing_kernel,
        [shape((n_dp, CAP), jnp.int32), shape((n_mp * queries, size), jnp.int32)],
        (along_x, *ids, list_place.reshape(1, -1)),
        24, 3 * 10**8, 10**6, [pltpu.VMEM((n_mp, queries, size), jnp.int32)], True,
    )
    asked = swap(request, ROWS)
    found = call(
        owner_kernel, shape((n_dp, 48, 128)), (asked, item_table), 40, 2 * 10**9, 2 * 10**6
    )
    fetched = swap(found, ROWS)
    pieces = call(
        pieces_kernel, [shape((384, 128))] * n_mp, (along_x, slot, fetched), 40, 10**9, 2 * 10**6, (), True
    )
    rows_in = exchange(pieces, "x")
    acts = shape((queries * size, width))
    outs = call(
        step_kernel,
        [shape((queries, 128), F32), shape((queries, width), F32)]
        + [shape((384, 128))] * n_mp
        + [acts] * 6
        + [shape((32, 128), F32)],
        (
            along_x, *rows_in, query_vec, labels,
            query_weight, key_weight, value_weight, output_weight,
            gain_attn.reshape(1, -1), gain_score.reshape(1, -1), w_score.reshape(1, -1),
        ),
        48, 4 * 10**9, 10**7,
        [
            pltpu.VMEM((n_mp, 384, 128), BF),
            pltpu.VMEM((HEADS * queries // 2, 128, 256), F32),
            pltpu.VMEM((HEADS * queries // 2, 128, 256), F32),
        ],
        True,
    )
    losses, query_grad, diff_base, kept = outs[0], outs[1], outs[2:6], outs[6:]

    column_grads = exchange(diff_base, "x")
    outgoing = call(
        slots_kernel, shape((n_dp, 48, 128)), (along_x, slot, *column_grads), 40, 10**9, 2 * 10**6,
        [pltpu.VMEM((n_mp, 384, 128), BF)], True,
    )
    arrived = swap(outgoing, ROWS)
    table_grad = call(
        landing_kernel,
        shape((stored, slab), F32),
        (asked.reshape(slots // 128, 128), arrived),
        40, 2 * 10**9, 4 * 10**6,
    )

    first, second = shape((4, n_yz, FIRST, 128)), shape((4, n_yz, 80 - FIRST, 128))
    keep_x, send_x, keep_y, send_y = call(
        gradients_kernel, [first, first, second, second], (core, *kept), 48, 2 * 10**9, 10**7,
        [pltpu.VMEM((4, width, width), F32)], True,
    )
    other_x = lax.ppermute(send_x, "c", [(0, 1), (1, 0)])
    other_y = lax.ppermute(send_y, "c", [(0, 1), (1, 0)])
    over_x = ring_sum(along_x, keep_x, other_x, "x")
    over_y = ring_sum(along_y, keep_y, other_y, "y")
    parts_x = swap(over_x, ("y", "z"))
    parts_y = swap(over_y, ("x", "z"))
    over_all = call(last_kernel, shape((80, 128)), (parts_x, parts_y), 8, 10**6, 10**6)
    blocks = exchange([over_all] * 4, "x")
    rows = width // n_dp
    finished = call(
        finish_kernel,
        [shape((rows, width), F32)] * 4 + [shape((32, 128), F32)],
        (along_x, *blocks), 8, 10**6, 10**6, [pltpu.VMEM((n_mp, 80, 128), BF)], True,
    )
    vectors = finished[4].reshape(-1)
    return (
        losses[:, 0],
        table_grad,
        query_grad,
        finished[0],
        finished[1],
        finished[2],
        finished[3],
        vectors[:width],
        vectors[width : 2 * width],
        vectors[2 * width : 3 * width],
    )


def solution(mesh):
    grid = Mesh(mesh.devices.reshape(4, 8, 2, 4), ("y", "z", "c", "x"))
    each = P(("y", "z", "c", "x"), None)
    placed = (each, P(), P(ROWS, "x"), each, each, P(), P(), P(), P(), P(), P(), P())
    return jax.shard_map(
        body,
        mesh=grid,
        in_specs=placed,
        out_specs=(
            P(("y", "z", "c", "x")),
            P(ROWS, "x"),
            each,
            P(ROWS, None),
            P(ROWS, None),
            P(ROWS, None),
            P(ROWS, None),
            P(),
            P(),
            P(),
        ),
        check_vma=False,
    )
```

```python
import jax
import jax.numpy as jnp
from jax import lax
from jax.experimental import pallas as pl
from jax.experimental.pallas import tpu as pltpu
from jax.sharding import Mesh
from jax.sharding import PartitionSpec as P

HEADS = 12
LIST_LEN = 256
EPSILON = 1e-06
SCORE_CAP = 20.0
RANK_CAP = 30.0

ROWS = ("y", "z", "c")
CAP = 32
SLAB = 192
BF = jnp.bfloat16
F32 = jnp.float32
MIB = 1024 * 1024


def dot(a, b, ca=1, cb=0):
    return lax.dot_general(a, b, (((ca,), (cb,)), ((), ())), preferred_element_type=F32)


def iota(shape, dim):
    return lax.broadcasted_iota(jnp.int32, shape, dim)


def whole(n):
    return [pl.BlockSpec(memory_space=pltpu.VMEM)] * n


def call(kernel, out_shape, args, mib, flops, size, scratch=(), scalars=0, awaited=()):
    outs = out_shape if isinstance(out_shape, (list, tuple)) else [out_shape]
    specs = whole(len(outs))
    in_specs = [pl.BlockSpec(memory_space=pltpu.SMEM)] * scalars + whole(len(args) - scalars)
    in_specs += [pl.BlockSpec(memory_space=pl.ANY)] * len(awaited)

    def run(*refs):
        kernel(*refs[: len(args)], *refs[len(args) + len(awaited) :])

    return pl.pallas_call(
        run,
        out_shape=out_shape,
        in_specs=in_specs,
        out_specs=specs if isinstance(out_shape, (list, tuple)) else specs[0],
        scratch_shapes=list(scratch),
        compiler_params=pltpu.CompilerParams(vmem_limit_bytes=mib * MIB),
        cost_estimate=pl.CostEstimate(flops=flops, bytes_accessed=size, transcendentals=0),
    )(*args, *awaited)


def shift(x, axis, by):
    return lax.ppermute(x, axis, [(i, (i + by) % 4) for i in range(4)])


def exchange(blocks, axis):
    return [blocks[0]] + [shift(blocks[k], axis, k) for k in (1, 2, 3)]


def collect(me, refs, held):
    for k, ref in enumerate(refs):
        held[(me - k) & 3] = ref[...]


def low_half(shape):
    return iota(shape, len(shape) - 1) < 64


def swap_halves(t):
    return jnp.concatenate([t[..., 64:], t[..., :64]], axis=-1)


def spread_tail(t):
    t = t.astype(F32)
    other = swap_halves(t)
    low = low_half(t.shape)
    return jnp.concatenate([jnp.where(low, t, other), jnp.where(low, other, t)], axis=1)


def unpack(block):
    b, rows, _ = block.shape
    n = rows // 3
    main = block[:, : 2 * n, :].reshape(b * 2 * n, 128)
    tail = spread_tail(block[:, 2 * n :, :]).astype(BF).reshape(b * 2 * n, 128)
    return jnp.concatenate([main, tail], axis=1)


def pack(full, n):
    tail = full[:, 128:]
    tail = jnp.where(low_half((n, 128)), tail[:n], tail[n:])
    return jnp.concatenate([full[:, :128], tail], axis=0).astype(BF)


def as_column(row):
    return jnp.transpose(jnp.broadcast_to(row, (128, 128)))


def routing_kernel(me_ref, a_ref, b_ref, c_ref, d_ref, place_ref, request_ref, slot_ref, held):
    collect(me_ref[0], (a_ref, b_ref, c_ref, d_ref), held)
    place = place_ref[...]
    lists = place.shape[1]
    lane = iota((128, 128), 1)
    owner_of_list = jnp.broadcast_to(place >> 3, (128, lists))
    row = iota((128, lists), 0)
    lookup = jnp.where(owner_of_list == row, 1.0, 0.0)
    lookup = jnp.where(row == 64, jnp.broadcast_to(place & 7, (128, lists)).astype(F32), lookup)
    lookup = lookup.astype(BF)
    before = (iota((128, 128), 1) < iota((128, 128), 0)).astype(F32).astype(BF)
    carry = jnp.zeros((1, 128), F32)
    request = jnp.zeros((128, 128), F32)
    for q in range(slot_ref.shape[0]):
        ids = as_column(held[q // 2, q % 2 : q % 2 + 1, :])
        list_id = ids >> 8
        chosen = jnp.concatenate(
            [(list_id == lane + 128 * t).astype(F32).astype(BF) for t in range(lists // 128)], axis=1
        )
        found = dot(chosen, lookup, 1, 1)
        sub = jnp.sum(jnp.where(lane == 64, found, 0.0), 1, keepdims=True)
        onehot = jnp.where(lane < 64, found, 0.0)
        onehot_low = onehot.astype(BF)
        ahead = dot(before, onehot_low) + carry
        carry = carry + jnp.sum(onehot, 0, keepdims=True)
        rank = jnp.sum(onehot * ahead, 1, keepdims=True)
        owner = jnp.sum(onehot * lane.astype(F32), 1, keepdims=True)
        slot = jnp.broadcast_to(owner * CAP + rank, (128, 128))
        slot_ref[q : q + 1, :] = jnp.transpose(slot)[0:1, :].astype(jnp.int32)
        rank = rank.astype(jnp.int32)
        place_in = (ids & 255).astype(F32)
        entry = jnp.where(rank == lane, sub + 1.0, jnp.where(rank == lane - CAP, place_in, 0.0))
        request = request + dot(onehot_low, entry.astype(BF), 0, 0)
    high = request[:64, :CAP]
    low = request[:64, CAP : 2 * CAP]
    asked = (high - 1.0) * LIST_LEN + low
    request_ref[...] = jnp.where(high > 0.5, asked, -1.0).astype(jnp.int32)


def owner_kernel(asked_ref, table_ref, out_ref):
    groups = asked_ref.shape[0]
    part = groups // 4
    asked = asked_ref[...]
    asked = jnp.concatenate([asked[part * k : part * (k + 1)] for k in range(4)], axis=1)
    table = table_ref[...]
    stored = table.shape[1]
    table = jnp.concatenate([table, table[128:]], axis=0)
    step = 4
    for r in range(0, part, step):
        column = jnp.concatenate([as_column(asked[r + i : r + i + 1]) for i in range(step)], axis=0)
        lane = iota((128 * step, 128), 1)
        chosen = jnp.concatenate(
            [(column == lane + 128 * t).astype(F32).astype(BF) for t in range(stored // 128)], axis=1
        )
        rows = dot(chosen, table, 1, 1)
        for i in range(step):
            for k in range(4):
                at = 128 * i + CAP * k
                out_ref[part * k + r + i] = pack(rows[at : at + CAP], CAP // 2)


def pieces_kernel(me_ref, slot_ref, fetched_ref, *out_refs):
    fetched = unpack(fetched_ref[...])
    slots = fetched.shape[0]
    for k, out_ref in enumerate(out_refs):
        m = (me_ref[0] + k) & 3
        column = jnp.concatenate([as_column(slot_ref[pl.ds(2 * m + i, 1), :]) for i in (0, 1)], axis=0)
        lane = iota((256, 128), 1)
        chosen = jnp.concatenate(
            [(column == lane + 128 * t).astype(F32).astype(BF) for t in range(slots // 128)], axis=1
        )
        out_ref[...] = pack(dot(chosen, fetched), 128)


def slots_kernel(me_ref, slot_ref, a_ref, b_ref, c_ref, d_ref, out_ref, held):
    collect(me_ref[0], (a_ref, b_ref, c_ref, d_ref), held)
    grads = unpack(held[...])
    groups = out_ref.shape[0]
    step = 16 * CAP
    for r in range(0, groups * CAP, step):
        row = iota((step, 128), 0) + r
        chosen = jnp.concatenate(
            [
                (jnp.broadcast_to(slot_ref[q : q + 1, :], (step, 128)) == row).astype(F32).astype(BF)
                for q in range(slot_ref.shape[0])
            ],
            axis=1,
        )
        rows = dot(chosen, grads)
        for i in range(16):
            out_ref[r // CAP + i] = pack(rows[CAP * i : CAP * (i + 1)], CAP // 2)


def landing_kernel(asked_ref, arrived_ref, out_ref):
    arrived = unpack(arrived_ref[...])
    stored = out_ref.shape[1]
    slots = arrived.shape[0]
    column = jnp.concatenate([as_column(asked_ref[q : q + 1, :]) for q in range(asked_ref.shape[0])], axis=0)
    step = 512
    lane = iota((slots, 128), 1)
    for r in range(0, stored, step):
        chosen = jnp.concatenate(
            [(column == lane + (r + 128 * t)).astype(F32).astype(BF) for t in range(step // 128)], axis=1
        )
        out_ref[:, r : r + step] = dot(arrived, chosen, 0, 0)[:SLAB]


def lane_mean(x):
    return jnp.sum(x, 1, keepdims=True) * (1.0 / x.shape[1])


def step_kernel(
    me_ref,
    core_ref,
    a_ref,
    b_ref,
    c_ref,
    d_ref,
    query_ref,
    labels_ref,
    wq_ref,
    wk_ref,
    wv_ref,
    wo_ref,
    gain_attn_ref,
    gain_score_ref,
    w_score_ref,
    losses_ref,
    query_grad_ref,
    base_0_ref,
    base_1_ref,
    base_2_ref,
    base_3_ref,
    keep_ref,
    send_ref,
    vectors_ref,
    held,
    scores_t,
    attend_t,
):
    me = me_ref[0]
    collect(me, (a_ref, b_ref, c_ref, d_ref), held)
    queries, width = query_ref.shape
    size = 128
    head = width // HEADS
    pairs = HEADS // 2
    shrink = head ** (-0.5)
    low = low_half((size, 128))

    parts = []
    for m in range(4):
        main = held[m, :256, :].astype(F32)
        tail = held[m, 256:, :].astype(F32)
        parts += [main, jnp.concatenate([tail[:, :64], tail[:, 64:]], axis=0)]
    rows_in = jnp.concatenate(parts, axis=1)
    vecs = query_ref[...].astype(F32)
    vecs = jnp.concatenate([jnp.broadcast_to(vecs[q : q + 1], (size, width)) for q in range(queries)], axis=0)
    base = rows_in + vecs
    inv_one = 1.0 / jnp.sqrt(lane_mean(base * base) + EPSILON)
    normed_one = base * inv_one
    gain_attn = gain_attn_ref[...]
    first_input = (normed_one * gain_attn).astype(BF)
    q_all = dot(first_input, wq_ref[...]).astype(BF)
    k_all = dot(first_input, wk_ref[...]).astype(BF)
    v_all = dot(first_input, wv_ref[...]).astype(BF)

    def cut(x, q, p):
        return x[size * q : size * (q + 1), 128 * p : 128 * (p + 1)]

    zero = jnp.zeros((size, 128), BF)

    def heads_apart(x):
        return jnp.concatenate([jnp.where(low, x, zero), jnp.where(low, zero, x)], axis=0)

    def heads_joined(x):
        return jnp.where(low, x[:size], x[size:])

    context = []
    for q in range(queries):
        line = []
        for p in range(pairs):
            logits = dot(cut(k_all, q, p), heads_apart(cut(q_all, q, p)), 1, 1)
            th = jnp.tanh(logits * (shrink / SCORE_CAP))
            raised = jnp.exp(SCORE_CAP * th)
            attend = raised * (1.0 / jnp.sum(raised, 0, keepdims=True))
            scores_t[q * pairs + p] = th
            attend_t[q * pairs + p] = attend
            line.append(heads_joined(dot(attend.astype(BF), cut(v_all, q, p), 0, 0)))
        context.append(jnp.concatenate(line, axis=1))
    context = jnp.concatenate(context, axis=0).astype(BF)

    mixed = base + dot(context, wo_ref[...])
    inv_two = 1.0 / jnp.sqrt(lane_mean(mixed * mixed) + EPSILON)
    normed_two = mixed * inv_two
    gain_score = gain_score_ref[...]
    w_score = w_score_ref[...]
    scaled_two = normed_two * gain_score
    capped_scores = jnp.tanh(jnp.sum(scaled_two * w_score, 1, keepdims=True) * (1.0 / RANK_CAP))
    scores = RANK_CAP * capped_scores
    raised = jnp.exp(scores)
    relevance = jnp.exp(labels_ref[...].astype(F32))
    target = relevance / jnp.sum(relevance, 1, keepdims=True)
    diffs = []
    for q in range(queries):
        at = slice(size * q, size * (q + 1))
        total = jnp.sum(raised[at], 0, keepdims=True)
        wanted = as_column(target[q : q + 1])[:, 0:1]
        loss = jnp.log(total) - jnp.sum(wanted * scores[at], 0, keepdims=True)
        losses_ref[q : q + 1, :] = jnp.broadcast_to(loss, (1, 128))
        diffs.append(raised[at] / total - wanted)
    diff_raw = jnp.concatenate(diffs, axis=0) * (1.0 - capped_scores * capped_scores)
    grad_w_score = jnp.sum(scaled_two * diff_raw, 0, keepdims=True)
    diff_scaled = diff_raw * w_score
    grad_gain_score = jnp.sum(normed_two * diff_scaled, 0, keepdims=True)
    diff_normed = diff_scaled * gain_score
    diff_mixed = (diff_normed - normed_two * lane_mean(diff_normed * normed_two)) * inv_two
    diff_low = diff_mixed.astype(BF)
    diff_context = dot(diff_low, wo_ref[...], 1, 1).astype(BF)

    diff_q, diff_k, diff_v = [], [], []
    for q in range(queries):
        line_q, line_k, line_v = [], [], []
        for p in range(pairs):
            th = scores_t[q * pairs + p]
            attend = attend_t[q * pairs + p]
            split = heads_apart(cut(diff_context, q, p))
            diff_attend = dot(cut(v_all, q, p), split, 1, 1)
            line_v.append(dot(attend.astype(BF), split))
            inner = diff_attend - jnp.sum(attend * diff_attend, 0, keepdims=True)
            diff_logits = (attend * inner * (1.0 - th * th) * shrink).astype(BF)
            line_q.append(heads_joined(dot(diff_logits, cut(k_all, q, p), 0, 0)))
            line_k.append(dot(diff_logits, heads_apart(cut(q_all, q, p))))
        diff_q.append(jnp.concatenate(line_q, axis=1))
        diff_k.append(jnp.concatenate(line_k, axis=1))
        diff_v.append(jnp.concatenate(line_v, axis=1))
    diff_q = jnp.concatenate(diff_q, axis=0).astype(BF)
    diff_k = jnp.concatenate(diff_k, axis=0).astype(BF)
    diff_v = jnp.concatenate(diff_v, axis=0).astype(BF)

    diff_input = dot(diff_q, wq_ref[...], 1, 1) + dot(diff_k, wk_ref[...], 1, 1) + dot(diff_v, wv_ref[...], 1, 1)
    grad_gain_attn = jnp.sum(normed_one * diff_input, 0, keepdims=True)
    diff_first = diff_input * gain_attn
    diff_base = diff_mixed + (diff_first - normed_one * lane_mean(diff_first * normed_one)) * inv_one
    for q in range(queries):
        query_grad_ref[q : q + 1, :] = jnp.sum(diff_base[size * q : size * (q + 1)], 0, keepdims=True)
    for m in range(4):
        slab = diff_base[:, SLAB * m : SLAB * (m + 1)]
        held[m, :256, :] = slab[:, :128].astype(BF)
        held[m, 256:, :] = jnp.concatenate([slab[:128, 128:], slab[128:, 128:]], axis=1).astype(BF)
    for k, ref in enumerate((base_0_ref, base_1_ref, base_2_ref, base_3_ref)):
        ref[...] = held[(me + k) & 3]
    first_core = core_ref[0] == 0
    first_pair = (first_input, first_input, diff_q, diff_k)
    second_pair = (first_input, context, diff_v, diff_low)
    for i in range(4):
        keep_ref[i] = jnp.where(first_core, first_pair[i], second_pair[i])
        send_ref[i] = jnp.where(first_core, second_pair[i], first_pair[i])
    vectors = [
        v[:, 128 * t : 128 * (t + 1)]
        for v in (grad_gain_attn, grad_gain_score, grad_w_score)
        for t in range(width // 128)
    ]
    vectors_ref[...] = jnp.concatenate(vectors + [jnp.zeros((32 - len(vectors), 128), F32)], axis=0)


FIRST = 48


def gradients_kernel(
    x_ref, y_ref, keep_ref, other_ref, vectors_ref,
    own_x, right_x, far_ax, far_bx, left_x, own_y, right_y, far_ay, far_by, left_y,
    grads, by_x, by_y,
):
    for j in (0, 1):
        left = jnp.concatenate([keep_ref[j], other_ref[j]], axis=0)
        right = jnp.concatenate([keep_ref[2 + j], other_ref[2 + j]], axis=0)
        grads[j] = dot(left, right, 0, 0)

    def assemble(at, carry):
        rows48 = jnp.concatenate([grads[j, pl.ds(pl.multiple_of(24 * at, 8), 24), :] for j in (0, 1)], axis=0)
        y, z = at >> 3, at & 7
        for m in range(4):
            tiles = []
            for h in range(9 * m, 9 * m + 9):
                rb, t = h // 6, h % 6
                tiles.append(rows48[8 * rb : 8 * rb + 8, 128 * t : 128 * (t + 1)])
            tiles.append(vectors_ref[8 * m : 8 * m + 8, :])
            block = jnp.concatenate(tiles, axis=0).astype(BF)
            by_x[m, at] = block[:FIRST]
            by_y[y, 8 * m + z] = block[FIRST:]
        return carry

    lax.fori_loop(0, by_x.shape[1], assemble, 0)
    n = far_ax.shape[0]
    for me, held, own, right, far_a, far_b, left in (
        (x_ref[0], by_x, own_x, right_x, far_ax, far_bx, left_x),
        (y_ref[0], by_y, own_y, right_y, far_ay, far_by, left_y),
    ):
        own[...] = held[me]
        right[...] = held[(me + 1) & 3]
        far_a[...] = held[(me + 2) & 3, :n]
        far_b[...] = held[(me + 2) & 3, n:]
        left[...] = held[(me + 3) & 3]


def plus(*refs):
    total = refs[0].astype(F32)
    for r in refs[1:]:
        total = total + r.astype(F32)
    return total.astype(BF)


def passing_kernel(right_ref, left_ref, far_a_ref, far_b_ref, right_out, left_out):
    n = far_a_ref.shape[0]
    right_out[:n] = plus(right_ref[:n], far_a_ref[...])
    right_out[n:] = right_ref[n:]
    left_out[:n] = left_ref[:n]
    left_out[n:] = plus(left_ref[n:], far_b_ref[...])


def three_kernel(a_ref, b_ref, c_ref, out_ref):
    out_ref[...] = plus(a_ref[...], b_ref[...], c_ref[...])


def second_kernel(me_ref, own_ref, right_ref, left_ref, *refs):
    out_refs, first_ref = refs[:4], refs[4]
    first_ref[...] = plus(own_ref[...], right_ref[...], left_ref[...])
    for k, ref in enumerate(out_refs):
        ref[...] = first_ref[(me_ref[0] + k) & 3]


def third_kernel(*refs):
    out_ref = refs[-1]
    x_refs, y_refs = refs[:4], refs[4:8]
    out_ref[:, :FIRST, :] = plus(*[r[...] for r in x_refs])
    out_ref[:, FIRST:, :] = plus(*[r[...] for r in y_refs])


def last_kernel(parts_ref, out_ref):
    out_ref[...] = plus(*[parts_ref[i] for i in range(parts_ref.shape[0])])


def finish_kernel(me_ref, core_ref, a_ref, b_ref, c_ref, d_ref, q_ref, k_ref, v_ref, o_ref, vec_ref, held):
    collect(me_ref[0], (a_ref, b_ref, c_ref, d_ref), held)
    blocks = held[...].astype(F32)
    first_core = core_ref[0] == 0
    rows48, vectors = [], []
    for at in (0, 80):
        tiles = [blocks[m, at + 8 * i : at + 8 * i + 8] for m in range(4) for i in range(9)]
        rows48.append(
            jnp.concatenate([jnp.concatenate(tiles[6 * rb : 6 * rb + 6], axis=1) for rb in range(6)], axis=0)
        )
        vectors.append(jnp.concatenate([blocks[m, at + 72 : at + 80] for m in range(4)], axis=0))
    own, other = rows48
    first_pair = jnp.where(first_core, own, other)
    second_pair = jnp.where(first_core, other, own)
    for pair, refs in ((first_pair, (q_ref, k_ref)), (second_pair, (v_ref, o_ref))):
        for i, ref in enumerate(refs):
            ref[...] = jnp.where(first_core, pair[24 * i : 24 * i + 12], pair[24 * i + 12 : 24 * i + 24])
    vec_ref[...] = vectors[0] + vectors[1]


def shape(dims, kind=BF):
    return jax.ShapeDtypeStruct(dims, kind)


def swap(x, axes):
    return lax.all_to_all(x, axes, split_axis=0, concat_axis=0, tiled=True)


def body(
    cand_item,
    list_place,
    item_table,
    query_vec,
    labels,
    query_weight,
    key_weight,
    value_weight,
    output_weight,
    gain_attn,
    gain_score,
    w_score,
):
    queries, size = cand_item.shape
    stored, slab = item_table.shape
    width = query_vec.shape[1]
    n_dp = lax.axis_size(ROWS)
    n_mp = lax.axis_size("x")
    n_yz = lax.axis_size(("y", "z"))
    slots = n_dp * CAP

    along_x = lax.axis_index("x").astype(jnp.int32).reshape(1)
    along_y = lax.axis_index("y").astype(jnp.int32).reshape(1)
    core = lax.axis_index("c").astype(jnp.int32).reshape(1)

    ids = exchange([cand_item] * 4, "x")
    request, slot = call(
        routing_kernel,
        [shape((n_dp, CAP), jnp.int32), shape((n_mp * queries, size), jnp.int32)],
        (along_x, *ids, list_place.reshape(1, -1)),
        8, 3 * 10**8, 10**6, [pltpu.VMEM((n_mp, queries, size), jnp.int32)], 1,
    )
    asked = swap(request, ROWS)
    found = call(
        owner_kernel, shape((n_dp, 48, 128)), (asked, item_table.T), 16, 2 * 10**9, 2 * 10**6
    )
    fetched = swap(found, ROWS)
    pieces = call(
        pieces_kernel, [shape((384, 128))] * n_mp, (along_x, slot, fetched), 16, 10**9, 2 * 10**6, (), 1
    )
    rows_in = exchange(pieces, "x")
    acts = shape((4, queries * size, width))
    outs = call(
        step_kernel,
        [shape((queries, 128), F32), shape((queries, width), F32)]
        + [shape((384, 128))] * n_mp
        + [acts] * 2
        + [shape((32, 128), F32)],
        (
            along_x, core, *rows_in, query_vec, labels,
            query_weight, key_weight, value_weight, output_weight,
            gain_attn.reshape(1, -1), gain_score.reshape(1, -1), w_score.reshape(1, -1),
        ),
        32, 4 * 10**9, 10**7,
        [
            pltpu.VMEM((n_mp, 384, 128), BF),
            pltpu.VMEM((HEADS * queries // 2, 128, 256), F32),
            pltpu.VMEM((HEADS * queries // 2, 128, 256), F32),
        ],
        2,
    )
    losses, query_grad, diff_base = outs[0], outs[1], outs[2:6]
    keep, send, vectors = outs[6:]

    column_grads = exchange(diff_base, "x")
    outgoing = call(
        slots_kernel, shape((n_dp, 48, 128)), (along_x, slot, *column_grads), 16, 10**9, 2 * 10**6,
        [pltpu.VMEM((n_mp, 384, 128), BF)], 1,
    )
    arrived = swap(outgoing, ROWS)
    table_grad = call(
        landing_kernel,
        shape((slab, stored), F32),
        (asked.reshape(slots // 128, 128), arrived),
        20, 2 * 10**9, 4 * 10**6,
    ).T

    other = lax.ppermute(send, "c", [(0, 1), (1, 0)])
    pieces = []
    for count in (FIRST, 80 - FIRST):
        block, half = shape((n_yz, count, 128)), shape((n_yz // 2, count, 128))
        pieces += [block, block, half, half, block]
    rings = call(
        gradients_kernel, pieces, (along_x, along_y, keep, other, vectors), 28, 2 * 10**9, 10**7,
        [
            pltpu.VMEM((2, width, width), F32),
            pltpu.VMEM((4, n_yz, FIRST, 128), BF),
            pltpu.VMEM((4, n_yz, 80 - FIRST, 128), BF),
        ],
        2, (column_grads[1],),
    )
    far = [
        (shift(far_a, axis, 1), shift(far_b, axis, 3))
        for axis, (_, _, far_a, far_b, _) in (("x", rings[:5]), ("y", rings[5:]))
    ]
    near = []
    for axis, (_, right, _, _, left), passed in zip("xy", (rings[:5], rings[5:]), far):
        right, left = call(
            passing_kernel, [shape(right.shape)] * 2, (right, left, *passed), 8, 10**6, 10**7, awaited=(outgoing,)
        )
        near.append((shift(right, axis, 1), shift(left, axis, 3)))
    summed = []
    for axis, me, own, arrive, count in (
        ("y", along_y, rings[0], near[0], FIRST),
        ("x", along_x, rings[5], near[1], 80 - FIRST),
    ):
        dims = (4, n_yz // 4, count, 128)
        blocks = call(
            second_kernel, [shape(dims[1:])] * 4,
            (me, own.reshape(dims), arrive[0].reshape(dims), arrive[1].reshape(dims)), 8, 10**6, 10**7,
            [pltpu.VMEM(dims, BF)], 1, (arrived,),
        )
        summed += exchange(blocks, axis)
    along = call(third_kernel, shape((n_yz // 4, 80, 128)), tuple(summed), 8, 10**6, 10**6)
    over_all = call(last_kernel, shape((80, 128)), (swap(along, "z"),), 4, 10**6, 10**6)
    other = lax.ppermute(over_all, "c", [(0, 1), (1, 0)])
    blocks = exchange([jnp.concatenate([over_all, other], axis=0)] * 4, "x")
    rows = width // n_dp
    finished = call(
        finish_kernel,
        [shape((rows, width), F32)] * 4 + [shape((32, 128), F32)],
        (along_x, core, *blocks), 4, 10**6, 10**6, [pltpu.VMEM((n_mp, 160, 128), BF)], 2,
    )
    vectors = finished[4].reshape(-1)
    return (
        losses[:, 0],
        table_grad,
        query_grad,
        finished[0],
        finished[1],
        finished[2],
        finished[3],
        vectors[:width],
        vectors[width : 2 * width],
        vectors[2 * width : 3 * width],
    )


def solution(mesh):
    grid = Mesh(mesh.devices.reshape(4, 8, 2, 4), ("y", "z", "c", "x"))
    each = P(("y", "z", "c", "x"), None)
    placed = (each, P(), P(ROWS, "x"), each, each, P(), P(), P(), P(), P(), P(), P())
    return jax.shard_map(
        body,
        mesh=grid,
        in_specs=placed,
        out_specs=(
            P(("y", "z", "c", "x")),
            P(ROWS, "x"),
            each,
            P(ROWS, None),
            P(ROWS, None),
            P(ROWS, None),
            P(ROWS, None),
            P(),
            P(),
            P(),
        ),
        check_vma=False,
    )
```

```python
import jax
import jax.numpy as jnp
from jax import lax
from jax.experimental import pallas as pl
from jax.experimental.pallas import tpu as pltpu
from jax.sharding import Mesh
from jax.sharding import PartitionSpec as P

HEADS = 12
LIST_LEN = 256
EPSILON = 1e-06
SCORE_CAP = 20.0
RANK_CAP = 30.0

ROWS = ("y", "z", "c")
CAP = 32
SLAB = 192
BF = jnp.bfloat16
F32 = jnp.float32
MIB = 1024 * 1024


def dot(a, b, ca=1, cb=0):
    return lax.dot_general(a, b, (((ca,), (cb,)), ((), ())), preferred_element_type=F32)


def iota(shape, dim):
    return lax.broadcasted_iota(jnp.int32, shape, dim)


def whole(n):
    return [pl.BlockSpec(memory_space=pltpu.VMEM)] * n


def call(kernel, out_shape, args, mib, flops, size, scratch=(), scalars=0, left=(), awaited=()):
    outs = out_shape if isinstance(out_shape, (list, tuple)) else [out_shape]
    specs = whole(len(outs))
    in_specs = [pl.BlockSpec(memory_space=pltpu.SMEM)] * scalars + whole(len(args) - scalars)
    for i in left:
        in_specs[i] = pl.BlockSpec(memory_space=pltpu.HBM)
    in_specs += [pl.BlockSpec(memory_space=pl.ANY)] * len(awaited)

    def run(*refs):
        kernel(*refs[: len(args)], *refs[len(args) + len(awaited) :])

    return pl.pallas_call(
        run,
        out_shape=out_shape,
        in_specs=in_specs,
        out_specs=specs if isinstance(out_shape, (list, tuple)) else specs[0],
        scratch_shapes=list(scratch),
        compiler_params=pltpu.CompilerParams(vmem_limit_bytes=mib * MIB),
        cost_estimate=pl.CostEstimate(flops=flops, bytes_accessed=size, transcendentals=0),
    )(*args, *awaited)


def shift(x, axis, by):
    return lax.ppermute(x, axis, [(i, (i + by) % 4) for i in range(4)])


def exchange(blocks, axis):
    far = shift(blocks[2], axis, 2)
    return [blocks[0], shift(blocks[1], axis, 1), far, shift(blocks[3], axis, 3)]


def collect(me, refs, held):
    for k, ref in enumerate(refs):
        held[(me - k) & 3] = ref[...]


def low_half(shape):
    return iota(shape, len(shape) - 1) < 64


def swap_halves(t):
    return jnp.concatenate([t[..., 64:], t[..., :64]], axis=-1)


def spread_tail(t):
    t = t.astype(F32)
    other = swap_halves(t)
    low = low_half(t.shape)
    return jnp.concatenate([jnp.where(low, t, other), jnp.where(low, other, t)], axis=1)


def unpack(block):
    b, rows, _ = block.shape
    n = rows // 3
    main = block[:, : 2 * n, :].reshape(b * 2 * n, 128)
    tail = spread_tail(block[:, 2 * n :, :]).astype(BF).reshape(b * 2 * n, 128)
    return jnp.concatenate([main, tail], axis=1)


def pack(full, n):
    tail = full[:, 128:]
    tail = jnp.where(low_half((n, 128)), tail[:n], tail[n:])
    return jnp.concatenate([full[:, :128], tail], axis=0).astype(BF)


def as_column(row):
    return jnp.transpose(jnp.broadcast_to(row, (128, 128)))


def routing_kernel(me_ref, a_ref, b_ref, c_ref, d_ref, place_hbm, request_ref, slot_ref, held, place_ref, sem):
    me = me_ref[0]
    copies = [
        pltpu.make_async_copy(place_hbm, place_ref, sem.at[0]),
        pltpu.make_async_copy(a_ref, held.at[me], sem.at[1]),
    ]
    for c in copies:
        c.start()
    for k, ref in ((1, b_ref), (2, c_ref), (3, d_ref)):
        held[(me - k) & 3] = ref[...]
    for c in copies:
        c.wait()
    place = place_ref[...]
    lists = place.shape[1]
    lane = iota((128, 128), 1)
    owner_of_list = jnp.broadcast_to(place >> 3, (128, lists))
    row = iota((128, lists), 0)
    lookup = jnp.where(owner_of_list == row, 1.0, 0.0)
    lookup = jnp.where(row == 64, jnp.broadcast_to(place & 7, (128, lists)).astype(F32), lookup)
    lookup = lookup.astype(BF)
    before = (iota((128, 128), 1) < iota((128, 128), 0)).astype(F32).astype(BF)
    carry = jnp.zeros((1, 128), F32)
    request = jnp.zeros((128, 128), F32)
    for q in range(slot_ref.shape[0]):
        ids = as_column(held[q // 2, q % 2 : q % 2 + 1, :])
        list_id = ids >> 8
        chosen = jnp.concatenate(
            [(list_id == lane + 128 * t).astype(F32).astype(BF) for t in range(lists // 128)], axis=1
        )
        found = dot(chosen, lookup, 1, 1)
        sub = jnp.sum(jnp.where(lane == 64, found, 0.0), 1, keepdims=True)
        onehot = jnp.where(lane < 64, found, 0.0)
        onehot_low = onehot.astype(BF)
        ahead = dot(before, onehot_low) + carry
        carry = carry + jnp.sum(onehot, 0, keepdims=True)
        rank = jnp.sum(onehot * ahead, 1, keepdims=True)
        owner = jnp.sum(onehot * lane.astype(F32), 1, keepdims=True)
        slot = jnp.broadcast_to(owner * CAP + rank, (128, 128))
        slot_ref[q : q + 1, :] = jnp.transpose(slot)[0:1, :].astype(jnp.int32)
        rank = rank.astype(jnp.int32)
        place_in = (ids & 255).astype(F32)
        entry = jnp.where(rank == lane, sub + 1.0, jnp.where(rank == lane - CAP, place_in, 0.0))
        request = request + dot(onehot_low, entry.astype(BF), 0, 0)
    high = request[:64, :CAP]
    low = request[:64, CAP : 2 * CAP]
    asked = (high - 1.0) * LIST_LEN + low
    request_ref[...] = jnp.where(high > 0.5, asked, -1.0).astype(jnp.int32)


def four_groups(asked):
    part = asked.shape[0] // 4
    return jnp.concatenate([asked[part * k : part * (k + 1)] for k in range(4)], axis=1)


def owner_kernel(asked_ref, table_hbm, out_ref, table_ref, sem):
    copies = [
        pltpu.make_async_copy(table_hbm, table_ref.at[pl.ds(0, SLAB)], sem.at[0]),
        pltpu.make_async_copy(table_hbm.at[pl.ds(128, 64)], table_ref.at[pl.ds(SLAB, 64)], sem.at[1]),
    ]
    for c in copies:
        c.start()
    asked = four_groups(asked_ref[...])
    part = asked.shape[0]
    stored = table_ref.shape[1]
    step = 4
    for r in range(0, part, step):
        column = jnp.concatenate([as_column(asked[r + i : r + i + 1]) for i in range(step)], axis=0)
        lane = iota((128 * step, 128), 1)
        chosen = jnp.concatenate(
            [(column == lane + 128 * t).astype(F32).astype(BF) for t in range(stored // 128)], axis=1
        )
        if r == 0:
            for c in copies:
                c.wait()
        rows = dot(chosen, table_ref[...], 1, 1)
        for i in range(step):
            for k in range(4):
                at = 128 * i + CAP * k
                out_ref[part * k + r + i] = pack(rows[at : at + CAP], CAP // 2)


def pieces_kernel(me_ref, slot_ref, fetched_ref, *out_refs):
    fetched = unpack(fetched_ref[...])
    slots = fetched.shape[0]
    for k, out_ref in enumerate(out_refs):
        m = (me_ref[0] + k) & 3
        column = jnp.concatenate([as_column(slot_ref[pl.ds(2 * m + i, 1), :]) for i in (0, 1)], axis=0)
        lane = iota((256, 128), 1)
        chosen = jnp.concatenate(
            [(column == lane + 128 * t).astype(F32).astype(BF) for t in range(slots // 128)], axis=1
        )
        out_ref[...] = pack(dot(chosen, fetched), 128)


def slots_kernel(me_ref, slot_ref, a_ref, b_ref, c_ref, d_ref, out_ref, held):
    collect(me_ref[0], (a_ref, b_ref, c_ref, d_ref), held)
    grads = unpack(held[...])
    groups = out_ref.shape[0]
    step = 16 * CAP
    for r in range(0, groups * CAP, step):
        row = iota((step, 128), 0) + r
        chosen = jnp.concatenate(
            [
                (jnp.broadcast_to(slot_ref[q : q + 1, :], (step, 128)) == row).astype(F32).astype(BF)
                for q in range(slot_ref.shape[0])
            ],
            axis=1,
        )
        rows = dot(chosen, grads)
        for i in range(16):
            out_ref[r // CAP + i] = pack(rows[CAP * i : CAP * (i + 1)], CAP // 2)


def landing_kernel(asked_ref, arrived_ref, out_ref):
    arrived = unpack(arrived_ref[...])
    stored = out_ref.shape[1]
    slots = arrived.shape[0]
    asked = four_groups(asked_ref[...])
    part = asked.shape[0]
    columns = [as_column(asked[r : r + 1]) for r in range(part)]
    column = jnp.concatenate(
        [columns[g % part][CAP * (g // part) : CAP * (g // part + 1)] for g in range(4 * part)], axis=0
    )
    step = 512
    lane = iota((slots, 128), 1)
    for r in range(0, stored, step):
        chosen = jnp.concatenate(
            [(column == lane + (r + 128 * t)).astype(F32).astype(BF) for t in range(step // 128)], axis=1
        )
        out_ref[:, r : r + step] = dot(arrived, chosen, 0, 0)[:SLAB]


def lane_mean(x):
    return jnp.sum(x, 1, keepdims=True) * (1.0 / x.shape[1])


def step_kernel(
    me_ref,
    core_ref,
    a_ref,
    b_ref,
    c_ref,
    d_ref,
    query_ref,
    labels_ref,
    wq_hbm,
    wk_hbm,
    wv_hbm,
    wo_hbm,
    gain_attn_ref,
    gain_score_ref,
    w_score_ref,
    losses_ref,
    query_grad_ref,
    base_0_ref,
    base_1_ref,
    base_2_ref,
    base_3_ref,
    keep_ref,
    send_ref,
    vectors_ref,
    held,
    scores_t,
    attend_t,
    wq_ref,
    wk_ref,
    wv_ref,
    wo_ref,
    sem,
):
    sources = (wq_hbm, wk_hbm, wv_hbm, wo_hbm)
    weights = (wq_ref, wk_ref, wv_ref, wo_ref)
    copies = [pltpu.make_async_copy(a, b, sem.at[i]) for i, (a, b) in enumerate(zip(sources, weights))]
    for c in copies:
        c.start()
    me = me_ref[0]
    collect(me, (a_ref, b_ref, c_ref, d_ref), held)
    queries, width = query_ref.shape
    size = 128
    head = width // HEADS
    pairs = HEADS // 2
    shrink = head ** (-0.5)
    low = low_half((size, 128))

    parts = []
    for m in range(4):
        main = held[m, :256, :].astype(F32)
        tail = held[m, 256:, :].astype(F32)
        parts += [main, jnp.concatenate([tail[:, :64], tail[:, 64:]], axis=0)]
    rows_in = jnp.concatenate(parts, axis=1)
    vecs = query_ref[...].astype(F32)
    vecs = jnp.concatenate([jnp.broadcast_to(vecs[q : q + 1], (size, width)) for q in range(queries)], axis=0)
    base = rows_in + vecs
    inv_one = 1.0 / jnp.sqrt(lane_mean(base * base) + EPSILON)
    normed_one = base * inv_one
    gain_attn = gain_attn_ref[...]
    first_input = (normed_one * gain_attn).astype(BF)
    for c in copies:
        c.wait()
    q_all = dot(first_input, wq_ref[...]).astype(BF)
    k_all = dot(first_input, wk_ref[...]).astype(BF)
    v_all = dot(first_input, wv_ref[...]).astype(BF)

    def cut(x, q, p):
        return x[size * q : size * (q + 1), 128 * p : 128 * (p + 1)]

    zero = jnp.zeros((size, 128), BF)

    def heads_apart(x):
        return jnp.concatenate([jnp.where(low, x, zero), jnp.where(low, zero, x)], axis=0)

    def heads_joined(x):
        return jnp.where(low, x[:size], x[size:])

    context = []
    for q in range(queries):
        line = []
        for p in range(pairs):
            logits = dot(cut(k_all, q, p), heads_apart(cut(q_all, q, p)), 1, 1)
            th = jnp.tanh(logits * (shrink / SCORE_CAP))
            raised = jnp.exp(SCORE_CAP * th)
            attend = raised * (1.0 / jnp.sum(raised, 0, keepdims=True))
            scores_t[q * pairs + p] = th
            attend_t[q * pairs + p] = attend
            line.append(heads_joined(dot(attend.astype(BF), cut(v_all, q, p), 0, 0)))
        context.append(jnp.concatenate(line, axis=1))
    context = jnp.concatenate(context, axis=0).astype(BF)

    mixed = base + dot(context, wo_ref[...])
    inv_two = 1.0 / jnp.sqrt(lane_mean(mixed * mixed) + EPSILON)
    normed_two = mixed * inv_two
    gain_score = gain_score_ref[...]
    w_score = w_score_ref[...]
    scaled_two = normed_two * gain_score
    capped_scores = jnp.tanh(jnp.sum(scaled_two * w_score, 1, keepdims=True) * (1.0 / RANK_CAP))
    scores = RANK_CAP * capped_scores
    raised = jnp.exp(scores)
    relevance = jnp.exp(labels_ref[...].astype(F32))
    target = relevance / jnp.sum(relevance, 1, keepdims=True)
    diffs = []
    for q in range(queries):
        at = slice(size * q, size * (q + 1))
        total = jnp.sum(raised[at], 0, keepdims=True)
        wanted = as_column(target[q : q + 1])[:, 0:1]
        loss = jnp.log(total) - jnp.sum(wanted * scores[at], 0, keepdims=True)
        losses_ref[q : q + 1, :] = jnp.broadcast_to(loss, (1, 128))
        diffs.append(raised[at] / total - wanted)
    diff_raw = jnp.concatenate(diffs, axis=0) * (1.0 - capped_scores * capped_scores)
    grad_w_score = jnp.sum(scaled_two * diff_raw, 0, keepdims=True)
    diff_scaled = diff_raw * w_score
    grad_gain_score = jnp.sum(normed_two * diff_scaled, 0, keepdims=True)
    diff_normed = diff_scaled * gain_score
    diff_mixed = (diff_normed - normed_two * lane_mean(diff_normed * normed_two)) * inv_two
    diff_low = diff_mixed.astype(BF)
    diff_context = dot(diff_low, wo_ref[...], 1, 1).astype(BF)

    diff_q, diff_k, diff_v = [], [], []
    for q in range(queries):
        line_q, line_k, line_v = [], [], []
        for p in range(pairs):
            th = scores_t[q * pairs + p]
            attend = attend_t[q * pairs + p]
            split = heads_apart(cut(diff_context, q, p))
            diff_attend = dot(cut(v_all, q, p), split, 1, 1)
            line_v.append(dot(attend.astype(BF), split))
            inner = diff_attend - jnp.sum(attend * diff_attend, 0, keepdims=True)
            diff_logits = (attend * inner * (1.0 - th * th) * shrink).astype(BF)
            line_q.append(heads_joined(dot(diff_logits, cut(k_all, q, p), 0, 0)))
            line_k.append(dot(diff_logits, heads_apart(cut(q_all, q, p))))
        diff_q.append(jnp.concatenate(line_q, axis=1))
        diff_k.append(jnp.concatenate(line_k, axis=1))
        diff_v.append(jnp.concatenate(line_v, axis=1))
    diff_q = jnp.concatenate(diff_q, axis=0).astype(BF)
    diff_k = jnp.concatenate(diff_k, axis=0).astype(BF)
    diff_v = jnp.concatenate(diff_v, axis=0).astype(BF)

    diff_input = dot(diff_q, wq_ref[...], 1, 1) + dot(diff_k, wk_ref[...], 1, 1) + dot(diff_v, wv_ref[...], 1, 1)
    grad_gain_attn = jnp.sum(normed_one * diff_input, 0, keepdims=True)
    diff_first = diff_input * gain_attn
    diff_base = diff_mixed + (diff_first - normed_one * lane_mean(diff_first * normed_one)) * inv_one
    for q in range(queries):
        query_grad_ref[q : q + 1, :] = jnp.sum(diff_base[size * q : size * (q + 1)], 0, keepdims=True)
    for m in range(4):
        slab = diff_base[:, SLAB * m : SLAB * (m + 1)]
        held[m, :256, :] = slab[:, :128].astype(BF)
        held[m, 256:, :] = jnp.concatenate([slab[:128, 128:], slab[128:, 128:]], axis=1).astype(BF)
    for k, ref in enumerate((base_0_ref, base_1_ref, base_2_ref, base_3_ref)):
        ref[...] = held[(me + k) & 3]
    first_core = core_ref[0] == 0
    first_pair = (first_input, first_input, diff_q, diff_k)
    second_pair = (first_input, context, diff_v, diff_low)
    for i in range(4):
        keep_ref[i] = jnp.where(first_core, first_pair[i], second_pair[i])
        send_ref[i] = jnp.where(first_core, second_pair[i], first_pair[i])
    vectors = [
        v[:, 128 * t : 128 * (t + 1)]
        for v in (grad_gain_attn, grad_gain_score, grad_w_score)
        for t in range(width // 128)
    ]
    vectors_ref[...] = jnp.concatenate(vectors + [jnp.zeros((32 - len(vectors), 128), F32)], axis=0)


FIRST = 48


def gradients_kernel(
    x_ref, y_ref, keep_ref, other_ref, vectors_ref,
    own_x, right_x, far_ax, far_bx, left_x, own_y, right_y, far_ay, far_by, left_y,
    grads, by_x, by_y,
):
    for j in (0, 1):
        left = jnp.concatenate([keep_ref[j], other_ref[j]], axis=0)
        right = jnp.concatenate([keep_ref[2 + j], other_ref[2 + j]], axis=0)
        grads[j] = dot(left, right, 0, 0)

    def assemble(at, carry):
        rows48 = jnp.concatenate([grads[j, pl.ds(pl.multiple_of(24 * at, 8), 24), :] for j in (0, 1)], axis=0)
        y, z = at >> 3, at & 7
        for m in range(4):
            tiles = []
            for h in range(9 * m, 9 * m + 9):
                rb, t = h // 6, h % 6
                tiles.append(rows48[8 * rb : 8 * rb + 8, 128 * t : 128 * (t + 1)])
            tiles.append(vectors_ref[8 * m : 8 * m + 8, :])
            block = jnp.concatenate(tiles, axis=0).astype(BF)
            by_x[m, at] = block[:FIRST]
            by_y[y, 8 * m + z] = block[FIRST:]
        return carry

    lax.fori_loop(0, by_x.shape[1], assemble, 0)
    n = far_ax.shape[0]
    for me, held, own, right, far_a, far_b, left in (
        (x_ref[0], by_x, own_x, right_x, far_ax, far_bx, left_x),
        (y_ref[0], by_y, own_y, right_y, far_ay, far_by, left_y),
    ):
        own[...] = held[me]
        right[...] = held[(me + 1) & 3]
        far_a[...] = held[(me + 2) & 3, :n]
        far_b[...] = held[(me + 2) & 3, n:]
        left[...] = held[(me + 3) & 3]


def plus(*refs):
    total = refs[0].astype(F32)
    for r in refs[1:]:
        total = total + r.astype(F32)
    return total.astype(BF)


def passing_kernel(right_ref, left_ref, far_a_ref, far_b_ref, right_out, left_out):
    n = far_a_ref.shape[0]
    right_out[:n] = plus(right_ref[:n], far_a_ref[...])
    right_out[n:] = right_ref[n:]
    left_out[:n] = left_ref[:n]
    left_out[n:] = plus(left_ref[n:], far_b_ref[...])


def three_kernel(a_ref, b_ref, c_ref, out_ref):
    out_ref[...] = plus(a_ref[...], b_ref[...], c_ref[...])


def second_kernel(me_ref, own_ref, right_ref, left_ref, *refs):
    out_refs, first_ref = refs[:4], refs[4]
    first_ref[...] = plus(own_ref[...], right_ref[...], left_ref[...])
    for k, ref in enumerate(out_refs):
        ref[...] = first_ref[(me_ref[0] + k) & 3]


def third_kernel(me_ref, *refs):
    held = refs[-1]
    x_refs, y_refs, out_refs = refs[:4], refs[4:8], refs[8:-1]
    held[:, :FIRST, :] = plus(*[r[...] for r in x_refs])
    held[:, FIRST:, :] = plus(*[r[...] for r in y_refs])
    for k, ref in enumerate(out_refs):
        ref[...] = held[(me_ref[0] + k) & 7]


def last_kernel(*refs):
    refs[-1][...] = plus(*[r[...] for r in refs[:-1]])


def finish_kernel(me_ref, core_ref, *refs):
    block_refs, (q_ref, k_ref, v_ref, o_ref), vec_refs, held = refs[:8], refs[8:12], refs[12:15], refs[15]
    collect(me_ref[0], block_refs[:4], held.at[0])
    collect(me_ref[0], block_refs[4:], held.at[1])
    blocks = held[...].astype(F32)
    first_core = core_ref[0] == 0
    rows48, vectors = [], []
    for c in (0, 1):
        tiles = [blocks[c, m, 8 * i : 8 * i + 8] for m in range(4) for i in range(9)]
        rows48.append(
            jnp.concatenate([jnp.concatenate(tiles[6 * rb : 6 * rb + 6], axis=1) for rb in range(6)], axis=0)
        )
        vectors.append(jnp.concatenate([blocks[c, m, 72:80] for m in range(4)], axis=0))
    own, other = rows48
    first_pair = jnp.where(first_core, own, other)
    second_pair = jnp.where(first_core, other, own)
    for pair, refs in ((first_pair, (q_ref, k_ref)), (second_pair, (v_ref, o_ref))):
        for i, ref in enumerate(refs):
            ref[...] = jnp.where(first_core, pair[24 * i : 24 * i + 12], pair[24 * i + 12 : 24 * i + 24])
    vectors = vectors[0] + vectors[1]
    for i, ref in enumerate(vec_refs):
        for t in range(6):
            ref[pl.ds(128 * t, 128)] = vectors[6 * i + t]


def shape(dims, kind=BF):
    return jax.ShapeDtypeStruct(dims, kind)


def swap(x, axes):
    return lax.all_to_all(x, axes, split_axis=0, concat_axis=0, tiled=True)


def body(
    cand_item,
    list_place,
    item_table,
    query_vec,
    labels,
    query_weight,
    key_weight,
    value_weight,
    output_weight,
    gain_attn,
    gain_score,
    w_score,
):
    queries, size = cand_item.shape
    stored, slab = item_table.shape
    width = query_vec.shape[1]
    n_dp = lax.axis_size(ROWS)
    n_mp = lax.axis_size("x")
    n_yz = lax.axis_size(("y", "z"))
    slots = n_dp * CAP

    along_x = lax.axis_index("x").astype(jnp.int32).reshape(1)
    along_y = lax.axis_index("y").astype(jnp.int32).reshape(1)
    core = lax.axis_index("c").astype(jnp.int32).reshape(1)

    ids = exchange([cand_item] * 4, "x")
    request, slot = call(
        routing_kernel,
        [shape((n_dp, CAP), jnp.int32), shape((n_mp * queries, size), jnp.int32)],
        (along_x, *ids, list_place.reshape(1, -1)),
        8, 3 * 10**8, 10**6,
        [
            pltpu.VMEM((n_mp, queries, size), jnp.int32),
            pltpu.VMEM((1, list_place.shape[0]), jnp.int32),
            pltpu.SemaphoreType.DMA((2,)),
        ],
        1, (1, 5),
    )
    asked = swap(request, ROWS)
    found = call(
        owner_kernel, shape((n_dp, 48, 128)), (asked, item_table.T), 16, 2 * 10**9, 2 * 10**6,
        [pltpu.VMEM((256, stored), BF), pltpu.SemaphoreType.DMA((2,))], 0, (1,),
    )
    fetched = swap(found, ROWS)
    pieces = call(
        pieces_kernel, [shape((384, 128))] * n_mp, (along_x, slot, fetched), 16, 10**9, 2 * 10**6, (), 1
    )
    rows_in = exchange(pieces, "x")
    acts = shape((4, queries * size, width))
    outs = call(
        step_kernel,
        [shape((queries, 128), F32), shape((queries, width), F32)]
        + [shape((384, 128))] * n_mp
        + [acts] * 2
        + [shape((32, 128), F32)],
        (
            along_x, core, *rows_in, query_vec, labels,
            query_weight, key_weight, value_weight, output_weight,
            gain_attn.reshape(1, -1), gain_score.reshape(1, -1), w_score.reshape(1, -1),
        ),
        32, 4 * 10**9, 10**7,
        [
            pltpu.VMEM((n_mp, 384, 128), BF),
            pltpu.VMEM((HEADS * queries // 2, 128, 256), F32),
            pltpu.VMEM((HEADS * queries // 2, 128, 256), F32),
        ]
        + [pltpu.VMEM((width, width), BF)] * 4
        + [pltpu.SemaphoreType.DMA((4,))],
        2, (8, 9, 10, 11),
    )
    losses, query_grad, diff_base = outs[0], outs[1], outs[2:6]
    keep, send, vectors = outs[6:]

    column_grads = exchange(diff_base, "x")

    other = lax.ppermute(send, "c", [(0, 1), (1, 0)])
    pieces = []
    for count in (FIRST, 80 - FIRST):
        block, half = shape((n_yz, count, 128)), shape((n_yz // 2, count, 128))
        pieces += [block, block, half, half, block]
    rings = call(
        gradients_kernel, pieces, (along_x, along_y, keep, other, vectors), 28, 2 * 10**9, 10**7,
        [
            pltpu.VMEM((2, width, width), F32),
            pltpu.VMEM((4, n_yz, FIRST, 128), BF),
            pltpu.VMEM((4, n_yz, 80 - FIRST, 128), BF),
        ],
        2, awaited=(column_grads[1],),
    )
    far = [
        (shift(far_a, axis, 1), shift(far_b, axis, 3))
        for axis, (_, _, far_a, far_b, _) in (("x", rings[:5]), ("y", rings[5:]))
    ]
    passing = [
        call(passing_kernel, [shape(ring[1].shape)] * 2, (ring[1], ring[4], *passed), 8, 10**6, 10**7)
        for ring, passed in zip((rings[:5], rings[5:]), far)
    ]
    near = [(shift(right, axis, 1), shift(left, axis, 3)) for axis, (right, left) in zip("xy", passing)]

    outgoing = call(
        slots_kernel, shape((n_dp, 48, 128)), (along_x, slot, *column_grads), 16, 10**9, 2 * 10**6,
        [pltpu.VMEM((n_mp, 384, 128), BF)], 1, awaited=[block for pair in passing for block in pair],
    )
    arrived = swap(outgoing, ROWS)
    table_grad = call(
        landing_kernel,
        shape((slab, stored), F32),
        (asked, arrived),
        20, 2 * 10**9, 4 * 10**6,
    ).T

    summed = []
    for axis, me, own, arrive, count in (
        ("y", along_y, rings[0], near[0], FIRST),
        ("x", along_x, rings[5], near[1], 80 - FIRST),
    ):
        dims = (4, n_yz // 4, count, 128)
        blocks = call(
            second_kernel, [shape(dims[1:])] * 4,
            (me, own.reshape(dims), arrive[0].reshape(dims), arrive[1].reshape(dims)), 8, 10**6, 10**7,
            [pltpu.VMEM(dims, BF)], 1,
        )
        summed += exchange(blocks, axis)
    along_z = lax.axis_index("z").astype(jnp.int32).reshape(1)
    n_z = lax.axis_size("z")
    along = call(
        third_kernel, [shape((80, 128))] * n_z, (along_z, *summed), 8, 10**6, 10**6,
        [pltpu.VMEM((n_z, 80, 128), BF)], 1,
    )
    order = sorted(range(1, n_z), key=lambda k: -min(k, n_z - k))
    arrive = [
        lax.ppermute(along[k], "z", [(i, (i + k) % n_z) for i in range(n_z)]) for k in order
    ]
    over_all = call(last_kernel, shape((80, 128)), (along[0], *arrive), 4, 10**6, 10**6, awaited=(arrived,))
    blocks = {(0, 0): over_all}
    for c, k in ((1, 2), (0, 2), (1, 1), (1, 3), (0, 1), (0, 3), (1, 0)):
        pairs = [((a, i), ((a + c) % 2, (i + k) % 4)) for a in range(2) for i in range(4)]
        blocks[c, k] = lax.ppermute(over_all, ("c", "x"), [(4 * p[0] + p[1], 4 * q[0] + q[1]) for p, q in pairs])
    blocks = [blocks[c, k] for c in (0, 1) for k in range(4)]
    rows = width // n_dp
    finished = call(
        finish_kernel,
        [shape((rows, width), F32)] * 4 + [shape((width,), F32)] * 3,
        (along_x, core, *blocks), 4, 10**6, 10**6, [pltpu.VMEM((2, n_mp, 80, 128), BF)], 2,
    )
    return (
        losses[:, 0],
        table_grad,
        query_grad,
        *finished,
    )


def solution(mesh):
    grid = Mesh(mesh.devices.reshape(4, 8, 2, 4), ("y", "z", "c", "x"))
    each = P(("y", "z", "c", "x"), None)
    placed = (each, P(), P(ROWS, "x"), each, each, P(), P(), P(), P(), P(), P(), P())
    return jax.shard_map(
        body,
        mesh=grid,
        in_specs=placed,
        out_specs=(
            P(("y", "z", "c", "x")),
            P(ROWS, "x"),
            each,
            P(ROWS, None),
            P(ROWS, None),
            P(ROWS, None),
            P(ROWS, None),
            P(),
            P(),
            P(),
        ),
        check_vma=False,
    )
```

```python
import jax
import jax.numpy as jnp
from jax import lax
from jax.experimental import pallas as pl
from jax.experimental.pallas import tpu as pltpu
from jax.sharding import Mesh
from jax.sharding import PartitionSpec as P

HEADS = 12
LIST_LEN = 256
EPSILON = 1e-06
SCORE_CAP = 20.0
RANK_CAP = 30.0

ROWS = ("y", "z", "c")
CAP = 32
SLAB = 192
BF = jnp.bfloat16
F32 = jnp.float32
MIB = 1024 * 1024


def dot(a, b, ca=1, cb=0):
    return lax.dot_general(a, b, (((ca,), (cb,)), ((), ())), preferred_element_type=F32)


def iota(shape, dim):
    return lax.broadcasted_iota(jnp.int32, shape, dim)


def whole(n):
    return [pl.BlockSpec(memory_space=pltpu.VMEM)] * n


def stays(x):
    return pltpu.with_memory_space_constraint(x, pltpu.HBM)


def call(kernel, out_shape, args, mib, flops, size, scratch=(), scalars=0, left=(), awaited=()):
    many = isinstance(out_shape, (list, tuple))
    outs = out_shape if many else [out_shape]
    specs = [
        pl.BlockSpec(memory_space=pltpu.VMEM if isinstance(o, jax.ShapeDtypeStruct) else pltpu.HBM) for o in outs
    ]
    in_specs = [pl.BlockSpec(memory_space=pltpu.SMEM)] * scalars + whole(len(args) - scalars)
    args = list(args)
    for i in left:
        in_specs[i] = pl.BlockSpec(memory_space=pltpu.HBM)
        args[i] = stays(args[i])
    in_specs += [pl.BlockSpec(memory_space=pl.ANY)] * len(awaited)

    def run(*refs):
        kernel(*refs[: len(args)], *refs[len(args) + len(awaited) :])

    return pl.pallas_call(
        run,
        out_shape=out_shape,
        in_specs=in_specs,
        out_specs=specs if many else specs[0],
        scratch_shapes=list(scratch),
        compiler_params=pltpu.CompilerParams(vmem_limit_bytes=mib * MIB),
        cost_estimate=pl.CostEstimate(flops=flops, bytes_accessed=size, transcendentals=0),
    )(*args, *awaited)


def shift(x, axis, by):
    return lax.ppermute(x, axis, [(i, (i + by) % 4) for i in range(4)])


def exchange(blocks, axis):
    far = shift(blocks[2], axis, 2)
    return [blocks[0], shift(blocks[1], axis, 1), far, shift(blocks[3], axis, 3)]


def collect(me, refs, held):
    for k, ref in enumerate(refs):
        held[(me - k) & 3] = ref[...]


def low_half(shape):
    return iota(shape, len(shape) - 1) < 64


def swap_halves(t):
    return jnp.concatenate([t[..., 64:], t[..., :64]], axis=-1)


def spread_tail(t):
    t = t.astype(F32)
    other = swap_halves(t)
    low = low_half(t.shape)
    return jnp.concatenate([jnp.where(low, t, other), jnp.where(low, other, t)], axis=1)


def unpack(block):
    b, rows, _ = block.shape
    n = rows // 3
    main = block[:, : 2 * n, :].reshape(b * 2 * n, 128)
    tail = spread_tail(block[:, 2 * n :, :]).astype(BF).reshape(b * 2 * n, 128)
    return jnp.concatenate([main, tail], axis=1)


def pack(full, n):
    tail = full[:, 128:]
    tail = jnp.where(low_half((n, 128)), tail[:n], tail[n:])
    return jnp.concatenate([full[:, :128], tail], axis=0).astype(BF)


def as_column(row):
    return jnp.transpose(jnp.broadcast_to(row, (128, 128)))


def routing_kernel(me_ref, a_ref, b_ref, c_ref, d_ref, place_hbm, request_ref, slot_ref, held, place_ref, sem):
    me = me_ref[0]
    copies = [
        pltpu.make_async_copy(place_hbm, place_ref, sem.at[0]),
        pltpu.make_async_copy(a_ref, held.at[me], sem.at[1]),
    ]
    for c in copies:
        c.start()
    for k, ref in ((1, b_ref), (2, c_ref), (3, d_ref)):
        held[(me - k) & 3] = ref[...]
    for c in copies:
        c.wait()
    place = place_ref[...]
    lists = place.shape[1]
    lane = iota((128, 128), 1)
    owner_of_list = jnp.broadcast_to(place >> 3, (128, lists))
    row = iota((128, lists), 0)
    lookup = jnp.where(owner_of_list == row, 1.0, 0.0)
    lookup = jnp.where(row == 64, jnp.broadcast_to(place & 7, (128, lists)).astype(F32), lookup)
    lookup = lookup.astype(BF)
    before = (iota((128, 128), 1) < iota((128, 128), 0)).astype(F32).astype(BF)
    carry = jnp.zeros((1, 128), F32)
    request = jnp.zeros((128, 128), F32)
    for q in range(slot_ref.shape[0]):
        ids = as_column(held[q // 2, q % 2 : q % 2 + 1, :])
        list_id = ids >> 8
        chosen = jnp.concatenate(
            [(list_id == lane + 128 * t).astype(F32).astype(BF) for t in range(lists // 128)], axis=1
        )
        found = dot(chosen, lookup, 1, 1)
        sub = jnp.sum(jnp.where(lane == 64, found, 0.0), 1, keepdims=True)
        onehot = jnp.where(lane < 64, found, 0.0)
        onehot_low = onehot.astype(BF)
        ahead = dot(before, onehot_low) + carry
        carry = carry + jnp.sum(onehot, 0, keepdims=True)
        rank = jnp.sum(onehot * ahead, 1, keepdims=True)
        owner = jnp.sum(onehot * lane.astype(F32), 1, keepdims=True)
        slot = jnp.broadcast_to(owner * CAP + rank, (128, 128))
        slot_ref[q : q + 1, :] = jnp.transpose(slot)[0:1, :].astype(jnp.int32)
        rank = rank.astype(jnp.int32)
        place_in = (ids & 255).astype(F32)
        entry = jnp.where(rank == lane, sub + 1.0, jnp.where(rank == lane - CAP, place_in, 0.0))
        request = request + dot(onehot_low, entry.astype(BF), 0, 0)
    high = request[:64, :CAP]
    low = request[:64, CAP : 2 * CAP]
    asked = (high - 1.0) * LIST_LEN + low
    request_ref[...] = jnp.where(high > 0.5, asked, -1.0).astype(jnp.int32)


def four_groups(asked):
    part = asked.shape[0] // 4
    return jnp.concatenate([asked[part * k : part * (k + 1)] for k in range(4)], axis=1)


def owner_kernel(asked_ref, table_hbm, out_ref, table_ref, sem):
    copies = [
        pltpu.make_async_copy(table_hbm, table_ref.at[pl.ds(0, SLAB)], sem.at[0]),
        pltpu.make_async_copy(table_hbm.at[pl.ds(128, 64)], table_ref.at[pl.ds(SLAB, 64)], sem.at[1]),
    ]
    for c in copies:
        c.start()
    asked = four_groups(asked_ref[...])
    part = asked.shape[0]
    stored = table_ref.shape[1]
    step = 4
    for r in range(0, part, step):
        column = jnp.concatenate([as_column(asked[r + i : r + i + 1]) for i in range(step)], axis=0)
        lane = iota((128 * step, 128), 1)
        chosen = jnp.concatenate(
            [(column == lane + 128 * t).astype(F32).astype(BF) for t in range(stored // 128)], axis=1
        )
        if r == 0:
            for c in copies:
                c.wait()
        rows = dot(chosen, table_ref[...], 1, 1)
        for i in range(step):
            for k in range(4):
                at = 128 * i + CAP * k
                out_ref[part * k + r + i] = pack(rows[at : at + CAP], CAP // 2)


def pieces_kernel(me_ref, slot_ref, fetched_ref, own_hbm, *refs):
    out_refs, own_ref, sem = refs[:3], refs[3], refs[4]
    fetched = unpack(fetched_ref[...])
    slots = fetched.shape[0]
    copy = pltpu.make_async_copy(own_ref, own_hbm, sem.at[0])
    for k, out_ref in enumerate((own_ref, *out_refs)):
        m = (me_ref[0] + k) & 3
        column = jnp.concatenate([as_column(slot_ref[pl.ds(2 * m + i, 1), :]) for i in (0, 1)], axis=0)
        lane = iota((256, 128), 1)
        chosen = jnp.concatenate(
            [(column == lane + 128 * t).astype(F32).astype(BF) for t in range(slots // 128)], axis=1
        )
        out_ref[...] = pack(dot(chosen, fetched), 128)
        if k == 0:
            copy.start()
    copy.wait()


def slots_kernel(me_ref, slot_ref, a_ref, b_ref, c_ref, d_ref, out_ref, held):
    collect(me_ref[0], (a_ref, b_ref, c_ref, d_ref), held)
    grads = unpack(held[...])
    groups = out_ref.shape[0]
    step = 16 * CAP
    for r in range(0, groups * CAP, step):
        row = iota((step, 128), 0) + r
        chosen = jnp.concatenate(
            [
                (jnp.broadcast_to(slot_ref[q : q + 1, :], (step, 128)) == row).astype(F32).astype(BF)
                for q in range(slot_ref.shape[0])
            ],
            axis=1,
        )
        rows = dot(chosen, grads)
        for i in range(16):
            out_ref[r // CAP + i] = pack(rows[CAP * i : CAP * (i + 1)], CAP // 2)


def landing_kernel(asked_ref, arrived_ref, out_ref):
    arrived = unpack(arrived_ref[...])
    stored = out_ref.shape[1]
    slots = arrived.shape[0]
    asked = four_groups(asked_ref[...])
    part = asked.shape[0]
    columns = [as_column(asked[r : r + 1]) for r in range(part)]
    column = jnp.concatenate(
        [columns[g % part][CAP * (g // part) : CAP * (g // part + 1)] for g in range(4 * part)], axis=0
    )
    step = 512
    lane = iota((slots, 128), 1)
    for r in range(0, stored, step):
        chosen = jnp.concatenate(
            [(column == lane + (r + 128 * t)).astype(F32).astype(BF) for t in range(step // 128)], axis=1
        )
        out_ref[:, r : r + step] = dot(arrived, chosen, 0, 0)[:SLAB]


def lane_mean(x):
    return jnp.sum(x, 1, keepdims=True) * (1.0 / x.shape[1])


def step_kernel(
    me_ref,
    core_ref,
    a_hbm,
    b_ref,
    c_ref,
    d_ref,
    query_ref,
    labels_ref,
    wq_hbm,
    wk_hbm,
    wv_hbm,
    wo_hbm,
    gain_attn_ref,
    gain_score_ref,
    w_score_ref,
    losses_ref,
    query_grad_ref,
    base_0_ref,
    base_1_ref,
    base_2_ref,
    base_3_ref,
    keep_hbm,
    send_hbm,
    vectors_ref,
    held,
    scores_t,
    attend_t,
    wq_ref,
    wk_ref,
    wv_ref,
    wo_ref,
    keep_ref,
    send_ref,
    sem,
):
    me = me_ref[0]
    own = pltpu.make_async_copy(a_hbm, held.at[me], sem.at[4])
    own.start()
    sources = (wq_hbm, wk_hbm, wv_hbm, wo_hbm)
    weights = (wq_ref, wk_ref, wv_ref, wo_ref)
    copies = [pltpu.make_async_copy(a, b, sem.at[i]) for i, (a, b) in enumerate(zip(sources, weights))]
    for c in copies:
        c.start()
    for k, ref in ((1, b_ref), (2, c_ref), (3, d_ref)):
        held[(me - k) & 3] = ref[...]
    own.wait()
    queries, width = query_ref.shape
    size = 128
    head = width // HEADS
    pairs = HEADS // 2
    shrink = head ** (-0.5)
    low = low_half((size, 128))

    parts = []
    for m in range(4):
        main = held[m, :256, :].astype(F32)
        tail = held[m, 256:, :].astype(F32)
        parts += [main, jnp.concatenate([tail[:, :64], tail[:, 64:]], axis=0)]
    rows_in = jnp.concatenate(parts, axis=1)
    vecs = query_ref[...].astype(F32)
    vecs = jnp.concatenate([jnp.broadcast_to(vecs[q : q + 1], (size, width)) for q in range(queries)], axis=0)
    base = rows_in + vecs
    inv_one = 1.0 / jnp.sqrt(lane_mean(base * base) + EPSILON)
    normed_one = base * inv_one
    gain_attn = gain_attn_ref[...]
    first_input = (normed_one * gain_attn).astype(BF)
    for c in copies:
        c.wait()
    q_all = dot(first_input, wq_ref[...]).astype(BF)
    k_all = dot(first_input, wk_ref[...]).astype(BF)
    v_all = dot(first_input, wv_ref[...]).astype(BF)

    def cut(x, q, p):
        return x[size * q : size * (q + 1), 128 * p : 128 * (p + 1)]

    zero = jnp.zeros((size, 128), BF)

    def heads_apart(x):
        return jnp.concatenate([jnp.where(low, x, zero), jnp.where(low, zero, x)], axis=0)

    def heads_joined(x):
        return jnp.where(low, x[:size], x[size:])

    context = []
    for q in range(queries):
        line = []
        for p in range(pairs):
            logits = dot(cut(k_all, q, p), heads_apart(cut(q_all, q, p)), 1, 1)
            th = jnp.tanh(logits * (shrink / SCORE_CAP))
            raised = jnp.exp(SCORE_CAP * th)
            attend = raised * (1.0 / jnp.sum(raised, 0, keepdims=True))
            scores_t[q * pairs + p] = th
            attend_t[q * pairs + p] = attend
            line.append(heads_joined(dot(attend.astype(BF), cut(v_all, q, p), 0, 0)))
        context.append(jnp.concatenate(line, axis=1))
    context = jnp.concatenate(context, axis=0).astype(BF)

    mixed = base + dot(context, wo_ref[...])
    inv_two = 1.0 / jnp.sqrt(lane_mean(mixed * mixed) + EPSILON)
    normed_two = mixed * inv_two
    gain_score = gain_score_ref[...]
    w_score = w_score_ref[...]
    scaled_two = normed_two * gain_score
    capped_scores = jnp.tanh(jnp.sum(scaled_two * w_score, 1, keepdims=True) * (1.0 / RANK_CAP))
    scores = RANK_CAP * capped_scores
    raised = jnp.exp(scores)
    relevance = jnp.exp(labels_ref[...].astype(F32))
    target = relevance / jnp.sum(relevance, 1, keepdims=True)
    diffs = []
    for q in range(queries):
        at = slice(size * q, size * (q + 1))
        total = jnp.sum(raised[at], 0, keepdims=True)
        wanted = as_column(target[q : q + 1])[:, 0:1]
        loss = jnp.log(total) - jnp.sum(wanted * scores[at], 0, keepdims=True)
        losses_ref[q : q + 1, :] = jnp.broadcast_to(loss, (1, 128))
        diffs.append(raised[at] / total - wanted)
    diff_raw = jnp.concatenate(diffs, axis=0) * (1.0 - capped_scores * capped_scores)
    grad_w_score = jnp.sum(scaled_two * diff_raw, 0, keepdims=True)
    diff_scaled = diff_raw * w_score
    grad_gain_score = jnp.sum(normed_two * diff_scaled, 0, keepdims=True)
    diff_normed = diff_scaled * gain_score
    diff_mixed = (diff_normed - normed_two * lane_mean(diff_normed * normed_two)) * inv_two
    diff_low = diff_mixed.astype(BF)
    diff_context = dot(diff_low, wo_ref[...], 1, 1).astype(BF)

    diff_q, diff_k, diff_v = [], [], []
    for q in range(queries):
        line_q, line_k, line_v = [], [], []
        for p in range(pairs):
            th = scores_t[q * pairs + p]
            attend = attend_t[q * pairs + p]
            split = heads_apart(cut(diff_context, q, p))
            diff_attend = dot(cut(v_all, q, p), split, 1, 1)
            line_v.append(dot(attend.astype(BF), split))
            inner = diff_attend - jnp.sum(attend * diff_attend, 0, keepdims=True)
            diff_logits = (attend * inner * (1.0 - th * th) * shrink).astype(BF)
            line_q.append(heads_joined(dot(diff_logits, cut(k_all, q, p), 0, 0)))
            line_k.append(dot(diff_logits, heads_apart(cut(q_all, q, p))))
        diff_q.append(jnp.concatenate(line_q, axis=1))
        diff_k.append(jnp.concatenate(line_k, axis=1))
        diff_v.append(jnp.concatenate(line_v, axis=1))
    diff_q = jnp.concatenate(diff_q, axis=0).astype(BF)
    diff_k = jnp.concatenate(diff_k, axis=0).astype(BF)
    diff_v = jnp.concatenate(diff_v, axis=0).astype(BF)

    first_core = core_ref[0] == 0
    first_pair = (first_input, first_input, diff_q, diff_k)
    second_pair = (first_input, context, diff_v, diff_low)
    for i in range(4):
        keep_ref[i] = jnp.where(first_core, first_pair[i], second_pair[i])
        send_ref[i] = jnp.where(first_core, second_pair[i], first_pair[i])
    sent = [
        pltpu.make_async_copy(send_ref, send_hbm, sem.at[5]),
        pltpu.make_async_copy(keep_ref, keep_hbm, sem.at[6]),
    ]
    for c in sent:
        c.start()

    diff_input = dot(diff_q, wq_ref[...], 1, 1) + dot(diff_k, wk_ref[...], 1, 1) + dot(diff_v, wv_ref[...], 1, 1)
    grad_gain_attn = jnp.sum(normed_one * diff_input, 0, keepdims=True)
    diff_first = diff_input * gain_attn
    diff_base = diff_mixed + (diff_first - normed_one * lane_mean(diff_first * normed_one)) * inv_one
    for q in range(queries):
        query_grad_ref[q : q + 1, :] = jnp.sum(diff_base[size * q : size * (q + 1)], 0, keepdims=True)
    for m in range(4):
        slab = diff_base[:, SLAB * m : SLAB * (m + 1)]
        held[m, :256, :] = slab[:, :128].astype(BF)
        held[m, 256:, :] = jnp.concatenate([slab[:128, 128:], slab[128:, 128:]], axis=1).astype(BF)
    for k, ref in enumerate((base_0_ref, base_1_ref, base_2_ref, base_3_ref)):
        ref[...] = held[(me + k) & 3]
    vectors = [
        v[:, 128 * t : 128 * (t + 1)]
        for v in (grad_gain_attn, grad_gain_score, grad_w_score)
        for t in range(width // 128)
    ]
    vectors_ref[...] = jnp.concatenate(vectors + [jnp.zeros((32 - len(vectors), 128), F32)], axis=0)
    for c in sent:
        c.wait()


FIRST = 48


def gradients_kernel(
    x_ref, y_ref, keep_hbm, other_ref, vectors_ref,
    own_x, right_x, far_ax, far_bx, left_x, own_y, right_y, far_ay, far_by, left_y,
    grads, by_x, by_y, keep_ref, sem,
):
    copy = pltpu.make_async_copy(keep_hbm, keep_ref, sem.at[0])
    copy.start()
    for j in (0, 1):
        grads[j] = dot(other_ref[j], other_ref[2 + j], 0, 0)
    copy.wait()
    for j in (0, 1):
        grads[j] = grads[j] + dot(keep_ref[j], keep_ref[2 + j], 0, 0)

    def assemble(at, carry):
        rows48 = jnp.concatenate([grads[j, pl.ds(pl.multiple_of(24 * at, 8), 24), :] for j in (0, 1)], axis=0)
        y, z = at >> 3, at & 7
        for m in range(4):
            tiles = []
            for h in range(9 * m, 9 * m + 9):
                rb, t = h // 6, h % 6
                tiles.append(rows48[8 * rb : 8 * rb + 8, 128 * t : 128 * (t + 1)])
            tiles.append(vectors_ref[8 * m : 8 * m + 8, :])
            block = jnp.concatenate(tiles, axis=0).astype(BF)
            by_x[m, at] = block[:FIRST]
            by_y[y, 8 * m + z] = block[FIRST:]
        return carry

    lax.fori_loop(0, by_x.shape[1], assemble, 0)
    n = far_ax.shape[0]
    for me, held, own, right, far_a, far_b, left in (
        (x_ref[0], by_x, own_x, right_x, far_ax, far_bx, left_x),
        (y_ref[0], by_y, own_y, right_y, far_ay, far_by, left_y),
    ):
        own[...] = held[me]
        right[...] = held[(me + 1) & 3]
        far_a[...] = held[(me + 2) & 3, :n]
        far_b[...] = held[(me + 2) & 3, n:]
        left[...] = held[(me + 3) & 3]


def plus(*refs):
    total = refs[0].astype(F32)
    for r in refs[1:]:
        total = total + r.astype(F32)
    return total.astype(BF)


def passing_kernel(right_ref, left_ref, far_a_ref, far_b_ref, right_out, left_out):
    n = far_a_ref.shape[0]
    right_out[:n] = plus(right_ref[:n], far_a_ref[...])
    right_out[n:] = right_ref[n:]
    left_out[:n] = left_ref[:n]
    left_out[n:] = plus(left_ref[n:], far_b_ref[...])


def three_kernel(a_ref, b_ref, c_ref, out_ref):
    out_ref[...] = plus(a_ref[...], b_ref[...], c_ref[...])


def second_kernel(me_ref, own_ref, right_ref, left_ref, *refs):
    out_refs, first_ref = refs[:4], refs[4]
    first_ref[...] = plus(own_ref[...], right_ref[...], left_ref[...])
    for k, ref in enumerate(out_refs):
        ref[...] = first_ref[(me_ref[0] + k) & 3]


def third_kernel(*refs):
    x_refs, y_refs, out_ref = refs[:4], refs[4:8], refs[8]
    out_ref[:, :FIRST, :] = plus(*[r[...] for r in x_refs])
    out_ref[:, FIRST:, :] = plus(*[r[...] for r in y_refs])


def last_kernel(parts_ref, out_ref):
    out_ref[...] = plus(*[parts_ref[i] for i in range(parts_ref.shape[0])])


def finish_kernel(me_ref, core_ref, *refs):
    block_refs, (q_ref, k_ref, v_ref, o_ref), vec_refs, held = refs[:4], refs[4:8], refs[8:11], refs[11]
    collect(me_ref[0], block_refs, held)
    blocks = held[...].astype(F32)
    first_core = core_ref[0] == 0
    rows48, vectors = [], []
    for at in (0, 80):
        tiles = [blocks[m, at + 8 * i : at + 8 * i + 8] for m in range(4) for i in range(9)]
        rows48.append(
            jnp.concatenate([jnp.concatenate(tiles[6 * rb : 6 * rb + 6], axis=1) for rb in range(6)], axis=0)
        )
        vectors.append(jnp.concatenate([blocks[m, at + 72 : at + 80] for m in range(4)], axis=0))
    own, other = rows48
    first_pair = jnp.where(first_core, own, other)
    second_pair = jnp.where(first_core, other, own)
    for pair, refs in ((first_pair, (q_ref, k_ref)), (second_pair, (v_ref, o_ref))):
        for i, ref in enumerate(refs):
            ref[...] = jnp.where(first_core, pair[24 * i : 24 * i + 12], pair[24 * i + 12 : 24 * i + 24])
    vectors = vectors[0] + vectors[1]
    for i, ref in enumerate(vec_refs):
        for t in range(6):
            ref[pl.ds(128 * t, 128)] = vectors[6 * i + t]


def shape(dims, kind=BF):
    return jax.ShapeDtypeStruct(dims, kind)


def swap(x, axes):
    return lax.all_to_all(x, axes, split_axis=0, concat_axis=0, tiled=True)


def body(
    cand_item,
    list_place,
    item_table,
    query_vec,
    labels,
    query_weight,
    key_weight,
    value_weight,
    output_weight,
    gain_attn,
    gain_score,
    w_score,
):
    queries, size = cand_item.shape
    stored, slab = item_table.shape
    width = query_vec.shape[1]
    n_dp = lax.axis_size(ROWS)
    n_mp = lax.axis_size("x")
    n_yz = lax.axis_size(("y", "z"))
    slots = n_dp * CAP

    along_x = lax.axis_index("x").astype(jnp.int32).reshape(1)
    along_y = lax.axis_index("y").astype(jnp.int32).reshape(1)
    core = lax.axis_index("c").astype(jnp.int32).reshape(1)

    ids = exchange([cand_item] * 4, "x")
    request, slot = call(
        routing_kernel,
        [shape((n_dp, CAP), jnp.int32), shape((n_mp * queries, size), jnp.int32)],
        (along_x, *ids, list_place.reshape(1, -1)),
        8, 3 * 10**8, 10**6,
        [
            pltpu.VMEM((n_mp, queries, size), jnp.int32),
            pltpu.VMEM((1, list_place.shape[0]), jnp.int32),
            pltpu.SemaphoreType.DMA((2,)),
        ],
        1, (1, 5),
    )
    asked = swap(request, ROWS)
    found = call(
        owner_kernel, shape((n_dp, 48, 128)), (asked, item_table.T), 16, 2 * 10**9, 2 * 10**6,
        [pltpu.VMEM((256, stored), BF), pltpu.SemaphoreType.DMA((2,))], 0, (1,),
    )
    fetched = swap(found, ROWS)
    pieces = call(
        pieces_kernel, [pltpu.HBM((384, 128), BF)] + [shape((384, 128))] * 3, (along_x, slot, fetched),
        16, 10**9, 2 * 10**6, [pltpu.VMEM((384, 128), BF), pltpu.SemaphoreType.DMA((1,))], 1,
    )
    rows_in = exchange(pieces, "x")
    acts = pltpu.HBM((4, queries * size, width), BF)
    outs = call(
        step_kernel,
        [shape((queries, 128), F32), shape((queries, width), F32)]
        + [shape((384, 128))] * n_mp
        + [acts] * 2
        + [shape((32, 128), F32)],
        (
            along_x, core, *rows_in, query_vec, labels,
            query_weight, key_weight, value_weight, output_weight,
            gain_attn.reshape(1, -1), gain_score.reshape(1, -1), w_score.reshape(1, -1),
        ),
        32, 4 * 10**9, 10**7,
        [
            pltpu.VMEM((n_mp, 384, 128), BF),
            pltpu.VMEM((HEADS * queries // 2, 128, 256), F32),
            pltpu.VMEM((HEADS * queries // 2, 128, 256), F32),
        ]
        + [pltpu.VMEM((width, width), BF)] * 4
        + [pltpu.VMEM((4, queries * size, width), BF)] * 2
        + [pltpu.SemaphoreType.DMA((7,))],
        2, (2, 8, 9, 10, 11),
    )
    losses, query_grad, diff_base = outs[0], outs[1], outs[2:6]
    keep, send, vectors = outs[6:]

    column_grads = exchange(diff_base, "x")

    other = lax.ppermute(send, "c", [(0, 1), (1, 0)])
    pieces = []
    for count in (FIRST, 80 - FIRST):
        block, half = shape((n_yz, count, 128)), shape((n_yz // 2, count, 128))
        pieces += [block, block, half, half, block]
    rings = call(
        gradients_kernel, pieces, (along_x, along_y, keep, other, vectors), 28, 2 * 10**9, 10**7,
        [
            pltpu.VMEM((2, width, width), F32),
            pltpu.VMEM((4, n_yz, FIRST, 128), BF),
            pltpu.VMEM((4, n_yz, 80 - FIRST, 128), BF),
            pltpu.VMEM((4, queries * size, width), BF),
            pltpu.SemaphoreType.DMA((1,)),
        ],
        2, (2,), (column_grads[2],),
    )
    far = [
        (shift(far_a, axis, 1), shift(far_b, axis, 3))
        for axis, (_, _, far_a, far_b, _) in (("x", rings[:5]), ("y", rings[5:]))
    ]
    passing = [
        call(passing_kernel, [shape(ring[1].shape)] * 2, (ring[1], ring[4], *passed), 8, 10**6, 10**7)
        for ring, passed in zip((rings[:5], rings[5:]), far)
    ]
    near = [(shift(right, axis, 1), shift(left, axis, 3)) for axis, (right, left) in zip("xy", passing)]

    outgoing = call(
        slots_kernel, shape((n_dp, 48, 128)), (along_x, slot, *column_grads), 16, 10**9, 2 * 10**6,
        [pltpu.VMEM((n_mp, 384, 128), BF)], 1, awaited=[block for pair in far for block in pair],
    )
    arrived = swap(outgoing, ROWS)
    table_grad = call(
        landing_kernel,
        shape((slab, stored), F32),
        (asked, arrived),
        20, 2 * 10**9, 4 * 10**6,
    ).T

    summed = []
    for axis, me, own, arrive, count in (
        ("y", along_y, rings[0], near[0], FIRST),
        ("x", along_x, rings[5], near[1], 80 - FIRST),
    ):
        dims = (4, n_yz // 4, count, 128)
        blocks = call(
            second_kernel, [shape(dims[1:])] * 4,
            (me, own.reshape(dims), arrive[0].reshape(dims), arrive[1].reshape(dims)), 8, 10**6, 10**7,
            [pltpu.VMEM(dims, BF)], 1,
        )
        summed += exchange(blocks, axis)
    along = call(third_kernel, shape((n_yz // 4, 80, 128)), tuple(summed), 8, 10**6, 10**6)
    over_all = call(
        last_kernel, shape((80, 128)), (swap(along, "z"),), 4, 10**6, 10**6, awaited=(arrived,)
    )
    other = lax.ppermute(over_all, "c", [(0, 1), (1, 0)])
    blocks = exchange([jnp.concatenate([over_all, other], axis=0)] * 4, "x")
    rows = width // n_dp
    finished = call(
        finish_kernel,
        [shape((rows, width), F32)] * 4 + [shape((width,), F32)] * 3,
        (along_x, core, *blocks), 4, 10**6, 10**6, [pltpu.VMEM((n_mp, 160, 128), BF)], 2,
    )
    return (
        losses[:, 0],
        table_grad,
        query_grad,
        *finished,
    )


def solution(mesh):
    grid = Mesh(mesh.devices.reshape(4, 8, 2, 4), ("y", "z", "c", "x"))
    each = P(("y", "z", "c", "x"), None)
    placed = (each, P(), P(ROWS, "x"), each, each, P(), P(), P(), P(), P(), P(), P())
    return jax.shard_map(
        body,
        mesh=grid,
        in_specs=placed,
        out_specs=(
            P(("y", "z", "c", "x")),
            P(ROWS, "x"),
            each,
            P(ROWS, None),
            P(ROWS, None),
            P(ROWS, None),
            P(ROWS, None),
            P(),
            P(),
            P(),
        ),
        check_vma=False,
    )
```

```python
import jax
import jax.numpy as jnp
from jax import lax
from jax.experimental import pallas as pl
from jax.experimental.pallas import tpu as pltpu
from jax.sharding import Mesh
from jax.sharding import PartitionSpec as P

HEADS = 12
LIST_LEN = 256
EPSILON = 1e-06
SCORE_CAP = 20.0
RANK_CAP = 30.0

ROWS = ("y", "z", "c")
CAP = 32
SLAB = 192
BF = jnp.bfloat16
F32 = jnp.float32
MIB = 1024 * 1024


def dot(a, b, ca=1, cb=0):
    return lax.dot_general(a, b, (((ca,), (cb,)), ((), ())), preferred_element_type=F32)


def iota(shape, dim):
    return lax.broadcasted_iota(jnp.int32, shape, dim)


def whole(n):
    return [pl.BlockSpec(memory_space=pltpu.VMEM)] * n


def stays(x):
    return pltpu.with_memory_space_constraint(x, pltpu.HBM)


def inside(x):
    return pltpu.with_memory_space_constraint(x, pltpu.VMEM)


def call(kernel, out_shape, args, mib, flops, size, scratch=(), scalars=0, left=(), awaited=()):
    many = isinstance(out_shape, (list, tuple))
    outs = out_shape if many else [out_shape]
    specs = whole(len(outs))
    in_specs = [pl.BlockSpec(memory_space=pltpu.SMEM)] * scalars + whole(len(args) - scalars)
    args = list(args)
    for i in left:
        in_specs[i] = pl.BlockSpec(memory_space=pltpu.HBM)
        args[i] = stays(args[i])
    in_specs += [pl.BlockSpec(memory_space=pl.ANY)] * len(awaited)

    def run(*refs):
        kernel(*refs[: len(args)], *refs[len(args) + len(awaited) :])

    return pl.pallas_call(
        run,
        out_shape=out_shape,
        in_specs=in_specs,
        out_specs=specs if many else specs[0],
        scratch_shapes=list(scratch),
        compiler_params=pltpu.CompilerParams(vmem_limit_bytes=mib * MIB),
        cost_estimate=pl.CostEstimate(flops=flops, bytes_accessed=size, transcendentals=0),
    )(*args, *awaited)


def shift(x, axis, by):
    return lax.ppermute(x, axis, [(i, (i + by) % 4) for i in range(4)])


def exchange(blocks, axis):
    far = shift(blocks[2], axis, 2)
    return [blocks[0], shift(blocks[1], axis, 1), far, shift(blocks[3], axis, 3)]


def collect(me, refs, held):
    for k, ref in enumerate(refs):
        held[(me - k) & 3] = ref[...]


def low_half(shape):
    return iota(shape, len(shape) - 1) < 64


def swap_halves(t):
    return jnp.concatenate([t[..., 64:], t[..., :64]], axis=-1)


def spread_tail(t):
    t = t.astype(F32)
    other = swap_halves(t)
    low = low_half(t.shape)
    return jnp.concatenate([jnp.where(low, t, other), jnp.where(low, other, t)], axis=1)


def unpack(block):
    b, rows, _ = block.shape
    n = rows // 3
    main = block[:, : 2 * n, :].reshape(b * 2 * n, 128)
    tail = spread_tail(block[:, 2 * n :, :]).astype(BF).reshape(b * 2 * n, 128)
    return jnp.concatenate([main, tail], axis=1)


def pack(full, n):
    tail = full[:, 128:]
    tail = jnp.where(low_half((n, 128)), tail[:n], tail[n:])
    return jnp.concatenate([full[:, :128], tail], axis=0).astype(BF)


def as_column(row):
    return jnp.transpose(jnp.broadcast_to(row, (128, 128)))


def lookup_kernel(place_hbm, ids_hbm, lookup_ref, ids_ref, place_ref, sem):
    copies = [
        pltpu.make_async_copy(place_hbm, place_ref, sem.at[0]),
        pltpu.make_async_copy(ids_hbm, ids_ref, sem.at[1]),
    ]
    for c in copies:
        c.start()
    for c in copies:
        c.wait()
    place = place_ref[...]
    lists = place.shape[1]
    owner_of_list = jnp.broadcast_to(place >> 3, (128, lists))
    row = iota((128, lists), 0)
    lookup = jnp.where(owner_of_list == row, 1.0, 0.0)
    lookup = jnp.where(row == 64, jnp.broadcast_to(place & 7, (128, lists)).astype(F32), lookup)
    lookup_ref[...] = lookup.astype(BF)


def routing_kernel(me_ref, a_ref, b_ref, c_ref, d_ref, lookup_ref, request_ref, slot_ref, held):
    collect(me_ref[0], (a_ref, b_ref, c_ref, d_ref), held)
    lookup = lookup_ref[...]
    lists = lookup.shape[1]
    lane = iota((128, 128), 1)
    before = (iota((128, 128), 1) < iota((128, 128), 0)).astype(F32).astype(BF)
    carry = jnp.zeros((1, 128), F32)
    request = jnp.zeros((128, 128), F32)
    for q in range(slot_ref.shape[0]):
        ids = as_column(held[q // 2, q % 2 : q % 2 + 1, :])
        list_id = ids >> 8
        chosen = jnp.concatenate(
            [(list_id == lane + 128 * t).astype(F32).astype(BF) for t in range(lists // 128)], axis=1
        )
        found = dot(chosen, lookup, 1, 1)
        sub = jnp.sum(jnp.where(lane == 64, found, 0.0), 1, keepdims=True)
        onehot = jnp.where(lane < 64, found, 0.0)
        onehot_low = onehot.astype(BF)
        ahead = dot(before, onehot_low) + carry
        carry = carry + jnp.sum(onehot, 0, keepdims=True)
        rank = jnp.sum(onehot * ahead, 1, keepdims=True)
        owner = jnp.sum(onehot * lane.astype(F32), 1, keepdims=True)
        slot = jnp.broadcast_to(owner * CAP + rank, (128, 128))
        slot_ref[q : q + 1, :] = jnp.transpose(slot)[0:1, :].astype(jnp.int32)
        rank = rank.astype(jnp.int32)
        place_in = (ids & 255).astype(F32)
        entry = jnp.where(rank == lane, sub + 1.0, jnp.where(rank == lane - CAP, place_in, 0.0))
        request = request + dot(onehot_low, entry.astype(BF), 0, 0)
    high = request[:64, :CAP]
    low = request[:64, CAP : 2 * CAP]
    asked = (high - 1.0) * LIST_LEN + low
    request_ref[...] = jnp.where(high > 0.5, asked, -1.0).astype(jnp.int32)


def four_groups(asked):
    part = asked.shape[0] // 4
    return jnp.concatenate([asked[part * k : part * (k + 1)] for k in range(4)], axis=1)


def load_kernel(table_hbm, *refs):
    hbm, table_ref, inside_refs, sem = refs[:4], refs[4], refs[5:9], refs[9]
    copies = [
        pltpu.make_async_copy(table_hbm, table_ref.at[pl.ds(0, SLAB)], sem.at[0]),
        pltpu.make_async_copy(table_hbm.at[pl.ds(128, 64)], table_ref.at[pl.ds(SLAB, 64)], sem.at[1]),
    ]
    for i, (a, b) in enumerate(zip(hbm, inside_refs)):
        copies.append(pltpu.make_async_copy(a, b, sem.at[2 + i]))
    for c in copies:
        c.start()
    for c in copies:
        c.wait()


def owner_kernel(asked_ref, table_ref, out_ref):
    asked = four_groups(asked_ref[...])
    part = asked.shape[0]
    stored = table_ref.shape[1]
    step = 4
    for r in range(0, part, step):
        column = jnp.concatenate([as_column(asked[r + i : r + i + 1]) for i in range(step)], axis=0)
        lane = iota((128 * step, 128), 1)
        chosen = jnp.concatenate(
            [(column == lane + 128 * t).astype(F32).astype(BF) for t in range(stored // 128)], axis=1
        )
        rows = dot(chosen, table_ref[...], 1, 1)
        for i in range(step):
            for k in range(4):
                at = 128 * i + CAP * k
                out_ref[part * k + r + i] = pack(rows[at : at + CAP], CAP // 2)


def pieces_kernel(me_ref, slot_ref, fetched_ref, *out_refs):
    fetched = unpack(fetched_ref[...])
    slots = fetched.shape[0]
    for k, out_ref in enumerate(out_refs):
        m = (me_ref[0] + k) & 3
        column = jnp.concatenate([as_column(slot_ref[pl.ds(2 * m + i, 1), :]) for i in (0, 1)], axis=0)
        lane = iota((256, 128), 1)
        chosen = jnp.concatenate(
            [(column == lane + 128 * t).astype(F32).astype(BF) for t in range(slots // 128)], axis=1
        )
        out_ref[...] = pack(dot(chosen, fetched), 128)


def slots_kernel(me_ref, slot_ref, a_ref, b_ref, c_ref, d_ref, out_ref, held):
    collect(me_ref[0], (a_ref, b_ref, c_ref, d_ref), held)
    grads = unpack(held[...])
    groups = out_ref.shape[0]
    step = 16 * CAP
    for r in range(0, groups * CAP, step):
        row = iota((step, 128), 0) + r
        chosen = jnp.concatenate(
            [
                (jnp.broadcast_to(slot_ref[q : q + 1, :], (step, 128)) == row).astype(F32).astype(BF)
                for q in range(slot_ref.shape[0])
            ],
            axis=1,
        )
        rows = dot(chosen, grads)
        for i in range(16):
            out_ref[r // CAP + i] = pack(rows[CAP * i : CAP * (i + 1)], CAP // 2)


def landing_kernel(asked_ref, arrived_ref, out_ref):
    arrived = unpack(arrived_ref[...])
    stored = out_ref.shape[1]
    slots = arrived.shape[0]
    asked = four_groups(asked_ref[...])
    part = asked.shape[0]
    columns = [as_column(asked[r : r + 1]) for r in range(part)]
    column = jnp.concatenate(
        [columns[g % part][CAP * (g // part) : CAP * (g // part + 1)] for g in range(4 * part)], axis=0
    )
    step = 512
    lane = iota((slots, 128), 1)
    for r in range(0, stored, step):
        chosen = jnp.concatenate(
            [(column == lane + (r + 128 * t)).astype(F32).astype(BF) for t in range(step // 128)], axis=1
        )
        out_ref[:, r : r + step] = dot(arrived, chosen, 0, 0)[:SLAB]


def lane_mean(x):
    return jnp.sum(x, 1, keepdims=True) * (1.0 / x.shape[1])


def step_kernel(
    me_ref,
    core_ref,
    a_ref,
    b_ref,
    c_ref,
    d_ref,
    query_ref,
    labels_ref,
    wq_ref,
    wk_ref,
    wv_ref,
    wo_ref,
    gain_attn_ref,
    gain_score_ref,
    w_score_ref,
    losses_ref,
    query_grad_ref,
    base_0_ref,
    base_1_ref,
    base_2_ref,
    base_3_ref,
    keep_ref,
    send_ref,
    vectors_ref,
    held,
    scores_t,
    attend_t,
):
    me = me_ref[0]
    collect(me, (a_ref, b_ref, c_ref, d_ref), held)
    queries, width = query_ref.shape
    size = 128
    head = width // HEADS
    pairs = HEADS // 2
    shrink = head ** (-0.5)
    low = low_half((size, 128))

    parts = []
    for m in range(4):
        main = held[m, :256, :].astype(F32)
        tail = held[m, 256:, :].astype(F32)
        parts += [main, jnp.concatenate([tail[:, :64], tail[:, 64:]], axis=0)]
    rows_in = jnp.concatenate(parts, axis=1)
    vecs = query_ref[...].astype(F32)
    vecs = jnp.concatenate([jnp.broadcast_to(vecs[q : q + 1], (size, width)) for q in range(queries)], axis=0)
    base = rows_in + vecs
    inv_one = 1.0 / jnp.sqrt(lane_mean(base * base) + EPSILON)
    normed_one = base * inv_one
    gain_attn = gain_attn_ref[...]
    first_input = (normed_one * gain_attn).astype(BF)
    q_all = dot(first_input, wq_ref[...]).astype(BF)
    k_all = dot(first_input, wk_ref[...]).astype(BF)
    v_all = dot(first_input, wv_ref[...]).astype(BF)

    def cut(x, q, p):
        return x[size * q : size * (q + 1), 128 * p : 128 * (p + 1)]

    zero = jnp.zeros((size, 128), BF)

    def heads_apart(x):
        return jnp.concatenate([jnp.where(low, x, zero), jnp.where(low, zero, x)], axis=0)

    def heads_joined(x):
        return jnp.where(low, x[:size], x[size:])

    context = []
    for q in range(queries):
        line = []
        for p in range(pairs):
            logits = dot(cut(k_all, q, p), heads_apart(cut(q_all, q, p)), 1, 1)
            th = jnp.tanh(logits * (shrink / SCORE_CAP))
            raised = jnp.exp(SCORE_CAP * th)
            attend = raised * (1.0 / jnp.sum(raised, 0, keepdims=True))
            scores_t[q * pairs + p] = th
            attend_t[q * pairs + p] = attend
            line.append(heads_joined(dot(attend.astype(BF), cut(v_all, q, p), 0, 0)))
        context.append(jnp.concatenate(line, axis=1))
    context = jnp.concatenate(context, axis=0).astype(BF)

    mixed = base + dot(context, wo_ref[...])
    inv_two = 1.0 / jnp.sqrt(lane_mean(mixed * mixed) + EPSILON)
    normed_two = mixed * inv_two
    gain_score = gain_score_ref[...]
    w_score = w_score_ref[...]
    scaled_two = normed_two * gain_score
    capped_scores = jnp.tanh(jnp.sum(scaled_two * w_score, 1, keepdims=True) * (1.0 / RANK_CAP))
    scores = RANK_CAP * capped_scores
    raised = jnp.exp(scores)
    relevance = jnp.exp(labels_ref[...].astype(F32))
    target = relevance / jnp.sum(relevance, 1, keepdims=True)
    diffs = []
    for q in range(queries):
        at = slice(size * q, size * (q + 1))
        total = jnp.sum(raised[at], 0, keepdims=True)
        wanted = as_column(target[q : q + 1])[:, 0:1]
        loss = jnp.log(total) - jnp.sum(wanted * scores[at], 0, keepdims=True)
        losses_ref[q : q + 1, :] = jnp.broadcast_to(loss, (1, 128))
        diffs.append(raised[at] / total - wanted)
    diff_raw = jnp.concatenate(diffs, axis=0) * (1.0 - capped_scores * capped_scores)
    grad_w_score = jnp.sum(scaled_two * diff_raw, 0, keepdims=True)
    diff_scaled = diff_raw * w_score
    grad_gain_score = jnp.sum(normed_two * diff_scaled, 0, keepdims=True)
    diff_normed = diff_scaled * gain_score
    diff_mixed = (diff_normed - normed_two * lane_mean(diff_normed * normed_two)) * inv_two
    diff_low = diff_mixed.astype(BF)
    diff_context = dot(diff_low, wo_ref[...], 1, 1).astype(BF)

    diff_q, diff_k, diff_v = [], [], []
    for q in range(queries):
        line_q, line_k, line_v = [], [], []
        for p in range(pairs):
            th = scores_t[q * pairs + p]
            attend = attend_t[q * pairs + p]
            split = heads_apart(cut(diff_context, q, p))
            diff_attend = dot(cut(v_all, q, p), split, 1, 1)
            line_v.append(dot(attend.astype(BF), split))
            inner = diff_attend - jnp.sum(attend * diff_attend, 0, keepdims=True)
            diff_logits = (attend * inner * (1.0 - th * th) * shrink).astype(BF)
            line_q.append(heads_joined(dot(diff_logits, cut(k_all, q, p), 0, 0)))
            line_k.append(dot(diff_logits, heads_apart(cut(q_all, q, p))))
        diff_q.append(jnp.concatenate(line_q, axis=1))
        diff_k.append(jnp.concatenate(line_k, axis=1))
        diff_v.append(jnp.concatenate(line_v, axis=1))
    diff_q = jnp.concatenate(diff_q, axis=0).astype(BF)
    diff_k = jnp.concatenate(diff_k, axis=0).astype(BF)
    diff_v = jnp.concatenate(diff_v, axis=0).astype(BF)

    first_core = core_ref[0] == 0
    first_pair = (first_input, first_input, diff_q, diff_k)
    second_pair = (first_input, context, diff_v, diff_low)
    for i in range(4):
        keep_ref[i] = jnp.where(first_core, first_pair[i], second_pair[i])
        send_ref[i] = jnp.where(first_core, second_pair[i], first_pair[i])

    diff_input = dot(diff_q, wq_ref[...], 1, 1) + dot(diff_k, wk_ref[...], 1, 1) + dot(diff_v, wv_ref[...], 1, 1)
    grad_gain_attn = jnp.sum(normed_one * diff_input, 0, keepdims=True)
    diff_first = diff_input * gain_attn
    diff_base = diff_mixed + (diff_first - normed_one * lane_mean(diff_first * normed_one)) * inv_one
    for q in range(queries):
        query_grad_ref[q : q + 1, :] = jnp.sum(diff_base[size * q : size * (q + 1)], 0, keepdims=True)
    for m in range(4):
        slab = diff_base[:, SLAB * m : SLAB * (m + 1)]
        held[m, :256, :] = slab[:, :128].astype(BF)
        held[m, 256:, :] = jnp.concatenate([slab[:128, 128:], slab[128:, 128:]], axis=1).astype(BF)
    for k, ref in enumerate((base_0_ref, base_1_ref, base_2_ref, base_3_ref)):
        ref[...] = held[(me + k) & 3]
    vectors = [
        v[:, 128 * t : 128 * (t + 1)]
        for v in (grad_gain_attn, grad_gain_score, grad_w_score)
        for t in range(width // 128)
    ]
    vectors_ref[...] = jnp.concatenate(vectors + [jnp.zeros((32 - len(vectors), 128), F32)], axis=0)


FIRST = 48


def gradients_kernel(
    x_ref, y_ref, keep_ref, other_ref, vectors_ref,
    own_x, right_x, far_ax, far_bx, left_x, own_y, right_y, far_ay, far_by, left_y,
    grads, by_x, by_y,
):
    for j in (0, 1):
        left = jnp.concatenate([keep_ref[j], other_ref[j]], axis=0)
        right = jnp.concatenate([keep_ref[2 + j], other_ref[2 + j]], axis=0)
        grads[j] = dot(left, right, 0, 0)

    def assemble(at, carry):
        rows48 = jnp.concatenate([grads[j, pl.ds(pl.multiple_of(24 * at, 8), 24), :] for j in (0, 1)], axis=0)
        y, z = at >> 3, at & 7
        for m in range(4):
            tiles = []
            for h in range(9 * m, 9 * m + 9):
                rb, t = h // 6, h % 6
                tiles.append(rows48[8 * rb : 8 * rb + 8, 128 * t : 128 * (t + 1)])
            tiles.append(vectors_ref[8 * m : 8 * m + 8, :])
            block = jnp.concatenate(tiles, axis=0).astype(BF)
            by_x[m, at] = block[:FIRST]
            by_y[y, 8 * m + z] = block[FIRST:]
        return carry

    lax.fori_loop(0, by_x.shape[1], assemble, 0)
    n = far_ax.shape[0]
    for me, held, own, right, far_a, far_b, left in (
        (x_ref[0], by_x, own_x, right_x, far_ax, far_bx, left_x),
        (y_ref[0], by_y, own_y, right_y, far_ay, far_by, left_y),
    ):
        own[...] = held[me]
        right[...] = held[(me + 1) & 3]
        far_a[...] = held[(me + 2) & 3, :n]
        far_b[...] = held[(me + 2) & 3, n:]
        left[...] = held[(me + 3) & 3]


def plus(*refs):
    total = refs[0].astype(F32)
    for r in refs[1:]:
        total = total + r.astype(F32)
    return total.astype(BF)


def passing_kernel(right_ref, left_ref, far_a_ref, far_b_ref, right_out, left_out):
    n = far_a_ref.shape[0]
    right_out[:n] = plus(right_ref[:n], far_a_ref[...])
    right_out[n:] = right_ref[n:]
    left_out[:n] = left_ref[:n]
    left_out[n:] = plus(left_ref[n:], far_b_ref[...])


def three_kernel(a_ref, b_ref, c_ref, out_ref):
    out_ref[...] = plus(a_ref[...], b_ref[...], c_ref[...])


def second_kernel(me_ref, own_ref, right_ref, left_ref, *refs):
    out_refs, first_ref = refs[:4], refs[4]
    first_ref[...] = plus(own_ref[...], right_ref[...], left_ref[...])
    for k, ref in enumerate(out_refs):
        ref[...] = first_ref[(me_ref[0] + k) & 3]


def third_kernel(*refs):
    x_refs, y_refs, out_ref = refs[:4], refs[4:8], refs[8]
    out_ref[:, :FIRST, :] = plus(*[r[...] for r in x_refs])
    out_ref[:, FIRST:, :] = plus(*[r[...] for r in y_refs])


def last_kernel(parts_ref, out_ref):
    total = plus(*[parts_ref[i] for i in range(parts_ref.shape[0])])
    for i in range(out_ref.shape[0]):
        out_ref[i] = total


def finish_kernel(core_ref, blocks_ref, q_ref, k_ref, v_ref, o_ref, *vec_refs):
    blocks = blocks_ref[...].astype(F32)
    first_core = core_ref[0] == 0
    rows48, vectors = [], []
    for at in (0, 4):
        tiles = [blocks[at + m, 8 * i : 8 * i + 8] for m in range(4) for i in range(9)]
        rows48.append(
            jnp.concatenate([jnp.concatenate(tiles[6 * rb : 6 * rb + 6], axis=1) for rb in range(6)], axis=0)
        )
        vectors.append(jnp.concatenate([blocks[at + m, 72:] for m in range(4)], axis=0))
    for pair, refs in ((rows48[0], (q_ref, k_ref)), (rows48[1], (v_ref, o_ref))):
        for i, ref in enumerate(refs):
            ref[...] = jnp.where(first_core, pair[24 * i : 24 * i + 12], pair[24 * i + 12 : 24 * i + 24])
    vectors = vectors[0] + vectors[1]
    for i, ref in enumerate(vec_refs):
        for t in range(6):
            ref[pl.ds(128 * t, 128)] = vectors[6 * i + t]


def shape(dims, kind=BF):
    return jax.ShapeDtypeStruct(dims, kind)


def swap(x, axes):
    return lax.all_to_all(x, axes, split_axis=0, concat_axis=0, tiled=True)


def body(
    cand_item,
    list_place,
    item_table,
    query_vec,
    labels,
    query_weight,
    key_weight,
    value_weight,
    output_weight,
    gain_attn,
    gain_score,
    w_score,
):
    queries, size = cand_item.shape
    stored, slab = item_table.shape
    width = query_vec.shape[1]
    n_dp = lax.axis_size(ROWS)
    n_mp = lax.axis_size("x")
    n_yz = lax.axis_size(("y", "z"))
    slots = n_dp * CAP

    along_x = lax.axis_index("x").astype(jnp.int32).reshape(1)
    along_y = lax.axis_index("y").astype(jnp.int32).reshape(1)
    core = lax.axis_index("c").astype(jnp.int32).reshape(1)

    ids = exchange([cand_item] * 4, "x")
    lookup, own_ids = call(
        lookup_kernel,
        [pltpu.VMEM((128, list_place.shape[0]), BF), pltpu.VMEM((queries, size), jnp.int32)],
        (list_place.reshape(1, -1), cand_item), 4, 10**6, 10**6,
        [pltpu.VMEM((1, list_place.shape[0]), jnp.int32), pltpu.SemaphoreType.DMA((2,))], 0, (0, 1),
    )
    request, slot = call(
        routing_kernel,
        [shape((n_dp, CAP), jnp.int32), shape((n_mp * queries, size), jnp.int32)],
        (along_x, own_ids, *ids[1:], lookup),
        8, 3 * 10**8, 10**6, [pltpu.VMEM((n_mp, queries, size), jnp.int32)], 1,
    )
    asked = swap(request, ROWS)
    loaded = call(
        load_kernel,
        [pltpu.VMEM((256, stored), BF)] + [pltpu.VMEM((width, width), BF)] * 4,
        (item_table.T, query_weight, key_weight, value_weight, output_weight), 4, 10**6, 10**7,
        [pltpu.SemaphoreType.DMA((6,))], 0, (0, 1, 2, 3, 4), (request,),
    )
    found = call(
        owner_kernel, shape((n_dp, 48, 128)), (asked, inside(loaded[0])), 16, 2 * 10**9, 2 * 10**6
    )
    fetched = swap(found, ROWS)
    pieces = call(
        pieces_kernel, [pltpu.VMEM((384, 128), BF)] * 4, (along_x, slot, fetched), 16, 10**9, 2 * 10**6, (), 1
    )
    rows_in = exchange(pieces, "x")
    acts = pltpu.VMEM((4, queries * size, width), BF)
    outs = call(
        step_kernel,
        [shape((queries, 128), F32), shape((queries, width), F32)]
        + [shape((384, 128))] * n_mp
        + [acts] * 2
        + [shape((32, 128), F32)],
        (
            along_x, core, inside(rows_in[0]), *rows_in[1:], query_vec, labels,
            *[inside(w) for w in loaded[1:]],
            gain_attn.reshape(1, -1), gain_score.reshape(1, -1), w_score.reshape(1, -1),
        ),
        32, 4 * 10**9, 10**7,
        [
            pltpu.VMEM((n_mp, 384, 128), BF),
            pltpu.VMEM((HEADS * queries // 2, 128, 256), F32),
            pltpu.VMEM((HEADS * queries // 2, 128, 256), F32),
        ],
        2,
    )
    losses, query_grad, diff_base = outs[0], outs[1], outs[2:6]
    keep, send, vectors = outs[6:]

    column_grads = exchange(diff_base, "x")

    other = lax.ppermute(send, "c", [(0, 1), (1, 0)])
    pieces = []
    for count in (FIRST, 80 - FIRST):
        block, half = shape((n_yz, count, 128)), shape((n_yz // 2, count, 128))
        pieces += [block, block, half, half, block]
    rings = call(
        gradients_kernel, pieces, (along_x, along_y, inside(keep), other, vectors), 28, 2 * 10**9, 10**7,
        [
            pltpu.VMEM((2, width, width), F32),
            pltpu.VMEM((4, n_yz, FIRST, 128), BF),
            pltpu.VMEM((4, n_yz, 80 - FIRST, 128), BF),
        ],
        2, (), column_grads[1:],
    )
    far = [
        (shift(far_a, axis, 1), shift(far_b, axis, 3))
        for axis, (_, _, far_a, far_b, _) in (("x", rings[:5]), ("y", rings[5:]))
    ]
    passing = [
        call(passing_kernel, [shape(ring[1].shape)] * 2, (ring[1], ring[4], *passed), 8, 10**6, 10**7)
        for ring, passed in zip((rings[:5], rings[5:]), far)
    ]
    near = [(shift(right, axis, 1), shift(left, axis, 3)) for axis, (right, left) in zip("xy", passing)]

    outgoing = call(
        slots_kernel, shape((n_dp, 48, 128)), (along_x, slot, *column_grads), 16, 10**9, 2 * 10**6,
        [pltpu.VMEM((n_mp, 384, 128), BF)], 1, awaited=[block for pair in far for block in pair],
    )
    arrived = swap(outgoing, ROWS)
    table_grad = call(
        landing_kernel,
        shape((slab, stored), F32),
        (asked, arrived),
        20, 2 * 10**9, 4 * 10**6,
    ).T

    summed = []
    for axis, me, own, arrive, count in (
        ("y", along_y, rings[0], near[0], FIRST),
        ("x", along_x, rings[5], near[1], 80 - FIRST),
    ):
        dims = (4, n_yz // 4, count, 128)
        blocks = call(
            second_kernel, [shape(dims[1:])] * 4,
            (me, own.reshape(dims), arrive[0].reshape(dims), arrive[1].reshape(dims)), 8, 10**6, 10**7,
            [pltpu.VMEM(dims, BF)], 1,
        )
        summed += exchange(blocks, axis)
    along = call(third_kernel, shape((n_yz // 4, 80, 128)), tuple(summed), 8, 10**6, 10**6, awaited=(arrived,))
    copies = call(last_kernel, shape((2 * n_mp, 80, 128)), (swap(along, "z"),), 4, 10**6, 10**6)
    blocks = swap(copies, ("c", "x"))
    rows = width // n_dp
    finished = call(
        finish_kernel,
        [shape((rows, width), F32)] * 4 + [shape((width,), F32)] * 3,
        (core, blocks), 4, 10**6, 10**6, (), 1,
    )
    return (
        losses[:, 0],
        table_grad,
        query_grad,
        *finished,
    )


def solution(mesh):
    grid = Mesh(mesh.devices.reshape(4, 8, 2, 4), ("y", "z", "c", "x"))
    each = P(("y", "z", "c", "x"), None)
    placed = (each, P(), P(ROWS, "x"), each, each, P(), P(), P(), P(), P(), P(), P())
    return jax.shard_map(
        body,
        mesh=grid,
        in_specs=placed,
        out_specs=(
            P(("y", "z", "c", "x")),
            P(ROWS, "x"),
            each,
            P(ROWS, None),
            P(ROWS, None),
            P(ROWS, None),
            P(ROWS, None),
            P(),
            P(),
            P(),
        ),
        check_vma=False,
    )
```

```python
import jax
import jax.numpy as jnp
from jax import lax
from jax.experimental import pallas as pl
from jax.experimental.pallas import tpu as pltpu
from jax.sharding import Mesh
from jax.sharding import PartitionSpec as P

HEADS = 12
LIST_LEN = 256
EPSILON = 1e-06
SCORE_CAP = 20.0
RANK_CAP = 30.0

ROWS = ("y", "z", "c")
CAP = 32
SLAB = 192
BF = jnp.bfloat16
F32 = jnp.float32
MIB = 1024 * 1024


def dot(a, b, ca=1, cb=0):
    return lax.dot_general(a, b, (((ca,), (cb,)), ((), ())), preferred_element_type=F32)


def iota(shape, dim):
    return lax.broadcasted_iota(jnp.int32, shape, dim)


def whole(n):
    return [pl.BlockSpec(memory_space=pltpu.VMEM)] * n


def inside(x):
    return pltpu.with_memory_space_constraint(x, pltpu.VMEM)


def stays(x):
    return pltpu.with_memory_space_constraint(x, pltpu.HBM)


def call(kernel, out_shape, args, mib, flops, size, scratch=(), scalars=0, left=(), awaited=()):
    many = isinstance(out_shape, (list, tuple))
    outs = out_shape if many else [out_shape]
    specs = [
        pl.BlockSpec(memory_space=pltpu.HBM if getattr(o, "memory_space", None) == pltpu.HBM else pltpu.VMEM)
        for o in outs
    ]
    in_specs = [pl.BlockSpec(memory_space=pltpu.SMEM)] * scalars + whole(len(args) - scalars)
    args = list(args)
    for i in left:
        in_specs[i] = pl.BlockSpec(memory_space=pltpu.HBM)
        args[i] = stays(args[i])
    in_specs += [pl.BlockSpec(memory_space=pl.ANY)] * len(awaited)

    def run(*refs):
        kernel(*refs[: len(args)], *refs[len(args) + len(awaited) :])

    return pl.pallas_call(
        run,
        out_shape=out_shape,
        in_specs=in_specs,
        out_specs=specs if many else specs[0],
        scratch_shapes=list(scratch),
        compiler_params=pltpu.CompilerParams(vmem_limit_bytes=mib * MIB),
        cost_estimate=pl.CostEstimate(flops=flops, bytes_accessed=size, transcendentals=0),
    )(*args, *awaited)


def shift(x, axis, by):
    return lax.ppermute(x, axis, [(i, (i + by) % 4) for i in range(4)])


def exchange(blocks, axis):
    far = shift(blocks[2], axis, 2)
    return [blocks[0], shift(blocks[1], axis, 1), far, shift(blocks[3], axis, 3)]


def collect(me, refs, held):
    for k, ref in enumerate(refs):
        held[(me - k) & 3] = ref[...]


def low_half(shape):
    return iota(shape, len(shape) - 1) < 64


def swap_halves(t):
    return jnp.concatenate([t[..., 64:], t[..., :64]], axis=-1)


def spread_tail(t):
    t = t.astype(F32)
    other = swap_halves(t)
    low = low_half(t.shape)
    return jnp.concatenate([jnp.where(low, t, other), jnp.where(low, other, t)], axis=1)


def unpack(block):
    b, rows, _ = block.shape
    n = rows // 3
    main = block[:, : 2 * n, :].reshape(b * 2 * n, 128)
    tail = spread_tail(block[:, 2 * n :, :]).astype(BF).reshape(b * 2 * n, 128)
    return jnp.concatenate([main, tail], axis=1)


def pack(full, n):
    tail = full[:, 128:]
    tail = jnp.where(low_half((n, 128)), tail[:n], tail[n:])
    return jnp.concatenate([full[:, :128], tail], axis=0).astype(BF)


def as_column(row):
    return jnp.transpose(jnp.broadcast_to(row, (128, 128)))


def routing_kernel(me_ref, a_ref, b_ref, c_ref, d_ref, place_hbm, request_ref, slot_ref, held, place_ref, sem):
    me = me_ref[0]
    copies = [
        pltpu.make_async_copy(place_hbm, place_ref, sem.at[0]),
        pltpu.make_async_copy(a_ref, held.at[me], sem.at[1]),
    ]
    for c in copies:
        c.start()
    for k, ref in ((1, b_ref), (2, c_ref), (3, d_ref)):
        held[(me - k) & 3] = ref[...]
    for c in copies:
        c.wait()
    place = place_ref[...]
    lists = place.shape[1]
    lane = iota((128, 128), 1)
    owner_of_list = jnp.broadcast_to(place >> 3, (128, lists))
    row = iota((128, lists), 0)
    lookup = jnp.where(owner_of_list == row, 1.0, 0.0)
    lookup = jnp.where(row == 64, jnp.broadcast_to(place & 7, (128, lists)).astype(F32), lookup)
    lookup = lookup.astype(BF)
    before = (iota((128, 128), 1) < iota((128, 128), 0)).astype(F32).astype(BF)
    carry = jnp.zeros((1, 128), F32)
    request = jnp.zeros((128, 128), F32)
    for q in range(slot_ref.shape[0]):
        ids = as_column(held[q // 2, q % 2 : q % 2 + 1, :])
        list_id = ids >> 8
        chosen = jnp.concatenate(
            [(list_id == lane + 128 * t).astype(F32).astype(BF) for t in range(lists // 128)], axis=1
        )
        found = dot(chosen, lookup, 1, 1)
        sub = jnp.sum(jnp.where(lane == 64, found, 0.0), 1, keepdims=True)
        onehot = jnp.where(lane < 64, found, 0.0)
        onehot_low = onehot.astype(BF)
        ahead = dot(before, onehot_low) + carry
        carry = carry + jnp.sum(onehot, 0, keepdims=True)
        rank = jnp.sum(onehot * ahead, 1, keepdims=True)
        owner = jnp.sum(onehot * lane.astype(F32), 1, keepdims=True)
        slot = jnp.broadcast_to(owner * CAP + rank, (128, 128))
        slot_ref[q : q + 1, :] = jnp.transpose(slot)[0:1, :].astype(jnp.int32)
        rank = rank.astype(jnp.int32)
        place_in = (ids & 255).astype(F32)
        entry = jnp.where(rank == lane, sub + 1.0, jnp.where(rank == lane - CAP, place_in, 0.0))
        request = request + dot(onehot_low, entry.astype(BF), 0, 0)
    high = request[:64, :CAP]
    low = request[:64, CAP : 2 * CAP]
    asked = (high - 1.0) * LIST_LEN + low
    request_ref[...] = jnp.where(high > 0.5, asked, -1.0).astype(jnp.int32)


def four_groups(asked):
    part = asked.shape[0] // 4
    return jnp.concatenate([asked[part * k : part * (k + 1)] for k in range(4)], axis=1)


def load_kernel(table_hbm, table_ref, sem):
    copies = [
        pltpu.make_async_copy(table_hbm, table_ref.at[pl.ds(0, SLAB)], sem.at[0]),
        pltpu.make_async_copy(table_hbm.at[pl.ds(128, 64)], table_ref.at[pl.ds(SLAB, 64)], sem.at[1]),
    ]
    for c in copies:
        c.start()
    for c in copies:
        c.wait()


def owner_kernel(asked_ref, table_ref, out_ref):
    asked = four_groups(asked_ref[...])
    part = asked.shape[0]
    stored = table_ref.shape[1]
    step = 4
    for r in range(0, part, step):
        column = jnp.concatenate([as_column(asked[r + i : r + i + 1]) for i in range(step)], axis=0)
        lane = iota((128 * step, 128), 1)
        chosen = jnp.concatenate(
            [(column == lane + 128 * t).astype(F32).astype(BF) for t in range(stored // 128)], axis=1
        )
        rows = dot(chosen, table_ref[...], 1, 1)
        for i in range(step):
            for k in range(4):
                at = 128 * i + CAP * k
                out_ref[part * k + r + i] = pack(rows[at : at + CAP], CAP // 2)


def pieces_kernel(me_ref, slot_ref, fetched_ref, own_hbm, *refs):
    out_refs, own_ref, sem = refs[:3], refs[3], refs[4]
    fetched = unpack(fetched_ref[...])
    slots = fetched.shape[0]
    copy = pltpu.make_async_copy(own_ref, own_hbm, sem.at[0])
    for k, out_ref in enumerate((own_ref, *out_refs)):
        m = (me_ref[0] + k) & 3
        column = jnp.concatenate([as_column(slot_ref[pl.ds(2 * m + i, 1), :]) for i in (0, 1)], axis=0)
        lane = iota((256, 128), 1)
        chosen = jnp.concatenate(
            [(column == lane + 128 * t).astype(F32).astype(BF) for t in range(slots // 128)], axis=1
        )
        out_ref[...] = pack(dot(chosen, fetched), 128)
        if k == 0:
            copy.start()
    copy.wait()


def slots_kernel(me_ref, slot_ref, a_ref, b_ref, c_ref, d_ref, out_ref, held):
    collect(me_ref[0], (a_ref, b_ref, c_ref, d_ref), held)
    grads = unpack(held[...])
    groups = out_ref.shape[0]
    step = 16 * CAP
    for r in range(0, groups * CAP, step):
        row = iota((step, 128), 0) + r
        chosen = jnp.concatenate(
            [
                (jnp.broadcast_to(slot_ref[q : q + 1, :], (step, 128)) == row).astype(F32).astype(BF)
                for q in range(slot_ref.shape[0])
            ],
            axis=1,
        )
        rows = dot(chosen, grads)
        for i in range(16):
            out_ref[r // CAP + i] = pack(rows[CAP * i : CAP * (i + 1)], CAP // 2)


def landing_kernel(asked_ref, arrived_ref, out_ref):
    arrived = unpack(arrived_ref[...])
    stored = out_ref.shape[1]
    slots = arrived.shape[0]
    asked = four_groups(asked_ref[...])
    part = asked.shape[0]
    columns = [as_column(asked[r : r + 1]) for r in range(part)]
    column = jnp.concatenate(
        [columns[g % part][CAP * (g // part) : CAP * (g // part + 1)] for g in range(4 * part)], axis=0
    )
    step = 512
    lane = iota((slots, 128), 1)
    for r in range(0, stored, step):
        chosen = jnp.concatenate(
            [(column == lane + (r + 128 * t)).astype(F32).astype(BF) for t in range(step // 128)], axis=1
        )
        out_ref[:, r : r + step] = dot(arrived, chosen, 0, 0)[:SLAB]


def lane_mean(x):
    return jnp.sum(x, 1, keepdims=True) * (1.0 / x.shape[1])


def step_kernel(
    me_ref,
    core_ref,
    a_hbm,
    b_ref,
    c_ref,
    d_ref,
    query_ref,
    labels_ref,
    wq_hbm,
    wk_hbm,
    wv_hbm,
    wo_hbm,
    gain_attn_ref,
    gain_score_ref,
    w_score_ref,
    losses_ref,
    query_grad_ref,
    base_0_ref,
    base_1_ref,
    base_2_ref,
    base_3_ref,
    keep_hbm,
    send_hbm,
    vectors_ref,
    held,
    scores_t,
    attend_t,
    wq_ref,
    wk_ref,
    wv_ref,
    wo_ref,
    keep_ref,
    send_ref,
    sem,
):
    me = me_ref[0]
    own = pltpu.make_async_copy(a_hbm, held.at[me], sem.at[4])
    own.start()
    sources = (wq_hbm, wk_hbm, wv_hbm, wo_hbm)
    weights = (wq_ref, wk_ref, wv_ref, wo_ref)
    copies = [pltpu.make_async_copy(a, b, sem.at[i]) for i, (a, b) in enumerate(zip(sources, weights))]
    for c in copies:
        c.start()
    for k, ref in ((1, b_ref), (2, c_ref), (3, d_ref)):
        held[(me - k) & 3] = ref[...]
    own.wait()
    queries, width = query_ref.shape
    size = 128
    head = width // HEADS
    pairs = HEADS // 2
    shrink = head ** (-0.5)
    low = low_half((size, 128))

    parts = []
    for m in range(4):
        main = held[m, :256, :].astype(F32)
        tail = held[m, 256:, :].astype(F32)
        parts += [main, jnp.concatenate([tail[:, :64], tail[:, 64:]], axis=0)]
    rows_in = jnp.concatenate(parts, axis=1)
    vecs = query_ref[...].astype(F32)
    vecs = jnp.concatenate([jnp.broadcast_to(vecs[q : q + 1], (size, width)) for q in range(queries)], axis=0)
    base = rows_in + vecs
    inv_one = 1.0 / jnp.sqrt(lane_mean(base * base) + EPSILON)
    normed_one = base * inv_one
    gain_attn = gain_attn_ref[...]
    first_input = (normed_one * gain_attn).astype(BF)
    copies[0].wait()
    q_all = dot(first_input, wq_ref[...]).astype(BF)
    copies[1].wait()
    k_all = dot(first_input, wk_ref[...]).astype(BF)
    copies[2].wait()
    v_all = dot(first_input, wv_ref[...]).astype(BF)

    def cut(x, q, p):
        return x[size * q : size * (q + 1), 128 * p : 128 * (p + 1)]

    zero = jnp.zeros((size, 128), BF)

    def heads_apart(x):
        return jnp.concatenate([jnp.where(low, x, zero), jnp.where(low, zero, x)], axis=0)

    def heads_joined(x):
        return jnp.where(low, x[:size], x[size:])

    context = []
    for q in range(queries):
        line = []
        for p in range(pairs):
            logits = dot(cut(k_all, q, p), heads_apart(cut(q_all, q, p)), 1, 1)
            th = jnp.tanh(logits * (shrink / SCORE_CAP))
            raised = jnp.exp(SCORE_CAP * th)
            attend = raised * (1.0 / jnp.sum(raised, 0, keepdims=True))
            scores_t[q * pairs + p] = th
            attend_t[q * pairs + p] = attend
            line.append(heads_joined(dot(attend.astype(BF), cut(v_all, q, p), 0, 0)))
        context.append(jnp.concatenate(line, axis=1))
    context = jnp.concatenate(context, axis=0).astype(BF)

    copies[3].wait()
    mixed = base + dot(context, wo_ref[...])
    inv_two = 1.0 / jnp.sqrt(lane_mean(mixed * mixed) + EPSILON)
    normed_two = mixed * inv_two
    gain_score = gain_score_ref[...]
    w_score = w_score_ref[...]
    scaled_two = normed_two * gain_score
    capped_scores = jnp.tanh(jnp.sum(scaled_two * w_score, 1, keepdims=True) * (1.0 / RANK_CAP))
    scores = RANK_CAP * capped_scores
    raised = jnp.exp(scores)
    relevance = jnp.exp(labels_ref[...].astype(F32))
    target = relevance / jnp.sum(relevance, 1, keepdims=True)
    diffs = []
    for q in range(queries):
        at = slice(size * q, size * (q + 1))
        total = jnp.sum(raised[at], 0, keepdims=True)
        wanted = as_column(target[q : q + 1])[:, 0:1]
        loss = jnp.log(total) - jnp.sum(wanted * scores[at], 0, keepdims=True)
        losses_ref[q : q + 1, :] = jnp.broadcast_to(loss, (1, 128))
        diffs.append(raised[at] / total - wanted)
    diff_raw = jnp.concatenate(diffs, axis=0) * (1.0 - capped_scores * capped_scores)
    grad_w_score = jnp.sum(scaled_two * diff_raw, 0, keepdims=True)
    diff_scaled = diff_raw * w_score
    grad_gain_score = jnp.sum(normed_two * diff_scaled, 0, keepdims=True)
    diff_normed = diff_scaled * gain_score
    diff_mixed = (diff_normed - normed_two * lane_mean(diff_normed * normed_two)) * inv_two
    diff_low = diff_mixed.astype(BF)
    diff_context = dot(diff_low, wo_ref[...], 1, 1).astype(BF)

    diff_q, diff_k, diff_v = [], [], []
    for q in range(queries):
        line_q, line_k, line_v = [], [], []
        for p in range(pairs):
            th = scores_t[q * pairs + p]
            attend = attend_t[q * pairs + p]
            split = heads_apart(cut(diff_context, q, p))
            diff_attend = dot(cut(v_all, q, p), split, 1, 1)
            line_v.append(dot(attend.astype(BF), split))
            inner = diff_attend - jnp.sum(attend * diff_attend, 0, keepdims=True)
            diff_logits = (attend * inner * (1.0 - th * th) * shrink).astype(BF)
            line_q.append(heads_joined(dot(diff_logits, cut(k_all, q, p), 0, 0)))
            line_k.append(dot(diff_logits, heads_apart(cut(q_all, q, p))))
        diff_q.append(jnp.concatenate(line_q, axis=1))
        diff_k.append(jnp.concatenate(line_k, axis=1))
        diff_v.append(jnp.concatenate(line_v, axis=1))
    diff_q = jnp.concatenate(diff_q, axis=0).astype(BF)
    diff_k = jnp.concatenate(diff_k, axis=0).astype(BF)
    diff_v = jnp.concatenate(diff_v, axis=0).astype(BF)

    first_core = core_ref[0] == 0
    first_pair = (first_input, first_input, diff_q, diff_k)
    second_pair = (first_input, context, diff_v, diff_low)
    for i in range(4):
        keep_ref[i] = jnp.where(first_core, first_pair[i], second_pair[i])
        send_ref[i] = jnp.where(first_core, second_pair[i], first_pair[i])
    sent = [
        pltpu.make_async_copy(send_ref, send_hbm, sem.at[5]),
        pltpu.make_async_copy(keep_ref, keep_hbm, sem.at[6]),
    ]
    for c in sent:
        c.start()

    diff_input = dot(diff_q, wq_ref[...], 1, 1) + dot(diff_k, wk_ref[...], 1, 1) + dot(diff_v, wv_ref[...], 1, 1)
    grad_gain_attn = jnp.sum(normed_one * diff_input, 0, keepdims=True)
    diff_first = diff_input * gain_attn
    diff_base = diff_mixed + (diff_first - normed_one * lane_mean(diff_first * normed_one)) * inv_one
    for q in range(queries):
        query_grad_ref[q : q + 1, :] = jnp.sum(diff_base[size * q : size * (q + 1)], 0, keepdims=True)
    for m in range(4):
        slab = diff_base[:, SLAB * m : SLAB * (m + 1)]
        held[m, :256, :] = slab[:, :128].astype(BF)
        held[m, 256:, :] = jnp.concatenate([slab[:128, 128:], slab[128:, 128:]], axis=1).astype(BF)
    for k, ref in enumerate((base_0_ref, base_1_ref, base_2_ref, base_3_ref)):
        ref[...] = held[(me + k) & 3]
    vectors = [
        v[:, 128 * t : 128 * (t + 1)]
        for v in (grad_gain_attn, grad_gain_score, grad_w_score)
        for t in range(width // 128)
    ]
    vectors_ref[...] = jnp.concatenate(vectors + [jnp.zeros((32 - len(vectors), 128), F32)], axis=0)
    for c in sent:
        c.wait()


def gradients_kernel(me_ref, keep_hbm, other_ref, vectors_ref, *refs):
    out_refs, (grads, held, keep_ref, sem) = refs[:4], refs[4:]
    copy = pltpu.make_async_copy(keep_hbm, keep_ref, sem.at[0])
    copy.start()
    for j in (0, 1):
        grads[j] = dot(other_ref[j], other_ref[2 + j], 0, 0)
    copy.wait()
    for j in (0, 1):
        grads[j] = grads[j] + dot(keep_ref[j], keep_ref[2 + j], 0, 0)

    def assemble(at, carry):
        rows48 = jnp.concatenate([grads[j, pl.ds(pl.multiple_of(24 * at, 8), 24), :] for j in (0, 1)], axis=0)
        for m in range(4):
            tiles = []
            for h in range(9 * m, 9 * m + 9):
                rb, t = h // 6, h % 6
                tiles.append(rows48[8 * rb : 8 * rb + 8, 128 * t : 128 * (t + 1)])
            tiles.append(vectors_ref[8 * m : 8 * m + 8, :])
            held[m, at] = jnp.concatenate(tiles, axis=0).astype(BF)
        return carry

    lax.fori_loop(0, held.shape[1], assemble, 0)
    for k, ref in enumerate(out_refs):
        ref[...] = held[(me_ref[0] + k) & 3]


def plus(*refs):
    total = refs[0].astype(F32)
    for r in refs[1:]:
        total = total + r.astype(F32)
    return total.astype(BF)


def sum_kernel(*refs):
    refs[-1][...] = plus(*[r[...] for r in refs[:-1]])


def last_kernel(parts_ref, out_ref):
    total = plus(*[parts_ref[i] for i in range(parts_ref.shape[0])])
    for i in range(out_ref.shape[0]):
        out_ref[i] = total


def finish_kernel(core_ref, blocks_ref, q_ref, k_ref, v_ref, o_ref, *vec_refs):
    blocks = blocks_ref[...].astype(F32)
    first_core = core_ref[0] == 0
    rows48, vectors = [], []
    for at in (0, 4):
        tiles = [blocks[at + m, 8 * i : 8 * i + 8] for m in range(4) for i in range(9)]
        rows48.append(
            jnp.concatenate([jnp.concatenate(tiles[6 * rb : 6 * rb + 6], axis=1) for rb in range(6)], axis=0)
        )
        vectors.append(jnp.concatenate([blocks[at + m, 72:] for m in range(4)], axis=0))
    for pair, refs in ((rows48[0], (q_ref, k_ref)), (rows48[1], (v_ref, o_ref))):
        for i, ref in enumerate(refs):
            ref[...] = jnp.where(first_core, pair[24 * i : 24 * i + 12], pair[24 * i + 12 : 24 * i + 24])
    vectors = vectors[0] + vectors[1]
    for i, ref in enumerate(vec_refs):
        for t in range(6):
            ref[pl.ds(128 * t, 128)] = vectors[6 * i + t]


def shape(dims, kind=BF):
    return jax.ShapeDtypeStruct(dims, kind)


def swap(x, axes):
    return lax.all_to_all(x, axes, split_axis=0, concat_axis=0, tiled=True)


def body(
    cand_item,
    list_place,
    item_table,
    query_vec,
    labels,
    query_weight,
    key_weight,
    value_weight,
    output_weight,
    gain_attn,
    gain_score,
    w_score,
):
    queries, size = cand_item.shape
    stored, slab = item_table.shape
    width = query_vec.shape[1]
    n_dp = lax.axis_size(ROWS)
    n_mp = lax.axis_size("x")
    n_yz = lax.axis_size(("y", "z"))
    slots = n_dp * CAP

    along_x = lax.axis_index("x").astype(jnp.int32).reshape(1)
    core = lax.axis_index("c").astype(jnp.int32).reshape(1)

    ids = exchange([cand_item] * 4, "x")
    request, slot = call(
        routing_kernel,
        [shape((n_dp, CAP), jnp.int32), shape((n_mp * queries, size), jnp.int32)],
        (along_x, *ids, list_place.reshape(1, -1)),
        8, 3 * 10**8, 10**6,
        [
            pltpu.VMEM((n_mp, queries, size), jnp.int32),
            pltpu.VMEM((1, list_place.shape[0]), jnp.int32),
            pltpu.SemaphoreType.DMA((2,)),
        ],
        1, (1, 5),
    )
    asked = swap(request, ROWS)
    table = call(
        load_kernel, pltpu.VMEM((256, stored), BF), (item_table.T,), 4, 10**6, 2 * 10**6,
        [pltpu.SemaphoreType.DMA((2,))], 0, (0,), (request,),
    )
    found = call(
        owner_kernel, shape((n_dp, 48, 128)), (asked, inside(table)), 16, 2 * 10**9, 2 * 10**6
    )
    fetched = swap(found, ROWS)
    pieces = call(
        pieces_kernel, [pltpu.HBM((384, 128), BF)] + [shape((384, 128))] * 3, (along_x, slot, fetched),
        16, 10**9, 2 * 10**6, [pltpu.VMEM((384, 128), BF), pltpu.SemaphoreType.DMA((1,))], 1,
    )
    rows_in = exchange(pieces, "x")
    acts = pltpu.HBM((4, queries * size, width), BF)
    outs = call(
        step_kernel,
        [shape((queries, 128), F32), shape((queries, width), F32)]
        + [shape((384, 128))] * n_mp
        + [acts] * 2
        + [shape((32, 128), F32)],
        (
            along_x, core, *rows_in, query_vec, labels,
            query_weight, key_weight, value_weight, output_weight,
            gain_attn.reshape(1, -1), gain_score.reshape(1, -1), w_score.reshape(1, -1),
        ),
        32, 4 * 10**9, 10**7,
        [
            pltpu.VMEM((n_mp, 384, 128), BF),
            pltpu.VMEM((HEADS * queries // 2, 128, 256), F32),
            pltpu.VMEM((HEADS * queries // 2, 128, 256), F32),
        ]
        + [pltpu.VMEM((width, width), BF)] * 4
        + [pltpu.VMEM((4, queries * size, width), BF)] * 2
        + [pltpu.SemaphoreType.DMA((7,))],
        2, (2, 8, 9, 10, 11),
    )
    losses, query_grad, diff_base = outs[0], outs[1], outs[2:6]
    keep, send, vectors = outs[6:]

    column_grads = exchange(diff_base, "x")

    other = lax.ppermute(send, "c", [(0, 1), (1, 0)])
    block = shape((n_yz, 80, 128))
    blocks = call(
        gradients_kernel, [block] * n_mp, (along_x, keep, other, vectors), 32, 2 * 10**9, 10**7,
        [
            pltpu.VMEM((2, width, width), F32),
            pltpu.VMEM((n_mp, n_yz, 80, 128), BF),
            pltpu.VMEM((4, queries * size, width), BF),
            pltpu.SemaphoreType.DMA((1,)),
        ],
        1, (1,), column_grads[1:],
    )
    blocks = exchange(blocks, "x")

    outgoing = call(
        slots_kernel, shape((n_dp, 48, 128)), (along_x, slot, *column_grads), 16, 10**9, 2 * 10**6,
        [pltpu.VMEM((n_mp, 384, 128), BF)], 1, awaited=(blocks[0],),
    )
    arrived = swap(outgoing, ROWS)
    table_grad = call(
        landing_kernel,
        shape((slab, stored), F32),
        (asked, arrived),
        20, 2 * 10**9, 4 * 10**6,
    ).T

    over_x = call(sum_kernel, block, tuple(blocks), 8, 10**6, 10**7, awaited=(arrived,))
    copies = call(last_kernel, shape((2 * n_mp, 80, 128)), (swap(over_x, ("y", "z")),), 4, 10**6, 10**6)
    blocks = swap(copies, ("c", "x"))
    rows = width // n_dp
    finished = call(
        finish_kernel,
        [shape((rows, width), F32)] * 4 + [shape((width,), F32)] * 3,
        (core, blocks), 4, 10**6, 10**6, (), 1,
    )
    return (
        losses[:, 0],
        table_grad,
        query_grad,
        *finished,
    )


def solution(mesh):
    grid = Mesh(mesh.devices.reshape(4, 8, 2, 4), ("y", "z", "c", "x"))
    each = P(("y", "z", "c", "x"), None)
    placed = (each, P(), P(ROWS, "x"), each, each, P(), P(), P(), P(), P(), P(), P())
    return jax.shard_map(
        body,
        mesh=grid,
        in_specs=placed,
        out_specs=(
            P(("y", "z", "c", "x")),
            P(ROWS, "x"),
            each,
            P(ROWS, None),
            P(ROWS, None),
            P(ROWS, None),
            P(ROWS, None),
            P(),
            P(),
            P(),
        ),
        check_vma=False,
    )
```

```python
import jax
import jax.numpy as jnp
from jax import lax
from jax.experimental import pallas as pl
from jax.experimental.pallas import tpu as pltpu
from jax.sharding import Mesh
from jax.sharding import PartitionSpec as P

HEADS = 12
LIST_LEN = 256
EPSILON = 1e-06
SCORE_CAP = 20.0
RANK_CAP = 30.0

ROWS = ("y", "z", "c")
CAP = 32
SLAB = 192
BF = jnp.bfloat16
F32 = jnp.float32
MIB = 1024 * 1024


def dot(a, b, ca=1, cb=0):
    return lax.dot_general(a, b, (((ca,), (cb,)), ((), ())), preferred_element_type=F32)


def iota(shape, dim):
    return lax.broadcasted_iota(jnp.int32, shape, dim)


def whole(n):
    return [pl.BlockSpec(memory_space=pltpu.VMEM)] * n


def inside(x):
    return pltpu.with_memory_space_constraint(x, pltpu.VMEM)


def stays(x):
    return pltpu.with_memory_space_constraint(x, pltpu.HBM)


def call(kernel, out_shape, args, mib, flops, size, scratch=(), scalars=0, left=(), awaited=()):
    many = isinstance(out_shape, (list, tuple))
    outs = out_shape if many else [out_shape]
    specs = [
        pl.BlockSpec(memory_space=pltpu.HBM if getattr(o, "memory_space", None) == pltpu.HBM else pltpu.VMEM)
        for o in outs
    ]
    in_specs = [pl.BlockSpec(memory_space=pltpu.SMEM)] * scalars + whole(len(args) - scalars)
    args = list(args)
    for i in left:
        in_specs[i] = pl.BlockSpec(memory_space=pltpu.HBM)
        args[i] = stays(args[i])
    in_specs += [pl.BlockSpec(memory_space=pl.ANY)] * len(awaited)

    def run(*refs):
        kernel(*refs[: len(args)], *refs[len(args) + len(awaited) :])

    return pl.pallas_call(
        run,
        out_shape=out_shape,
        in_specs=in_specs,
        out_specs=specs if many else specs[0],
        scratch_shapes=list(scratch),
        compiler_params=pltpu.CompilerParams(vmem_limit_bytes=mib * MIB),
        cost_estimate=pl.CostEstimate(flops=flops, bytes_accessed=size, transcendentals=0),
    )(*args, *awaited)


def after(x, awaited):
    return pl.pallas_call(
        lambda *refs: None,
        out_shape=shape(x.shape, x.dtype),
        in_specs=[pl.BlockSpec(memory_space=pl.ANY)] * 2,
        out_specs=pl.BlockSpec(memory_space=pl.ANY),
        input_output_aliases={0: 0},
    )(x, awaited)


def shift(x, axis, by):
    return lax.ppermute(x, axis, [(i, (i + by) % 4) for i in range(4)])


def exchange(blocks, axis):
    far = shift(blocks[2], axis, 2)
    return [blocks[0], shift(blocks[1], axis, 1), far, shift(blocks[3], axis, 3)]


def collect(me, refs, held):
    for k, ref in enumerate(refs):
        held[(me - k) & 3] = ref[...]


def low_half(shape):
    return iota(shape, len(shape) - 1) < 64


def swap_halves(t):
    return jnp.concatenate([t[..., 64:], t[..., :64]], axis=-1)


def spread_tail(t):
    t = t.astype(F32)
    other = swap_halves(t)
    low = low_half(t.shape)
    return jnp.concatenate([jnp.where(low, t, other), jnp.where(low, other, t)], axis=1)


def unpack(block):
    b, rows, _ = block.shape
    n = rows // 3
    main = block[:, : 2 * n, :].reshape(b * 2 * n, 128)
    tail = spread_tail(block[:, 2 * n :, :]).astype(BF).reshape(b * 2 * n, 128)
    return jnp.concatenate([main, tail], axis=1)


def pack(full, n):
    tail = full[:, 128:]
    tail = jnp.where(low_half((n, 128)), tail[:n], tail[n:])
    return jnp.concatenate([full[:, :128], tail], axis=0).astype(BF)


def as_column(row):
    return jnp.transpose(jnp.broadcast_to(row, (128, 128)))


def lookup_kernel(place_hbm, ids_hbm, lookup_ref, ids_ref, place_ref, sem):
    copies = [
        pltpu.make_async_copy(place_hbm, place_ref, sem.at[0]),
        pltpu.make_async_copy(ids_hbm, ids_ref, sem.at[1]),
    ]
    for c in copies:
        c.start()
    for c in copies:
        c.wait()
    place = place_ref[...]
    lists = place.shape[1]
    owner_of_list = jnp.broadcast_to(place >> 3, (128, lists))
    row = iota((128, lists), 0)
    lookup = jnp.where(owner_of_list == row, 1.0, 0.0)
    lookup = jnp.where(row == 64, jnp.broadcast_to(place & 7, (128, lists)).astype(F32), lookup)
    lookup_ref[...] = lookup.astype(BF)


def routing_kernel(me_ref, a_ref, b_ref, c_ref, d_ref, lookup_ref, request_ref, slot_ref, held):
    collect(me_ref[0], (a_ref, b_ref, c_ref, d_ref), held)
    lookup = lookup_ref[...]
    lists = lookup.shape[1]
    lane = iota((128, 128), 1)
    before = (iota((128, 128), 1) < iota((128, 128), 0)).astype(F32).astype(BF)
    carry = jnp.zeros((1, 128), F32)
    request = jnp.zeros((128, 128), F32)
    for q in range(slot_ref.shape[0]):
        ids = as_column(held[q // 2, q % 2 : q % 2 + 1, :])
        list_id = ids >> 8
        chosen = jnp.concatenate(
            [(list_id == lane + 128 * t).astype(F32).astype(BF) for t in range(lists // 128)], axis=1
        )
        found = dot(chosen, lookup, 1, 1)
        sub = jnp.sum(jnp.where(lane == 64, found, 0.0), 1, keepdims=True)
        onehot = jnp.where(lane < 64, found, 0.0)
        onehot_low = onehot.astype(BF)
        ahead = dot(before, onehot_low) + carry
        carry = carry + jnp.sum(onehot, 0, keepdims=True)
        rank = jnp.sum(onehot * ahead, 1, keepdims=True)
        owner = jnp.sum(onehot * lane.astype(F32), 1, keepdims=True)
        slot = jnp.broadcast_to(owner * CAP + rank, (128, 128))
        slot_ref[q : q + 1, :] = jnp.transpose(slot)[0:1, :].astype(jnp.int32)
        rank = rank.astype(jnp.int32)
        place_in = (ids & 255).astype(F32)
        entry = jnp.where(rank == lane, sub + 1.0, jnp.where(rank == lane - CAP, place_in, 0.0))
        request = request + dot(onehot_low, entry.astype(BF), 0, 0)
    high = request[:64, :CAP]
    low = request[:64, CAP : 2 * CAP]
    asked = (high - 1.0) * LIST_LEN + low
    request_ref[...] = jnp.where(high > 0.5, asked, -1.0).astype(jnp.int32)


def four_groups(asked):
    part = asked.shape[0] // 4
    return jnp.concatenate([asked[part * k : part * (k + 1)] for k in range(4)], axis=1)


def load_kernel(table_hbm, table_ref, sem):
    copies = [
        pltpu.make_async_copy(table_hbm, table_ref.at[pl.ds(0, SLAB)], sem.at[0]),
        pltpu.make_async_copy(table_hbm.at[pl.ds(128, 64)], table_ref.at[pl.ds(SLAB, 64)], sem.at[1]),
    ]
    for c in copies:
        c.start()
    for c in copies:
        c.wait()


def owner_kernel(asked_ref, table_ref, out_ref):
    asked = four_groups(asked_ref[...])
    part = asked.shape[0]
    stored = table_ref.shape[1]
    step = 4
    for r in range(0, part, step):
        column = jnp.concatenate([as_column(asked[r + i : r + i + 1]) for i in range(step)], axis=0)
        lane = iota((128 * step, 128), 1)
        chosen = jnp.concatenate(
            [(column == lane + 128 * t).astype(F32).astype(BF) for t in range(stored // 128)], axis=1
        )
        rows = dot(chosen, table_ref[...], 1, 1)
        for i in range(step):
            for k in range(4):
                at = 128 * i + CAP * k
                out_ref[part * k + r + i] = pack(rows[at : at + CAP], CAP // 2)


def pieces_kernel(me_ref, slot_ref, fetched_ref, own_hbm, *refs):
    out_refs, own_ref, sem = refs[:3], refs[3], refs[4]
    fetched = unpack(fetched_ref[...])
    slots = fetched.shape[0]
    copy = pltpu.make_async_copy(own_ref, own_hbm, sem.at[0])
    for k, out_ref in enumerate((own_ref, *out_refs)):
        m = (me_ref[0] + k) & 3
        column = jnp.concatenate([as_column(slot_ref[pl.ds(2 * m + i, 1), :]) for i in (0, 1)], axis=0)
        lane = iota((256, 128), 1)
        chosen = jnp.concatenate(
            [(column == lane + 128 * t).astype(F32).astype(BF) for t in range(slots // 128)], axis=1
        )
        out_ref[...] = pack(dot(chosen, fetched), 128)
        if k == 0:
            copy.start()
    copy.wait()


def slots_kernel(me_ref, slot_ref, a_ref, b_ref, c_ref, d_ref, out_ref, held):
    collect(me_ref[0], (a_ref, b_ref, c_ref, d_ref), held)
    grads = unpack(held[...])
    groups = out_ref.shape[0]
    step = 16 * CAP
    for r in range(0, groups * CAP, step):
        row = iota((step, 128), 0) + r
        chosen = jnp.concatenate(
            [
                (jnp.broadcast_to(slot_ref[q : q + 1, :], (step, 128)) == row).astype(F32).astype(BF)
                for q in range(slot_ref.shape[0])
            ],
            axis=1,
        )
        rows = dot(chosen, grads)
        for i in range(16):
            out_ref[r // CAP + i] = pack(rows[CAP * i : CAP * (i + 1)], CAP // 2)


def landing_kernel(asked_ref, arrived_ref, out_hbm, out_ref, sem):
    arrived = unpack(arrived_ref[...])
    stored = out_ref.shape[1]
    slots = arrived.shape[0]
    asked = four_groups(asked_ref[...])
    part = asked.shape[0]
    columns = [as_column(asked[r : r + 1]) for r in range(part)]
    column = jnp.concatenate(
        [columns[g % part][CAP * (g // part) : CAP * (g // part + 1)] for g in range(4 * part)], axis=0
    )
    step = 512
    copies = []
    lane = iota((slots, 128), 1)
    for r in range(0, stored, step):
        chosen = jnp.concatenate(
            [(column == lane + (r + 128 * t)).astype(F32).astype(BF) for t in range(step // 128)], axis=1
        )
        out_ref[:, r : r + step] = dot(arrived, chosen, 0, 0)[:SLAB]
        at = pl.ds(r, step)
        copies.append(pltpu.make_async_copy(out_ref.at[:, at], out_hbm.at[:, at], sem.at[r // step]))
        copies[-1].start()
    for c in copies:
        c.wait()


def lane_mean(x):
    return jnp.sum(x, 1, keepdims=True) * (1.0 / x.shape[1])


def step_kernel(
    me_ref,
    core_ref,
    a_hbm,
    b_ref,
    c_ref,
    d_ref,
    query_ref,
    labels_ref,
    wq_hbm,
    wk_hbm,
    wv_hbm,
    wo_hbm,
    gain_attn_ref,
    gain_score_ref,
    w_score_ref,
    losses_ref,
    query_grad_ref,
    base_0_ref,
    base_1_ref,
    base_2_ref,
    base_3_ref,
    keep_hbm,
    send_hbm,
    vectors_ref,
    held,
    scores_t,
    attend_t,
    wq_ref,
    wk_ref,
    wv_ref,
    wo_ref,
    keep_ref,
    send_ref,
    sem,
):
    me = me_ref[0]
    own = pltpu.make_async_copy(a_hbm, held.at[me], sem.at[4])
    own.start()
    sources = (wq_hbm, wk_hbm, wv_hbm, wo_hbm)
    weights = (wq_ref, wk_ref, wv_ref, wo_ref)
    copies = [pltpu.make_async_copy(a, b, sem.at[i]) for i, (a, b) in enumerate(zip(sources, weights))]
    for c in copies:
        c.start()
    for k, ref in ((1, b_ref), (2, c_ref), (3, d_ref)):
        held[(me - k) & 3] = ref[...]
    own.wait()
    queries, width = query_ref.shape
    size = 128
    head = width // HEADS
    pairs = HEADS // 2
    shrink = head ** (-0.5)
    low = low_half((size, 128))

    parts = []
    for m in range(4):
        main = held[m, :256, :].astype(F32)
        tail = held[m, 256:, :].astype(F32)
        parts += [main, jnp.concatenate([tail[:, :64], tail[:, 64:]], axis=0)]
    rows_in = jnp.concatenate(parts, axis=1)
    vecs = query_ref[...].astype(F32)
    vecs = jnp.concatenate([jnp.broadcast_to(vecs[q : q + 1], (size, width)) for q in range(queries)], axis=0)
    base = rows_in + vecs
    inv_one = 1.0 / jnp.sqrt(lane_mean(base * base) + EPSILON)
    normed_one = base * inv_one
    gain_attn = gain_attn_ref[...]
    first_input = (normed_one * gain_attn).astype(BF)
    copies[0].wait()
    q_all = dot(first_input, wq_ref[...]).astype(BF)
    copies[1].wait()
    k_all = dot(first_input, wk_ref[...]).astype(BF)
    copies[2].wait()
    v_all = dot(first_input, wv_ref[...]).astype(BF)

    def cut(x, q, p):
        return x[size * q : size * (q + 1), 128 * p : 128 * (p + 1)]

    zero = jnp.zeros((size, 128), BF)

    def heads_apart(x):
        return jnp.concatenate([jnp.where(low, x, zero), jnp.where(low, zero, x)], axis=0)

    def heads_joined(x):
        return jnp.where(low, x[:size], x[size:])

    context = []
    for q in range(queries):
        line = []
        for p in range(pairs):
            logits = dot(cut(k_all, q, p), heads_apart(cut(q_all, q, p)), 1, 1)
            th = jnp.tanh(logits * (shrink / SCORE_CAP))
            raised = jnp.exp(SCORE_CAP * th)
            attend = raised * (1.0 / jnp.sum(raised, 0, keepdims=True))
            scores_t[q * pairs + p] = th
            attend_t[q * pairs + p] = attend
            line.append(heads_joined(dot(attend.astype(BF), cut(v_all, q, p), 0, 0)))
        context.append(jnp.concatenate(line, axis=1))
    context = jnp.concatenate(context, axis=0).astype(BF)

    copies[3].wait()
    mixed = base + dot(context, wo_ref[...])
    inv_two = 1.0 / jnp.sqrt(lane_mean(mixed * mixed) + EPSILON)
    normed_two = mixed * inv_two
    gain_score = gain_score_ref[...]
    w_score = w_score_ref[...]
    scaled_two = normed_two * gain_score
    capped_scores = jnp.tanh(jnp.sum(scaled_two * w_score, 1, keepdims=True) * (1.0 / RANK_CAP))
    scores = RANK_CAP * capped_scores
    raised = jnp.exp(scores)
    relevance = jnp.exp(labels_ref[...].astype(F32))
    target = relevance / jnp.sum(relevance, 1, keepdims=True)
    diffs = []
    for q in range(queries):
        at = slice(size * q, size * (q + 1))
        total = jnp.sum(raised[at], 0, keepdims=True)
        wanted = as_column(target[q : q + 1])[:, 0:1]
        loss = jnp.log(total) - jnp.sum(wanted * scores[at], 0, keepdims=True)
        losses_ref[q : q + 1, :] = jnp.broadcast_to(loss, (1, 128))
        diffs.append(raised[at] / total - wanted)
    diff_raw = jnp.concatenate(diffs, axis=0) * (1.0 - capped_scores * capped_scores)
    grad_w_score = jnp.sum(scaled_two * diff_raw, 0, keepdims=True)
    diff_scaled = diff_raw * w_score
    grad_gain_score = jnp.sum(normed_two * diff_scaled, 0, keepdims=True)
    diff_normed = diff_scaled * gain_score
    diff_mixed = (diff_normed - normed_two * lane_mean(diff_normed * normed_two)) * inv_two
    diff_low = diff_mixed.astype(BF)
    diff_context = dot(diff_low, wo_ref[...], 1, 1).astype(BF)

    diff_q, diff_k, diff_v = [], [], []
    for q in range(queries):
        line_q, line_k, line_v = [], [], []
        for p in range(pairs):
            th = scores_t[q * pairs + p]
            attend = attend_t[q * pairs + p]
            split = heads_apart(cut(diff_context, q, p))
            diff_attend = dot(cut(v_all, q, p), split, 1, 1)
            line_v.append(dot(attend.astype(BF), split))
            inner = diff_attend - jnp.sum(attend * diff_attend, 0, keepdims=True)
            diff_logits = (attend * inner * (1.0 - th * th) * shrink).astype(BF)
            line_q.append(heads_joined(dot(diff_logits, cut(k_all, q, p), 0, 0)))
            line_k.append(dot(diff_logits, heads_apart(cut(q_all, q, p))))
        diff_q.append(jnp.concatenate(line_q, axis=1))
        diff_k.append(jnp.concatenate(line_k, axis=1))
        diff_v.append(jnp.concatenate(line_v, axis=1))
    diff_q = jnp.concatenate(diff_q, axis=0).astype(BF)
    diff_k = jnp.concatenate(diff_k, axis=0).astype(BF)
    diff_v = jnp.concatenate(diff_v, axis=0).astype(BF)

    first_core = core_ref[0] == 0
    first_pair = (first_input, first_input, diff_q, diff_k)
    second_pair = (first_input, context, diff_v, diff_low)
    for i in range(4):
        keep_ref[i] = jnp.where(first_core, first_pair[i], second_pair[i])
        send_ref[i] = jnp.where(first_core, second_pair[i], first_pair[i])
    sent = [
        pltpu.make_async_copy(send_ref, send_hbm, sem.at[5]),
        pltpu.make_async_copy(keep_ref, keep_hbm, sem.at[6]),
    ]
    for c in sent:
        c.start()

    diff_input = dot(diff_q, wq_ref[...], 1, 1) + dot(diff_k, wk_ref[...], 1, 1) + dot(diff_v, wv_ref[...], 1, 1)
    grad_gain_attn = jnp.sum(normed_one * diff_input, 0, keepdims=True)
    diff_first = diff_input * gain_attn
    diff_base = diff_mixed + (diff_first - normed_one * lane_mean(diff_first * normed_one)) * inv_one
    for q in range(queries):
        query_grad_ref[q : q + 1, :] = jnp.sum(diff_base[size * q : size * (q + 1)], 0, keepdims=True)
    for m in range(4):
        slab = diff_base[:, SLAB * m : SLAB * (m + 1)]
        held[m, :256, :] = slab[:, :128].astype(BF)
        held[m, 256:, :] = jnp.concatenate([slab[:128, 128:], slab[128:, 128:]], axis=1).astype(BF)
    for k, ref in enumerate((base_0_ref, base_1_ref, base_2_ref, base_3_ref)):
        ref[...] = held[(me + k) & 3]
    vectors = [
        v[:, 128 * t : 128 * (t + 1)]
        for v in (grad_gain_attn, grad_gain_score, grad_w_score)
        for t in range(width // 128)
    ]
    vectors_ref[...] = jnp.concatenate(vectors + [jnp.zeros((32 - len(vectors), 128), F32)], axis=0)
    for c in sent:
        c.wait()


def gradients_kernel(keep_hbm, other_ref, vectors_ref, out_ref, grads, keep_ref, sem):
    copies = [pltpu.make_async_copy(keep_hbm.at[i], keep_ref.at[i], sem.at[i]) for i in (0, 2, 1, 3)]
    for c in copies:
        c.start()
    for j in (0, 1):
        copies[2 * j].wait()
        copies[2 * j + 1].wait()
        left = jnp.concatenate([keep_ref[j], other_ref[j]], axis=0)
        right = jnp.concatenate([keep_ref[2 + j], other_ref[2 + j]], axis=0)
        grads[j] = dot(left, right, 0, 0)

    def assemble(at, carry):
        rows48 = jnp.concatenate([grads[j, pl.ds(pl.multiple_of(24 * at, 8), 24), :] for j in (0, 1)], axis=0)
        for m in range(4):
            tiles = []
            for h in range(9 * m, 9 * m + 9):
                rb, t = h // 6, h % 6
                tiles.append(rows48[8 * rb : 8 * rb + 8, 128 * t : 128 * (t + 1)])
            tiles.append(vectors_ref[8 * m : 8 * m + 8, :])
            out_ref[m, at] = jnp.concatenate(tiles, axis=0).astype(BF)
        return carry

    lax.fori_loop(0, out_ref.shape[1], assemble, 0)


def plus(*refs):
    total = refs[0].astype(F32)
    for r in refs[1:]:
        total = total + r.astype(F32)
    return total.astype(BF)


def last_kernel(parts_ref, out_ref):
    total = plus(*[parts_ref[i] for i in range(parts_ref.shape[0])])
    for i in range(out_ref.shape[0]):
        out_ref[i] = total


def finish_kernel(core_ref, blocks_ref, q_ref, k_ref, v_ref, o_ref, *vec_refs):
    blocks = blocks_ref[...].astype(F32)
    first_core = core_ref[0] == 0
    rows48, vectors = [], []
    for at in (0, 4):
        tiles = [blocks[at + m, 8 * i : 8 * i + 8] for m in range(4) for i in range(9)]
        rows48.append(
            jnp.concatenate([jnp.concatenate(tiles[6 * rb : 6 * rb + 6], axis=1) for rb in range(6)], axis=0)
        )
        vectors.append(jnp.concatenate([blocks[at + m, 72:] for m in range(4)], axis=0))
    for pair, refs in ((rows48[0], (q_ref, k_ref)), (rows48[1], (v_ref, o_ref))):
        for i, ref in enumerate(refs):
            ref[...] = jnp.where(first_core, pair[24 * i : 24 * i + 12], pair[24 * i + 12 : 24 * i + 24])
    vectors = vectors[0] + vectors[1]
    for i, ref in enumerate(vec_refs):
        for t in range(6):
            ref[pl.ds(128 * t, 128)] = vectors[6 * i + t]


def shape(dims, kind=BF):
    return jax.ShapeDtypeStruct(dims, kind)


def swap(x, axes):
    return lax.all_to_all(x, axes, split_axis=0, concat_axis=0, tiled=True)


def body(
    cand_item,
    list_place,
    item_table,
    query_vec,
    labels,
    query_weight,
    key_weight,
    value_weight,
    output_weight,
    gain_attn,
    gain_score,
    w_score,
):
    queries, size = cand_item.shape
    stored, slab = item_table.shape
    width = query_vec.shape[1]
    n_dp = lax.axis_size(ROWS)
    n_mp = lax.axis_size("x")
    n_yz = lax.axis_size(("y", "z"))
    slots = n_dp * CAP

    along_x = lax.axis_index("x").astype(jnp.int32).reshape(1)
    core = lax.axis_index("c").astype(jnp.int32).reshape(1)

    ids = exchange([cand_item] * 4, "x")
    lookup, own_ids = call(
        lookup_kernel,
        [pltpu.VMEM((128, list_place.shape[0]), BF), pltpu.VMEM((queries, size), jnp.int32)],
        (list_place.reshape(1, -1), cand_item), 4, 10**6, 10**6,
        [pltpu.VMEM((1, list_place.shape[0]), jnp.int32), pltpu.SemaphoreType.DMA((2,))], 0, (0, 1),
    )
    request, slot = call(
        routing_kernel,
        [shape((n_dp, CAP), jnp.int32), shape((n_mp * queries, size), jnp.int32)],
        (along_x, own_ids, *ids[1:], lookup),
        8, 3 * 10**8, 10**6, [pltpu.VMEM((n_mp, queries, size), jnp.int32)], 1,
    )
    asked = swap(request, ROWS)
    table = call(
        load_kernel, pltpu.VMEM((256, stored), BF), (item_table.T,), 4, 10**6, 2 * 10**6,
        [pltpu.SemaphoreType.DMA((2,))], 0, (0,), (request,),
    )
    found = call(
        owner_kernel, shape((n_dp, 48, 128)), (asked, inside(table)), 16, 2 * 10**9, 2 * 10**6
    )
    fetched = swap(found, ROWS)
    pieces = call(
        pieces_kernel, [pltpu.HBM((384, 128), BF)] + [shape((384, 128))] * 3, (along_x, slot, fetched),
        16, 10**9, 2 * 10**6, [pltpu.VMEM((384, 128), BF), pltpu.SemaphoreType.DMA((1,))], 1,
    )
    rows_in = exchange(pieces, "x")
    acts = pltpu.HBM((4, queries * size, width), BF)
    outs = call(
        step_kernel,
        [shape((queries, 128), F32), shape((queries, width), F32)]
        + [shape((384, 128))] * n_mp
        + [acts] * 2
        + [shape((32, 128), F32)],
        (
            along_x, core, *rows_in, query_vec, labels,
            query_weight, key_weight, value_weight, output_weight,
            gain_attn.reshape(1, -1), gain_score.reshape(1, -1), w_score.reshape(1, -1),
        ),
        32, 4 * 10**9, 10**7,
        [
            pltpu.VMEM((n_mp, 384, 128), BF),
            pltpu.VMEM((HEADS * queries // 2, 128, 256), F32),
            pltpu.VMEM((HEADS * queries // 2, 128, 256), F32),
        ]
        + [pltpu.VMEM((width, width), BF)] * 4
        + [pltpu.VMEM((4, queries * size, width), BF)] * 2
        + [pltpu.SemaphoreType.DMA((7,))],
        2, (2, 8, 9, 10, 11),
    )
    losses, query_grad, diff_base = outs[0], outs[1], outs[2:6]
    keep, send, vectors = outs[6:]

    column_grads = exchange(diff_base, "x")

    other = lax.ppermute(send, "c", [(0, 1), (1, 0)])
    blocks = call(
        gradients_kernel, shape((n_mp, n_yz, 80, 128)), (keep, other, vectors), 32, 2 * 10**9, 10**7,
        [
            pltpu.VMEM((2, width, width), F32),
            pltpu.VMEM((4, queries * size, width), BF),
            pltpu.SemaphoreType.DMA((4,)),
        ],
        0, (0,), (column_grads[2],),
    )
    over_x = lax.psum_scatter(blocks.reshape(-1, 128), "x", scatter_dimension=0, tiled=True)

    outgoing = call(
        slots_kernel, shape((n_dp, 48, 128)), (along_x, slot, *column_grads), 16, 10**9, 2 * 10**6,
        [pltpu.VMEM((n_mp, 384, 128), BF)], 1, awaited=(blocks,),
    )
    arrived = swap(outgoing, ROWS)
    landed = call(
        landing_kernel,
        pltpu.HBM((slab, stored), F32),
        (asked, arrived),
        20, 2 * 10**9, 4 * 10**6, [pltpu.VMEM((slab, stored), F32), pltpu.SemaphoreType.DMA((4,))],
    )
    table_grad = landed.T

    parts = swap(after(over_x, arrived).reshape(n_yz, 80, 128), ("y", "z"))
    copies = call(last_kernel, shape((2 * n_mp, 80, 128)), (parts,), 4, 10**6, 10**6, awaited=(landed,))
    blocks = swap(copies, ("c", "x"))
    rows = width // n_dp
    finished = call(
        finish_kernel,
        [shape((rows, width), F32)] * 4 + [shape((width,), F32)] * 3,
        (core, blocks), 4, 10**6, 10**6, (), 1,
    )
    return (
        losses[:, 0],
        table_grad,
        query_grad,
        *finished,
    )


def solution(mesh):
    grid = Mesh(mesh.devices.reshape(4, 8, 2, 4), ("y", "z", "c", "x"))
    each = P(("y", "z", "c", "x"), None)
    placed = (each, P(), P(ROWS, "x"), each, each, P(), P(), P(), P(), P(), P(), P())
    return jax.shard_map(
        body,
        mesh=grid,
        in_specs=placed,
        out_specs=(
            P(("y", "z", "c", "x")),
            P(ROWS, "x"),
            each,
            P(ROWS, None),
            P(ROWS, None),
            P(ROWS, None),
            P(ROWS, None),
            P(),
            P(),
            P(),
        ),
        check_vma=False,
    )
```

```python
import jax
import jax.numpy as jnp
from jax import lax
from jax.experimental import pallas as pl
from jax.experimental.pallas import tpu as pltpu
from jax.sharding import Mesh
from jax.sharding import PartitionSpec as P

HEADS = 12
LIST_LEN = 256
EPSILON = 1e-06
SCORE_CAP = 20.0
RANK_CAP = 30.0

ROWS = ("y", "z", "c")
CAP = 32
SLAB = 192
BF = jnp.bfloat16
F32 = jnp.float32
MIB = 1024 * 1024


def dot(a, b, ca=1, cb=0):
    return lax.dot_general(a, b, (((ca,), (cb,)), ((), ())), preferred_element_type=F32)


def iota(shape, dim):
    return lax.broadcasted_iota(jnp.int32, shape, dim)


def whole(n):
    return [pl.BlockSpec(memory_space=pltpu.VMEM)] * n


def inside(x):
    return pltpu.with_memory_space_constraint(x, pltpu.VMEM)


def stays(x):
    return pltpu.with_memory_space_constraint(x, pltpu.HBM)


def call(kernel, out_shape, args, mib, flops, size, scratch=(), scalars=0, left=(), awaited=()):
    many = isinstance(out_shape, (list, tuple))
    outs = out_shape if many else [out_shape]
    specs = [
        pl.BlockSpec(memory_space=pltpu.HBM if getattr(o, "memory_space", None) == pltpu.HBM else pltpu.VMEM)
        for o in outs
    ]
    in_specs = [pl.BlockSpec(memory_space=pltpu.SMEM)] * scalars + whole(len(args) - scalars)
    args = list(args)
    for i in left:
        in_specs[i] = pl.BlockSpec(memory_space=pltpu.HBM)
        args[i] = stays(args[i])
    in_specs += [pl.BlockSpec(memory_space=pl.ANY)] * len(awaited)

    def run(*refs):
        kernel(*refs[: len(args)], *refs[len(args) + len(awaited) :])

    return pl.pallas_call(
        run,
        out_shape=out_shape,
        in_specs=in_specs,
        out_specs=specs if many else specs[0],
        scratch_shapes=list(scratch),
        compiler_params=pltpu.CompilerParams(vmem_limit_bytes=mib * MIB),
        cost_estimate=pl.CostEstimate(flops=flops, bytes_accessed=size, transcendentals=0),
    )(*args, *awaited)


def after(x, awaited):
    return pl.pallas_call(
        lambda *refs: None,
        out_shape=shape(x.shape, x.dtype),
        in_specs=[pl.BlockSpec(memory_space=pl.ANY)] * 2,
        out_specs=pl.BlockSpec(memory_space=pl.ANY),
        input_output_aliases={0: 0},
    )(x, awaited)


def shift(x, axis, by):
    return lax.ppermute(x, axis, [(i, (i + by) % 4) for i in range(4)])


def exchange(blocks, axis):
    far = shift(blocks[2], axis, 2)
    return [blocks[0], shift(blocks[1], axis, 1), far, shift(blocks[3], axis, 3)]


def collect(me, refs, held):
    for k, ref in enumerate(refs):
        held[(me - k) & 3] = ref[...]


def low_half(shape):
    return iota(shape, len(shape) - 1) < 64


def swap_halves(t):
    return jnp.concatenate([t[..., 64:], t[..., :64]], axis=-1)


def spread_tail(t):
    t = t.astype(F32)
    other = swap_halves(t)
    low = low_half(t.shape)
    return jnp.concatenate([jnp.where(low, t, other), jnp.where(low, other, t)], axis=1)


def unpack(block):
    b, rows, _ = block.shape
    n = rows // 3
    main = block[:, : 2 * n, :].reshape(b * 2 * n, 128)
    tail = spread_tail(block[:, 2 * n :, :]).astype(BF).reshape(b * 2 * n, 128)
    return jnp.concatenate([main, tail], axis=1)


def pack(full, n):
    tail = full[:, 128:]
    tail = jnp.where(low_half((n, 128)), tail[:n], tail[n:])
    return jnp.concatenate([full[:, :128], tail], axis=0).astype(BF)


def as_column(row):
    return jnp.transpose(jnp.broadcast_to(row, (128, 128)))


def lookup_kernel(place_hbm, ids_hbm, lookup_ref, ids_ref, place_ref, sem):
    copies = [
        pltpu.make_async_copy(place_hbm, place_ref, sem.at[0]),
        pltpu.make_async_copy(ids_hbm, ids_ref, sem.at[1]),
    ]
    for c in copies:
        c.start()
    for c in copies:
        c.wait()
    place = place_ref[...]
    lists = place.shape[1]
    owner_of_list = jnp.broadcast_to(place >> 3, (128, lists))
    row = iota((128, lists), 0)
    lookup = jnp.where(owner_of_list == row, 1.0, 0.0)
    lookup = jnp.where(row == 64, jnp.broadcast_to(place & 7, (128, lists)).astype(F32), lookup)
    lookup_ref[...] = lookup.astype(BF)


def routing_kernel(me_ref, a_ref, b_ref, c_ref, d_ref, lookup_ref, request_ref, slot_ref, held):
    collect(me_ref[0], (a_ref, b_ref, c_ref, d_ref), held)
    lookup = lookup_ref[...]
    lists = lookup.shape[1]
    lane = iota((128, 128), 1)
    before = (iota((128, 128), 1) < iota((128, 128), 0)).astype(F32).astype(BF)
    carry = jnp.zeros((1, 128), F32)
    request = jnp.zeros((128, 128), F32)
    for q in range(slot_ref.shape[0]):
        ids = as_column(held[q // 2, q % 2 : q % 2 + 1, :])
        list_id = ids >> 8
        chosen = jnp.concatenate(
            [(list_id == lane + 128 * t).astype(F32).astype(BF) for t in range(lists // 128)], axis=1
        )
        found = dot(chosen, lookup, 1, 1)
        sub = jnp.sum(jnp.where(lane == 64, found, 0.0), 1, keepdims=True)
        onehot = jnp.where(lane < 64, found, 0.0)
        onehot_low = onehot.astype(BF)
        ahead = dot(before, onehot_low) + carry
        carry = carry + jnp.sum(onehot, 0, keepdims=True)
        rank = jnp.sum(onehot * ahead, 1, keepdims=True)
        owner = jnp.sum(onehot * lane.astype(F32), 1, keepdims=True)
        slot = jnp.broadcast_to(owner * CAP + rank, (128, 128))
        slot_ref[q : q + 1, :] = jnp.transpose(slot)[0:1, :].astype(jnp.int32)
        rank = rank.astype(jnp.int32)
        place_in = (ids & 255).astype(F32)
        entry = jnp.where(rank == lane, sub + 1.0, jnp.where(rank == lane - CAP, place_in, 0.0))
        request = request + dot(onehot_low, entry.astype(BF), 0, 0)
    high = request[:64, :CAP]
    low = request[:64, CAP : 2 * CAP]
    asked = (high - 1.0) * LIST_LEN + low
    request_ref[...] = jnp.where(high > 0.5, asked, -1.0).astype(jnp.int32)


def four_groups(asked):
    part = asked.shape[0] // 4
    return jnp.concatenate([asked[part * k : part * (k + 1)] for k in range(4)], axis=1)


def load_kernel(table_hbm, table_ref, sem):
    copies = [
        pltpu.make_async_copy(table_hbm, table_ref.at[pl.ds(0, SLAB)], sem.at[0]),
        pltpu.make_async_copy(table_hbm.at[pl.ds(128, 64)], table_ref.at[pl.ds(SLAB, 64)], sem.at[1]),
    ]
    for c in copies:
        c.start()
    for c in copies:
        c.wait()


def owner_kernel(asked_ref, table_ref, out_ref):
    asked = four_groups(asked_ref[...])
    part = asked.shape[0]
    stored = table_ref.shape[1]
    step = 4
    for r in range(0, part, step):
        column = jnp.concatenate([as_column(asked[r + i : r + i + 1]) for i in range(step)], axis=0)
        lane = iota((128 * step, 128), 1)
        chosen = jnp.concatenate(
            [(column == lane + 128 * t).astype(F32).astype(BF) for t in range(stored // 128)], axis=1
        )
        rows = dot(chosen, table_ref[...], 1, 1)
        for i in range(step):
            for k in range(4):
                at = 128 * i + CAP * k
                out_ref[part * k + r + i] = pack(rows[at : at + CAP], CAP // 2)


def pieces_kernel(me_ref, slot_ref, fetched_ref, own_hbm, *refs):
    out_refs, own_ref, sem = refs[:3], refs[3], refs[4]
    fetched = unpack(fetched_ref[...])
    slots = fetched.shape[0]
    copy = pltpu.make_async_copy(own_ref, own_hbm, sem.at[0])
    for k, out_ref in enumerate((own_ref, *out_refs)):
        m = (me_ref[0] + k) & 3
        column = jnp.concatenate([as_column(slot_ref[pl.ds(2 * m + i, 1), :]) for i in (0, 1)], axis=0)
        lane = iota((256, 128), 1)
        chosen = jnp.concatenate(
            [(column == lane + 128 * t).astype(F32).astype(BF) for t in range(slots // 128)], axis=1
        )
        out_ref[...] = pack(dot(chosen, fetched), 128)
        if k == 0:
            copy.start()
    copy.wait()


def slots_kernel(me_ref, slot_ref, a_ref, b_ref, c_ref, d_ref, out_ref, held):
    collect(me_ref[0], (a_ref, b_ref, c_ref, d_ref), held)
    grads = unpack(held[...])
    groups = out_ref.shape[0]
    step = 16 * CAP
    for r in range(0, groups * CAP, step):
        row = iota((step, 128), 0) + r
        chosen = jnp.concatenate(
            [
                (jnp.broadcast_to(slot_ref[q : q + 1, :], (step, 128)) == row).astype(F32).astype(BF)
                for q in range(slot_ref.shape[0])
            ],
            axis=1,
        )
        rows = dot(chosen, grads)
        for i in range(16):
            out_ref[r // CAP + i] = pack(rows[CAP * i : CAP * (i + 1)], CAP // 2)


def landing_kernel(asked_ref, arrived_ref, out_hbm, token_ref, out_ref, sem):
    token_ref[...] = jnp.zeros_like(token_ref)
    arrived = unpack(arrived_ref[...])
    stored = out_ref.shape[1]
    slots = arrived.shape[0]
    asked = four_groups(asked_ref[...])
    part = asked.shape[0]
    columns = [as_column(asked[r : r + 1]) for r in range(part)]
    column = jnp.concatenate(
        [columns[g % part][CAP * (g // part) : CAP * (g // part + 1)] for g in range(4 * part)], axis=0
    )
    step = 512
    copies = []
    lane = iota((slots, 128), 1)
    for r in range(0, stored, step):
        chosen = jnp.concatenate(
            [(column == lane + (r + 128 * t)).astype(F32).astype(BF) for t in range(step // 128)], axis=1
        )
        out_ref[:, r : r + step] = dot(arrived, chosen, 0, 0)[:SLAB]
        at = pl.ds(r, step)
        copies.append(pltpu.make_async_copy(out_ref.at[:, at], out_hbm.at[:, at], sem.at[r // step]))
        copies[-1].start()
    for c in copies:
        c.wait()


def lane_mean(x):
    return jnp.sum(x, 1, keepdims=True) * (1.0 / x.shape[1])


def step_kernel(
    me_ref,
    core_ref,
    a_hbm,
    b_ref,
    c_ref,
    d_ref,
    query_ref,
    labels_ref,
    wq_hbm,
    wk_hbm,
    wv_hbm,
    wo_hbm,
    gain_attn_ref,
    gain_score_ref,
    w_score_ref,
    losses_ref,
    query_grad_ref,
    base_0_ref,
    base_1_ref,
    base_2_ref,
    base_3_ref,
    keep_hbm,
    send_hbm,
    vectors_ref,
    held,
    scores_t,
    attend_t,
    wq_ref,
    wk_ref,
    wv_ref,
    wo_ref,
    keep_ref,
    send_ref,
    sem,
):
    me = me_ref[0]
    own = pltpu.make_async_copy(a_hbm, held.at[me], sem.at[4])
    own.start()
    sources = (wq_hbm, wk_hbm, wv_hbm, wo_hbm)
    weights = (wq_ref, wk_ref, wv_ref, wo_ref)
    copies = [pltpu.make_async_copy(a, b, sem.at[i]) for i, (a, b) in enumerate(zip(sources, weights))]
    for c in copies:
        c.start()
    for k, ref in ((1, b_ref), (2, c_ref), (3, d_ref)):
        held[(me - k) & 3] = ref[...]
    own.wait()
    queries, width = query_ref.shape
    size = 128
    head = width // HEADS
    pairs = HEADS // 2
    shrink = head ** (-0.5)
    low = low_half((size, 128))

    parts = []
    for m in range(4):
        main = held[m, :256, :].astype(F32)
        tail = held[m, 256:, :].astype(F32)
        parts += [main, jnp.concatenate([tail[:, :64], tail[:, 64:]], axis=0)]
    rows_in = jnp.concatenate(parts, axis=1)
    vecs = query_ref[...].astype(F32)
    vecs = jnp.concatenate([jnp.broadcast_to(vecs[q : q + 1], (size, width)) for q in range(queries)], axis=0)
    base = rows_in + vecs
    inv_one = 1.0 / jnp.sqrt(lane_mean(base * base) + EPSILON)
    normed_one = base * inv_one
    gain_attn = gain_attn_ref[...]
    first_input = (normed_one * gain_attn).astype(BF)
    copies[0].wait()
    q_all = dot(first_input, wq_ref[...]).astype(BF)
    copies[1].wait()
    k_all = dot(first_input, wk_ref[...]).astype(BF)
    copies[2].wait()
    v_all = dot(first_input, wv_ref[...]).astype(BF)

    def cut(x, q, p):
        return x[size * q : size * (q + 1), 128 * p : 128 * (p + 1)]

    zero = jnp.zeros((size, 128), BF)

    def heads_apart(x):
        return jnp.concatenate([jnp.where(low, x, zero), jnp.where(low, zero, x)], axis=0)

    def heads_joined(x):
        return jnp.where(low, x[:size], x[size:])

    context = []
    for q in range(queries):
        line = []
        for p in range(pairs):
            logits = dot(cut(k_all, q, p), heads_apart(cut(q_all, q, p)), 1, 1)
            th = jnp.tanh(logits * (shrink / SCORE_CAP))
            raised = jnp.exp(SCORE_CAP * th)
            attend = raised * (1.0 / jnp.sum(raised, 0, keepdims=True))
            scores_t[q * pairs + p] = th
            attend_t[q * pairs + p] = attend
            line.append(heads_joined(dot(attend.astype(BF), cut(v_all, q, p), 0, 0)))
        context.append(jnp.concatenate(line, axis=1))
    context = jnp.concatenate(context, axis=0).astype(BF)

    copies[3].wait()
    mixed = base + dot(context, wo_ref[...])
    inv_two = 1.0 / jnp.sqrt(lane_mean(mixed * mixed) + EPSILON)
    normed_two = mixed * inv_two
    gain_score = gain_score_ref[...]
    w_score = w_score_ref[...]
    scaled_two = normed_two * gain_score
    capped_scores = jnp.tanh(jnp.sum(scaled_two * w_score, 1, keepdims=True) * (1.0 / RANK_CAP))
    scores = RANK_CAP * capped_scores
    raised = jnp.exp(scores)
    relevance = jnp.exp(labels_ref[...].astype(F32))
    target = relevance / jnp.sum(relevance, 1, keepdims=True)
    diffs = []
    for q in range(queries):
        at = slice(size * q, size * (q + 1))
        total = jnp.sum(raised[at], 0, keepdims=True)
        wanted = as_column(target[q : q + 1])[:, 0:1]
        loss = jnp.log(total) - jnp.sum(wanted * scores[at], 0, keepdims=True)
        losses_ref[q : q + 1, :] = jnp.broadcast_to(loss, (1, 128))
        diffs.append(raised[at] / total - wanted)
    diff_raw = jnp.concatenate(diffs, axis=0) * (1.0 - capped_scores * capped_scores)
    grad_w_score = jnp.sum(scaled_two * diff_raw, 0, keepdims=True)
    diff_scaled = diff_raw * w_score
    grad_gain_score = jnp.sum(normed_two * diff_scaled, 0, keepdims=True)
    diff_normed = diff_scaled * gain_score
    diff_mixed = (diff_normed - normed_two * lane_mean(diff_normed * normed_two)) * inv_two
    diff_low = diff_mixed.astype(BF)
    diff_context = dot(diff_low, wo_ref[...], 1, 1).astype(BF)

    diff_q, diff_k, diff_v = [], [], []
    for q in range(queries):
        line_q, line_k, line_v = [], [], []
        for p in range(pairs):
            th = scores_t[q * pairs + p]
            attend = attend_t[q * pairs + p]
            split = heads_apart(cut(diff_context, q, p))
            diff_attend = dot(cut(v_all, q, p), split, 1, 1)
            line_v.append(dot(attend.astype(BF), split))
            inner = diff_attend - jnp.sum(attend * diff_attend, 0, keepdims=True)
            diff_logits = (attend * inner * (1.0 - th * th) * shrink).astype(BF)
            line_q.append(heads_joined(dot(diff_logits, cut(k_all, q, p), 0, 0)))
            line_k.append(dot(diff_logits, heads_apart(cut(q_all, q, p))))
        diff_q.append(jnp.concatenate(line_q, axis=1))
        diff_k.append(jnp.concatenate(line_k, axis=1))
        diff_v.append(jnp.concatenate(line_v, axis=1))
    diff_q = jnp.concatenate(diff_q, axis=0).astype(BF)
    diff_k = jnp.concatenate(diff_k, axis=0).astype(BF)
    diff_v = jnp.concatenate(diff_v, axis=0).astype(BF)

    first_core = core_ref[0] == 0
    first_pair = (first_input, first_input, diff_q, diff_k)
    second_pair = (first_input, context, diff_v, diff_low)
    for i in range(4):
        keep_ref[i] = jnp.where(first_core, first_pair[i], second_pair[i])
        send_ref[i] = jnp.where(first_core, second_pair[i], first_pair[i])
    sent = [
        pltpu.make_async_copy(send_ref, send_hbm, sem.at[5]),
        pltpu.make_async_copy(keep_ref, keep_hbm, sem.at[6]),
    ]
    for c in sent:
        c.start()

    diff_input = dot(diff_q, wq_ref[...], 1, 1) + dot(diff_k, wk_ref[...], 1, 1) + dot(diff_v, wv_ref[...], 1, 1)
    grad_gain_attn = jnp.sum(normed_one * diff_input, 0, keepdims=True)
    diff_first = diff_input * gain_attn
    diff_base = diff_mixed + (diff_first - normed_one * lane_mean(diff_first * normed_one)) * inv_one
    for q in range(queries):
        query_grad_ref[q : q + 1, :] = jnp.sum(diff_base[size * q : size * (q + 1)], 0, keepdims=True)
    for m in range(4):
        slab = diff_base[:, SLAB * m : SLAB * (m + 1)]
        held[m, :256, :] = slab[:, :128].astype(BF)
        held[m, 256:, :] = jnp.concatenate([slab[:128, 128:], slab[128:, 128:]], axis=1).astype(BF)
    for k, ref in enumerate((base_0_ref, base_1_ref, base_2_ref, base_3_ref)):
        ref[...] = held[(me + k) & 3]
    vectors = [
        v[:, 128 * t : 128 * (t + 1)]
        for v in (grad_gain_attn, grad_gain_score, grad_w_score)
        for t in range(width // 128)
    ]
    vectors_ref[...] = jnp.concatenate(vectors + [jnp.zeros((32 - len(vectors), 128), F32)], axis=0)
    for c in sent:
        c.wait()


def gradients_kernel(me_ref, keep_hbm, other_ref, vectors_ref, *refs):
    out_refs, (token_ref, grads, held, keep_ref, sem) = refs[:4], refs[4:]
    token_ref[...] = jnp.zeros_like(token_ref)
    copies = [pltpu.make_async_copy(keep_hbm.at[i], keep_ref.at[i], sem.at[i]) for i in (0, 2, 1, 3)]
    for c in copies:
        c.start()
    for j in (0, 1):
        copies[2 * j].wait()
        copies[2 * j + 1].wait()
        left = jnp.concatenate([keep_ref[j], other_ref[j]], axis=0)
        right = jnp.concatenate([keep_ref[2 + j], other_ref[2 + j]], axis=0)
        grads[j] = dot(left, right, 0, 0)

    def assemble(at, carry):
        rows48 = jnp.concatenate([grads[j, pl.ds(pl.multiple_of(24 * at, 8), 24), :] for j in (0, 1)], axis=0)
        for m in range(4):
            tiles = []
            for h in range(9 * m, 9 * m + 9):
                rb, t = h // 6, h % 6
                tiles.append(rows48[8 * rb : 8 * rb + 8, 128 * t : 128 * (t + 1)])
            tiles.append(vectors_ref[8 * m : 8 * m + 8, :])
            held[m, at] = jnp.concatenate(tiles, axis=0).astype(BF)
        return carry

    lax.fori_loop(0, held.shape[1], assemble, 0)
    copies = []
    for k, ref in enumerate(out_refs):
        copies.append(pltpu.make_async_copy(held.at[(me_ref[0] + k) & 3], ref, sem.at[4 + k]))
        copies[-1].start()
    for c in copies:
        c.wait()


def plus(*refs):
    total = refs[0].astype(F32)
    for r in refs[1:]:
        total = total + r.astype(F32)
    return total.astype(BF)


def sum_kernel(own_hbm, b_ref, c_ref, d_ref, out_hbm, own_ref, out_ref, sem):
    copy = pltpu.make_async_copy(own_hbm, own_ref, sem.at[0])
    copy.start()
    copy.wait()
    n = own_ref.shape[0] // 2
    copies = []
    for i in (0, 1):
        at = pl.ds(n * i, n)
        out_ref[n * i : n * (i + 1)] = plus(*[r[n * i : n * (i + 1)] for r in (own_ref, b_ref, c_ref, d_ref)])
        copies.append(pltpu.make_async_copy(out_ref.at[at], out_hbm.at[at], sem.at[1 + i]))
        copies[-1].start()
    for c in copies:
        c.wait()


def last_kernel(parts_ref, out_ref):
    total = plus(*[parts_ref[i] for i in range(parts_ref.shape[0])])
    for i in range(out_ref.shape[0]):
        out_ref[i] = total


def finish_kernel(core_ref, blocks_ref, q_ref, k_ref, v_ref, o_ref, *vec_refs):
    blocks = blocks_ref[...].astype(F32)
    first_core = core_ref[0] == 0
    rows48, vectors = [], []
    for at in (0, 4):
        tiles = [blocks[at + m, 8 * i : 8 * i + 8] for m in range(4) for i in range(9)]
        rows48.append(
            jnp.concatenate([jnp.concatenate(tiles[6 * rb : 6 * rb + 6], axis=1) for rb in range(6)], axis=0)
        )
        vectors.append(jnp.concatenate([blocks[at + m, 72:] for m in range(4)], axis=0))
    for pair, refs in ((rows48[0], (q_ref, k_ref)), (rows48[1], (v_ref, o_ref))):
        for i, ref in enumerate(refs):
            ref[...] = jnp.where(first_core, pair[24 * i : 24 * i + 12], pair[24 * i + 12 : 24 * i + 24])
    vectors = vectors[0] + vectors[1]
    for i, ref in enumerate(vec_refs):
        for t in range(6):
            ref[pl.ds(128 * t, 128)] = vectors[6 * i + t]


def shape(dims, kind=BF):
    return jax.ShapeDtypeStruct(dims, kind)


def swap(x, axes):
    return lax.all_to_all(x, axes, split_axis=0, concat_axis=0, tiled=True)


def body(
    cand_item,
    list_place,
    item_table,
    query_vec,
    labels,
    query_weight,
    key_weight,
    value_weight,
    output_weight,
    gain_attn,
    gain_score,
    w_score,
):
    queries, size = cand_item.shape
    stored, slab = item_table.shape
    width = query_vec.shape[1]
    n_dp = lax.axis_size(ROWS)
    n_mp = lax.axis_size("x")
    n_yz = lax.axis_size(("y", "z"))
    slots = n_dp * CAP

    along_x = lax.axis_index("x").astype(jnp.int32).reshape(1)
    core = lax.axis_index("c").astype(jnp.int32).reshape(1)

    ids = exchange([cand_item] * 4, "x")
    lookup, own_ids = call(
        lookup_kernel,
        [pltpu.VMEM((128, list_place.shape[0]), BF), pltpu.VMEM((queries, size), jnp.int32)],
        (list_place.reshape(1, -1), cand_item), 4, 10**6, 10**6,
        [pltpu.VMEM((1, list_place.shape[0]), jnp.int32), pltpu.SemaphoreType.DMA((2,))], 0, (0, 1),
    )
    request, slot = call(
        routing_kernel,
        [shape((n_dp, CAP), jnp.int32), shape((n_mp * queries, size), jnp.int32)],
        (along_x, own_ids, *ids[1:], lookup),
        8, 3 * 10**8, 10**6, [pltpu.VMEM((n_mp, queries, size), jnp.int32)], 1,
    )
    asked = swap(request, ROWS)
    table = call(
        load_kernel, pltpu.VMEM((256, stored), BF), (item_table.T,), 4, 10**6, 2 * 10**6,
        [pltpu.SemaphoreType.DMA((2,))], 0, (0,), (request,),
    )
    found = call(
        owner_kernel, shape((n_dp, 48, 128)), (asked, inside(table)), 16, 2 * 10**9, 2 * 10**6
    )
    fetched = swap(found, ROWS)
    pieces = call(
        pieces_kernel, [pltpu.HBM((384, 128), BF)] + [shape((384, 128))] * 3, (along_x, slot, fetched),
        16, 10**9, 2 * 10**6, [pltpu.VMEM((384, 128), BF), pltpu.SemaphoreType.DMA((1,))], 1,
    )
    rows_in = exchange(pieces, "x")
    acts = pltpu.HBM((4, queries * size, width), BF)
    outs = call(
        step_kernel,
        [shape((queries, 128), F32), shape((queries, width), F32)]
        + [shape((384, 128))] * n_mp
        + [acts] * 2
        + [shape((32, 128), F32)],
        (
            along_x, core, *rows_in, query_vec, labels,
            query_weight, key_weight, value_weight, output_weight,
            gain_attn.reshape(1, -1), gain_score.reshape(1, -1), w_score.reshape(1, -1),
        ),
        32, 4 * 10**9, 10**7,
        [
            pltpu.VMEM((n_mp, 384, 128), BF),
            pltpu.VMEM((HEADS * queries // 2, 128, 256), F32),
            pltpu.VMEM((HEADS * queries // 2, 128, 256), F32),
        ]
        + [pltpu.VMEM((width, width), BF)] * 4
        + [pltpu.VMEM((4, queries * size, width), BF)] * 2
        + [pltpu.SemaphoreType.DMA((7,))],
        2, (2, 8, 9, 10, 11),
    )
    losses, query_grad, diff_base = outs[0], outs[1], outs[2:6]
    keep, send, vectors = outs[6:]

    column_grads = exchange(diff_base, "x")

    other = lax.ppermute(send, "c", [(0, 1), (1, 0)])
    block = shape((n_yz, 80, 128))
    *blocks, made = call(
        gradients_kernel, [pltpu.HBM(block.shape, BF)] * n_mp + [shape((8, 128), F32)], (along_x, keep, other, vectors), 32, 2 * 10**9, 10**7,
        [
            pltpu.VMEM((2, width, width), F32),
            pltpu.VMEM((n_mp, n_yz, 80, 128), BF),
            pltpu.VMEM((4, queries * size, width), BF),
            pltpu.SemaphoreType.DMA((8,)),
        ],
        1, (1,), column_grads[1:],
    )
    arrive = exchange(blocks, "x")

    outgoing = call(
        slots_kernel, shape((n_dp, 48, 128)), (along_x, slot, *column_grads), 16, 10**9, 2 * 10**6,
        [pltpu.VMEM((n_mp, 384, 128), BF)], 1, awaited=(made,),
    )
    arrived = swap(outgoing, ROWS)
    landed, token = call(
        landing_kernel,
        [pltpu.HBM((slab, stored), F32), shape((8, 128), F32)],
        (asked, arrived),
        20, 2 * 10**9, 4 * 10**6, [pltpu.VMEM((slab, stored), F32), pltpu.SemaphoreType.DMA((4,))],
    )
    table_grad = landed.T

    over_x = call(
        sum_kernel, pltpu.HBM(block.shape, BF), tuple(arrive), 8, 10**12, 10**7,
        [pltpu.VMEM(block.shape, BF), pltpu.VMEM(block.shape, BF), pltpu.SemaphoreType.DMA((3,))], 0, (0,),
    )
    parts = swap(after(over_x, arrived), ("y", "z"))
    copies = call(last_kernel, shape((2 * n_mp, 80, 128)), (parts,), 4, 10**6, 10**6, awaited=(token,))
    blocks = swap(copies, ("c", "x"))
    rows = width // n_dp
    finished = call(
        finish_kernel,
        [shape((rows, width), F32)] * 4 + [shape((width,), F32)] * 3,
        (core, blocks), 4, 10**6, 10**6, (), 1,
    )
    return (
        losses[:, 0],
        table_grad,
        query_grad,
        *finished,
    )


def solution(mesh):
    grid = Mesh(mesh.devices.reshape(4, 8, 2, 4), ("y", "z", "c", "x"))
    each = P(("y", "z", "c", "x"), None)
    placed = (each, P(), P(ROWS, "x"), each, each, P(), P(), P(), P(), P(), P(), P())
    return jax.shard_map(
        body,
        mesh=grid,
        in_specs=placed,
        out_specs=(
            P(("y", "z", "c", "x")),
            P(ROWS, "x"),
            each,
            P(ROWS, None),
            P(ROWS, None),
            P(ROWS, None),
            P(ROWS, None),
            P(),
            P(),
            P(),
        ),
        check_vma=False,
    )
```

```python
import jax
import jax.numpy as jnp
from jax import lax
from jax.experimental import pallas as pl
from jax.experimental.pallas import tpu as pltpu
from jax.sharding import Mesh
from jax.sharding import PartitionSpec as P

HEADS = 12
LIST_LEN = 256
EPSILON = 1e-06
SCORE_CAP = 20.0
RANK_CAP = 30.0

ROWS = ("y", "z", "c")
CAP = 32
SLAB = 192
BF = jnp.bfloat16
F32 = jnp.float32
MIB = 1024 * 1024


def dot(a, b, ca=1, cb=0):
    return lax.dot_general(a, b, (((ca,), (cb,)), ((), ())), preferred_element_type=F32)


def iota(shape, dim):
    return lax.broadcasted_iota(jnp.int32, shape, dim)


def whole(n):
    return [pl.BlockSpec(memory_space=pltpu.VMEM)] * n


def inside(x):
    return pltpu.with_memory_space_constraint(x, pltpu.VMEM)


def stays(x):
    return pltpu.with_memory_space_constraint(x, pltpu.HBM)


def call(kernel, out_shape, args, mib, flops, size, scratch=(), scalars=0, left=(), awaited=()):
    many = isinstance(out_shape, (list, tuple))
    outs = out_shape if many else [out_shape]
    specs = [
        pl.BlockSpec(memory_space=pltpu.HBM if getattr(o, "memory_space", None) == pltpu.HBM else pltpu.VMEM)
        for o in outs
    ]
    in_specs = [pl.BlockSpec(memory_space=pltpu.SMEM)] * scalars + whole(len(args) - scalars)
    args = list(args)
    for i in left:
        in_specs[i] = pl.BlockSpec(memory_space=pltpu.HBM)
        args[i] = stays(args[i])
    in_specs += [pl.BlockSpec(memory_space=pl.ANY)] * len(awaited)

    def run(*refs):
        kernel(*refs[: len(args)], *refs[len(args) + len(awaited) :])

    return pl.pallas_call(
        run,
        out_shape=out_shape,
        in_specs=in_specs,
        out_specs=specs if many else specs[0],
        scratch_shapes=list(scratch),
        compiler_params=pltpu.CompilerParams(vmem_limit_bytes=mib * MIB),
        cost_estimate=pl.CostEstimate(flops=flops, bytes_accessed=size, transcendentals=0),
    )(*args, *awaited)


def after(x, awaited):
    return pl.pallas_call(
        lambda *refs: None,
        out_shape=shape(x.shape, x.dtype),
        in_specs=[pl.BlockSpec(memory_space=pl.ANY)] * 2,
        out_specs=pl.BlockSpec(memory_space=pl.ANY),
        input_output_aliases={0: 0},
    )(x, awaited)


def shift(x, axis, by):
    return lax.ppermute(x, axis, [(i, (i + by) % 4) for i in range(4)])


def exchange(blocks, axis):
    far = shift(blocks[2], axis, 2)
    return [blocks[0], shift(blocks[1], axis, 1), far, shift(blocks[3], axis, 3)]


def collect(me, refs, held):
    for k, ref in enumerate(refs):
        held[(me - k) & 3] = ref[...]


def low_half(shape):
    return iota(shape, len(shape) - 1) < 64


def swap_halves(t):
    return jnp.concatenate([t[..., 64:], t[..., :64]], axis=-1)


def spread_tail(t):
    t = t.astype(F32)
    other = swap_halves(t)
    low = low_half(t.shape)
    return jnp.concatenate([jnp.where(low, t, other), jnp.where(low, other, t)], axis=1)


def unpack(block):
    b, rows, _ = block.shape
    n = rows // 3
    main = block[:, : 2 * n, :].reshape(b * 2 * n, 128)
    tail = spread_tail(block[:, 2 * n :, :]).astype(BF).reshape(b * 2 * n, 128)
    return jnp.concatenate([main, tail], axis=1)


def pack(full, n):
    tail = full[:, 128:]
    tail = jnp.where(low_half((n, 128)), tail[:n], tail[n:])
    return jnp.concatenate([full[:, :128], tail], axis=0).astype(BF)


def as_column(row):
    return jnp.transpose(jnp.broadcast_to(row, (128, 128)))


def lookup_kernel(place_hbm, ids_hbm, lookup_ref, ids_ref, place_ref, sem):
    copies = [
        pltpu.make_async_copy(place_hbm, place_ref, sem.at[0]),
        pltpu.make_async_copy(ids_hbm, ids_ref, sem.at[1]),
    ]
    for c in copies:
        c.start()
    for c in copies:
        c.wait()
    place = place_ref[...]
    lists = place.shape[1]
    owner_of_list = jnp.broadcast_to(place >> 3, (128, lists))
    row = iota((128, lists), 0)
    lookup = jnp.where(owner_of_list == row, 1.0, 0.0)
    lookup = jnp.where(row == 64, jnp.broadcast_to(place & 7, (128, lists)).astype(F32), lookup)
    lookup_ref[...] = lookup.astype(BF)


def routing_kernel(me_ref, a_ref, b_ref, c_ref, d_ref, lookup_ref, request_ref, slot_ref, held):
    collect(me_ref[0], (a_ref, b_ref, c_ref, d_ref), held)
    lookup = lookup_ref[...]
    lists = lookup.shape[1]
    lane = iota((128, 128), 1)
    before = (iota((128, 128), 1) < iota((128, 128), 0)).astype(F32).astype(BF)
    carry = jnp.zeros((1, 128), F32)
    request = jnp.zeros((128, 128), F32)
    for q in range(slot_ref.shape[0]):
        ids = as_column(held[q // 2, q % 2 : q % 2 + 1, :])
        list_id = ids >> 8
        chosen = jnp.concatenate(
            [(list_id == lane + 128 * t).astype(F32).astype(BF) for t in range(lists // 128)], axis=1
        )
        found = dot(chosen, lookup, 1, 1)
        sub = jnp.sum(jnp.where(lane == 64, found, 0.0), 1, keepdims=True)
        onehot = jnp.where(lane < 64, found, 0.0)
        onehot_low = onehot.astype(BF)
        ahead = dot(before, onehot_low) + carry
        carry = carry + jnp.sum(onehot, 0, keepdims=True)
        rank = jnp.sum(onehot * ahead, 1, keepdims=True)
        owner = jnp.sum(onehot * lane.astype(F32), 1, keepdims=True)
        slot = jnp.broadcast_to(owner * CAP + rank, (128, 128))
        slot_ref[q : q + 1, :] = jnp.transpose(slot)[0:1, :].astype(jnp.int32)
        rank = rank.astype(jnp.int32)
        place_in = (ids & 255).astype(F32)
        entry = jnp.where(rank == lane, sub + 1.0, jnp.where(rank == lane - CAP, place_in, 0.0))
        request = request + dot(onehot_low, entry.astype(BF), 0, 0)
    high = request[:64, :CAP]
    low = request[:64, CAP : 2 * CAP]
    asked = (high - 1.0) * LIST_LEN + low
    request_ref[...] = jnp.where(high > 0.5, asked, -1.0).astype(jnp.int32)


def four_groups(asked):
    part = asked.shape[0] // 4
    return jnp.concatenate([asked[part * k : part * (k + 1)] for k in range(4)], axis=1)


def load_kernel(table_hbm, table_ref, sem):
    copies = [
        pltpu.make_async_copy(table_hbm, table_ref.at[pl.ds(0, SLAB)], sem.at[0]),
        pltpu.make_async_copy(table_hbm.at[pl.ds(128, 64)], table_ref.at[pl.ds(SLAB, 64)], sem.at[1]),
    ]
    for c in copies:
        c.start()
    for c in copies:
        c.wait()


def owner_kernel(asked_ref, table_ref, out_ref):
    asked = four_groups(asked_ref[...])
    part = asked.shape[0]
    stored = table_ref.shape[1]
    step = 4
    for r in range(0, part, step):
        column = jnp.concatenate([as_column(asked[r + i : r + i + 1]) for i in range(step)], axis=0)
        lane = iota((128 * step, 128), 1)
        chosen = jnp.concatenate(
            [(column == lane + 128 * t).astype(F32).astype(BF) for t in range(stored // 128)], axis=1
        )
        rows = dot(chosen, table_ref[...], 1, 1)
        for i in range(step):
            for k in range(4):
                at = 128 * i + CAP * k
                out_ref[part * k + r + i] = pack(rows[at : at + CAP], CAP // 2)


def pieces_kernel(me_ref, slot_ref, fetched_ref, own_hbm, *refs):
    out_refs, own_ref, sem = refs[:3], refs[3], refs[4]
    fetched = unpack(fetched_ref[...])
    slots = fetched.shape[0]
    copy = pltpu.make_async_copy(own_ref, own_hbm, sem.at[0])
    for k, out_ref in enumerate((own_ref, *out_refs)):
        m = (me_ref[0] + k) & 3
        column = jnp.concatenate([as_column(slot_ref[pl.ds(2 * m + i, 1), :]) for i in (0, 1)], axis=0)
        lane = iota((256, 128), 1)
        chosen = jnp.concatenate(
            [(column == lane + 128 * t).astype(F32).astype(BF) for t in range(slots // 128)], axis=1
        )
        out_ref[...] = pack(dot(chosen, fetched), 128)
        if k == 0:
            copy.start()
    copy.wait()


def slots_kernel(me_ref, slot_ref, a_ref, b_ref, c_ref, d_ref, out_hbm, held, out_ref, sem):
    collect(me_ref[0], (a_ref, b_ref, c_ref, d_ref), held)
    grads = unpack(held[...])
    groups = out_ref.shape[0]
    step = 16 * CAP
    copies = []
    for r in range(0, groups * CAP, step):
        row = iota((step, 128), 0) + r
        chosen = jnp.concatenate(
            [
                (jnp.broadcast_to(slot_ref[q : q + 1, :], (step, 128)) == row).astype(F32).astype(BF)
                for q in range(slot_ref.shape[0])
            ],
            axis=1,
        )
        rows = dot(chosen, grads)
        for i in range(16):
            out_ref[r // CAP + i] = pack(rows[CAP * i : CAP * (i + 1)], CAP // 2)
        at = pl.ds(r // CAP, 16)
        copies.append(pltpu.make_async_copy(out_ref.at[at], out_hbm.at[at], sem.at[r // step]))
        copies[-1].start()
    for c in copies:
        c.wait()


def landing_kernel(asked_ref, arrived_ref, out_hbm, token_ref, out_ref, sem):
    token_ref[...] = jnp.zeros_like(token_ref)
    arrived = unpack(arrived_ref[...])
    stored = out_ref.shape[1]
    slots = arrived.shape[0]
    asked = four_groups(asked_ref[...])
    part = asked.shape[0]
    columns = [as_column(asked[r : r + 1]) for r in range(part)]
    column = jnp.concatenate(
        [columns[g % part][CAP * (g // part) : CAP * (g // part + 1)] for g in range(4 * part)], axis=0
    )
    step = 512
    copies = []
    lane = iota((slots, 128), 1)
    for r in range(0, stored, step):
        chosen = jnp.concatenate(
            [(column == lane + (r + 128 * t)).astype(F32).astype(BF) for t in range(step // 128)], axis=1
        )
        out_ref[:, r : r + step] = dot(arrived, chosen, 0, 0)[:SLAB]
        at = pl.ds(r, step)
        copies.append(pltpu.make_async_copy(out_ref.at[:, at], out_hbm.at[:, at], sem.at[r // step]))
        copies[-1].start()
    for c in copies:
        c.wait()


def lane_mean(x):
    return jnp.sum(x, 1, keepdims=True) * (1.0 / x.shape[1])


def step_kernel(
    me_ref,
    core_ref,
    a_hbm,
    b_ref,
    c_ref,
    d_ref,
    query_ref,
    labels_ref,
    wq_hbm,
    wk_hbm,
    wv_hbm,
    wo_hbm,
    gain_attn_ref,
    gain_score_ref,
    w_score_ref,
    losses_ref,
    query_grad_ref,
    base_0_ref,
    base_1_ref,
    base_2_ref,
    base_3_ref,
    keep_hbm,
    send_hbm,
    vectors_ref,
    held,
    scores_t,
    attend_t,
    wq_ref,
    wk_ref,
    wv_ref,
    wo_ref,
    keep_ref,
    send_ref,
    sem,
):
    me = me_ref[0]
    own = pltpu.make_async_copy(a_hbm, held.at[me], sem.at[8])
    own.start()
    sources = (wq_hbm, wk_hbm, wv_hbm, wo_hbm)
    weights = (wq_ref, wk_ref, wv_ref, wo_ref)
    half = wq_ref.shape[0] // 2
    copies = [
        pltpu.make_async_copy(a.at[pl.ds(half * h, half)], b.at[pl.ds(half * h, half)], sem.at[2 * i + h])
        for i, (a, b) in enumerate(zip(sources, weights))
        for h in (0, 1)
    ]
    for c in copies:
        c.start()
    for k, ref in ((1, b_ref), (2, c_ref), (3, d_ref)):
        held[(me - k) & 3] = ref[...]
    own.wait()
    queries, width = query_ref.shape
    size = 128
    head = width // HEADS
    pairs = HEADS // 2
    shrink = head ** (-0.5)
    low = low_half((size, 128))

    parts = []
    for m in range(4):
        main = held[m, :256, :].astype(F32)
        tail = held[m, 256:, :].astype(F32)
        parts += [main, jnp.concatenate([tail[:, :64], tail[:, 64:]], axis=0)]
    rows_in = jnp.concatenate(parts, axis=1)
    vecs = query_ref[...].astype(F32)
    vecs = jnp.concatenate([jnp.broadcast_to(vecs[q : q + 1], (size, width)) for q in range(queries)], axis=0)
    base = rows_in + vecs
    inv_one = 1.0 / jnp.sqrt(lane_mean(base * base) + EPSILON)
    normed_one = base * inv_one
    gain_attn = gain_attn_ref[...]
    first_input = (normed_one * gain_attn).astype(BF)
    for c in copies[0 : 2]:
        c.wait()
    q_all = dot(first_input, wq_ref[...]).astype(BF)
    for c in copies[2 : 4]:
        c.wait()
    k_all = dot(first_input, wk_ref[...]).astype(BF)
    for c in copies[4 : 6]:
        c.wait()
    v_all = dot(first_input, wv_ref[...]).astype(BF)

    def cut(x, q, p):
        return x[size * q : size * (q + 1), 128 * p : 128 * (p + 1)]

    zero = jnp.zeros((size, 128), BF)

    def heads_apart(x):
        return jnp.concatenate([jnp.where(low, x, zero), jnp.where(low, zero, x)], axis=0)

    def heads_joined(x):
        return jnp.where(low, x[:size], x[size:])

    context = []
    for q in range(queries):
        line = []
        for p in range(pairs):
            logits = dot(cut(k_all, q, p), heads_apart(cut(q_all, q, p)), 1, 1)
            th = jnp.tanh(logits * (shrink / SCORE_CAP))
            raised = jnp.exp(SCORE_CAP * th)
            attend = raised * (1.0 / jnp.sum(raised, 0, keepdims=True))
            scores_t[q * pairs + p] = th
            attend_t[q * pairs + p] = attend
            line.append(heads_joined(dot(attend.astype(BF), cut(v_all, q, p), 0, 0)))
        context.append(jnp.concatenate(line, axis=1))
    context = jnp.concatenate(context, axis=0).astype(BF)

    for c in copies[6 : 8]:
        c.wait()
    mixed = base + dot(context, wo_ref[...])
    inv_two = 1.0 / jnp.sqrt(lane_mean(mixed * mixed) + EPSILON)
    normed_two = mixed * inv_two
    gain_score = gain_score_ref[...]
    w_score = w_score_ref[...]
    scaled_two = normed_two * gain_score
    capped_scores = jnp.tanh(jnp.sum(scaled_two * w_score, 1, keepdims=True) * (1.0 / RANK_CAP))
    scores = RANK_CAP * capped_scores
    raised = jnp.exp(scores)
    relevance = jnp.exp(labels_ref[...].astype(F32))
    target = relevance / jnp.sum(relevance, 1, keepdims=True)
    diffs = []
    for q in range(queries):
        at = slice(size * q, size * (q + 1))
        total = jnp.sum(raised[at], 0, keepdims=True)
        wanted = as_column(target[q : q + 1])[:, 0:1]
        loss = jnp.log(total) - jnp.sum(wanted * scores[at], 0, keepdims=True)
        losses_ref[q : q + 1, :] = jnp.broadcast_to(loss, (1, 128))
        diffs.append(raised[at] / total - wanted)
    diff_raw = jnp.concatenate(diffs, axis=0) * (1.0 - capped_scores * capped_scores)
    grad_w_score = jnp.sum(scaled_two * diff_raw, 0, keepdims=True)
    diff_scaled = diff_raw * w_score
    grad_gain_score = jnp.sum(normed_two * diff_scaled, 0, keepdims=True)
    diff_normed = diff_scaled * gain_score
    diff_mixed = (diff_normed - normed_two * lane_mean(diff_normed * normed_two)) * inv_two
    diff_low = diff_mixed.astype(BF)
    diff_context = dot(diff_low, wo_ref[...], 1, 1).astype(BF)

    diff_q, diff_k, diff_v = [], [], []
    for q in range(queries):
        line_q, line_k, line_v = [], [], []
        for p in range(pairs):
            th = scores_t[q * pairs + p]
            attend = attend_t[q * pairs + p]
            split = heads_apart(cut(diff_context, q, p))
            diff_attend = dot(cut(v_all, q, p), split, 1, 1)
            line_v.append(dot(attend.astype(BF), split))
            inner = diff_attend - jnp.sum(attend * diff_attend, 0, keepdims=True)
            diff_logits = (attend * inner * (1.0 - th * th) * shrink).astype(BF)
            line_q.append(heads_joined(dot(diff_logits, cut(k_all, q, p), 0, 0)))
            line_k.append(dot(diff_logits, heads_apart(cut(q_all, q, p))))
        diff_q.append(jnp.concatenate(line_q, axis=1))
        diff_k.append(jnp.concatenate(line_k, axis=1))
        diff_v.append(jnp.concatenate(line_v, axis=1))
    diff_q = jnp.concatenate(diff_q, axis=0).astype(BF)
    diff_k = jnp.concatenate(diff_k, axis=0).astype(BF)
    diff_v = jnp.concatenate(diff_v, axis=0).astype(BF)

    first_core = core_ref[0] == 0
    first_pair = (first_input, first_input, diff_q, diff_k)
    second_pair = (first_input, context, diff_v, diff_low)
    for i in range(4):
        keep_ref[i] = jnp.where(first_core, first_pair[i], second_pair[i])
        send_ref[i] = jnp.where(first_core, second_pair[i], first_pair[i])
    sent = [
        pltpu.make_async_copy(a.at[i], b.at[i], sem.at[9 + 4 * j + i])
        for j, (a, b) in enumerate(((send_ref, send_hbm), (keep_ref, keep_hbm)))
        for i in range(4)
    ]
    for c in sent:
        c.start()

    diff_input = dot(diff_q, wq_ref[...], 1, 1) + dot(diff_k, wk_ref[...], 1, 1) + dot(diff_v, wv_ref[...], 1, 1)
    grad_gain_attn = jnp.sum(normed_one * diff_input, 0, keepdims=True)
    diff_first = diff_input * gain_attn
    diff_base = diff_mixed + (diff_first - normed_one * lane_mean(diff_first * normed_one)) * inv_one
    for q in range(queries):
        query_grad_ref[q : q + 1, :] = jnp.sum(diff_base[size * q : size * (q + 1)], 0, keepdims=True)
    for m in range(4):
        slab = diff_base[:, SLAB * m : SLAB * (m + 1)]
        held[m, :256, :] = slab[:, :128].astype(BF)
        held[m, 256:, :] = jnp.concatenate([slab[:128, 128:], slab[128:, 128:]], axis=1).astype(BF)
    for k, ref in enumerate((base_0_ref, base_1_ref, base_2_ref, base_3_ref)):
        ref[...] = held[(me + k) & 3]
    vectors = [
        v[:, 128 * t : 128 * (t + 1)]
        for v in (grad_gain_attn, grad_gain_score, grad_w_score)
        for t in range(width // 128)
    ]
    vectors_ref[...] = jnp.concatenate(vectors + [jnp.zeros((32 - len(vectors), 128), F32)], axis=0)
    for c in sent:
        c.wait()


def gradients_kernel(me_ref, keep_hbm, other_ref, vectors_ref, *refs):
    out_refs, (token_ref, grads, held, keep_ref, sem) = refs[:4], refs[4:]
    token_ref[...] = jnp.zeros_like(token_ref)
    copies = [pltpu.make_async_copy(keep_hbm.at[i], keep_ref.at[i], sem.at[i]) for i in (0, 2, 1, 3)]
    for c in copies:
        c.start()
    for j in (0, 1):
        copies[2 * j].wait()
        copies[2 * j + 1].wait()
        left = jnp.concatenate([keep_ref[j], other_ref[j]], axis=0)
        right = jnp.concatenate([keep_ref[2 + j], other_ref[2 + j]], axis=0)
        grads[j] = dot(left, right, 0, 0)

    def assemble(at, carry):
        rows48 = jnp.concatenate([grads[j, pl.ds(pl.multiple_of(24 * at, 8), 24), :] for j in (0, 1)], axis=0)
        for m in range(4):
            tiles = []
            for h in range(9 * m, 9 * m + 9):
                rb, t = h // 6, h % 6
                tiles.append(rows48[8 * rb : 8 * rb + 8, 128 * t : 128 * (t + 1)])
            tiles.append(vectors_ref[8 * m : 8 * m + 8, :])
            held[m, at] = jnp.concatenate(tiles, axis=0).astype(BF)
        return carry

    copies = []
    n = held.shape[1] // 2
    for part in (0, 1):
        lax.fori_loop(n * part, n * (part + 1), assemble, 0)
        at = pl.ds(n * part, n)
        for k, ref in enumerate(out_refs):
            source = held.at[(me_ref[0] + k) & 3, at]
            copies.append(pltpu.make_async_copy(source, ref.at[at], sem.at[4 + 4 * part + k]))
            copies[-1].start()
    for c in copies:
        c.wait()


def plus(*refs):
    total = refs[0].astype(F32)
    for r in refs[1:]:
        total = total + r.astype(F32)
    return total.astype(BF)


def sum_kernel(own_hbm, b_ref, c_ref, d_ref, out_hbm, own_ref, out_ref, sem):
    n = own_ref.shape[0] // 4
    loads = [
        pltpu.make_async_copy(own_hbm.at[pl.ds(n * i, n)], own_ref.at[pl.ds(n * i, n)], sem.at[i]) for i in range(4)
    ]
    for c in loads:
        c.start()
    copies = []
    for i in range(4):
        at = pl.ds(n * i, n)
        loads[i].wait()
        out_ref[n * i : n * (i + 1)] = plus(*[r[n * i : n * (i + 1)] for r in (own_ref, b_ref, c_ref, d_ref)])
        copies.append(pltpu.make_async_copy(out_ref.at[at], out_hbm.at[at], sem.at[4 + i]))
        copies[-1].start()
    for c in copies:
        c.wait()


def last_kernel(parts_ref, out_ref):
    total = plus(*[parts_ref[i] for i in range(parts_ref.shape[0])])
    for i in range(out_ref.shape[0]):
        out_ref[i] = total


def finish_kernel(core_ref, blocks_ref, q_ref, k_ref, v_ref, o_ref, *vec_refs):
    blocks = blocks_ref[...].astype(F32)
    first_core = core_ref[0] == 0
    rows48, vectors = [], []
    for at in (0, 4):
        tiles = [blocks[at + m, 8 * i : 8 * i + 8] for m in range(4) for i in range(9)]
        rows48.append(
            jnp.concatenate([jnp.concatenate(tiles[6 * rb : 6 * rb + 6], axis=1) for rb in range(6)], axis=0)
        )
        vectors.append(jnp.concatenate([blocks[at + m, 72:] for m in range(4)], axis=0))
    for pair, refs in ((rows48[0], (q_ref, k_ref)), (rows48[1], (v_ref, o_ref))):
        for i, ref in enumerate(refs):
            ref[...] = jnp.where(first_core, pair[24 * i : 24 * i + 12], pair[24 * i + 12 : 24 * i + 24])
    vectors = vectors[0] + vectors[1]
    for i, ref in enumerate(vec_refs):
        for t in range(6):
            ref[pl.ds(128 * t, 128)] = vectors[6 * i + t]


def shape(dims, kind=BF):
    return jax.ShapeDtypeStruct(dims, kind)


def swap(x, axes):
    return lax.all_to_all(x, axes, split_axis=0, concat_axis=0, tiled=True)


def body(
    cand_item,
    list_place,
    item_table,
    query_vec,
    labels,
    query_weight,
    key_weight,
    value_weight,
    output_weight,
    gain_attn,
    gain_score,
    w_score,
):
    queries, size = cand_item.shape
    stored, slab = item_table.shape
    width = query_vec.shape[1]
    n_dp = lax.axis_size(ROWS)
    n_mp = lax.axis_size("x")
    n_yz = lax.axis_size(("y", "z"))
    slots = n_dp * CAP

    along_x = lax.axis_index("x").astype(jnp.int32).reshape(1)
    core = lax.axis_index("c").astype(jnp.int32).reshape(1)

    ids = exchange([cand_item] * 4, "x")
    lookup, own_ids = call(
        lookup_kernel,
        [pltpu.VMEM((128, list_place.shape[0]), BF), pltpu.VMEM((queries, size), jnp.int32)],
        (list_place.reshape(1, -1), cand_item), 4, 10**6, 10**6,
        [pltpu.VMEM((1, list_place.shape[0]), jnp.int32), pltpu.SemaphoreType.DMA((2,))], 0, (0, 1),
    )
    request, slot = call(
        routing_kernel,
        [shape((n_dp, CAP), jnp.int32), shape((n_mp * queries, size), jnp.int32)],
        (along_x, own_ids, *ids[1:], lookup),
        8, 3 * 10**8, 10**6, [pltpu.VMEM((n_mp, queries, size), jnp.int32)], 1,
    )
    asked = swap(request, ROWS)
    table = call(
        load_kernel, pltpu.VMEM((256, stored), BF), (item_table.T,), 4, 10**6, 2 * 10**6,
        [pltpu.SemaphoreType.DMA((2,))], 0, (0,), (request,),
    )
    found = call(
        owner_kernel, shape((n_dp, 48, 128)), (asked, inside(table)), 16, 2 * 10**9, 2 * 10**6
    )
    fetched = swap(found, ROWS)
    pieces = call(
        pieces_kernel, [pltpu.HBM((384, 128), BF)] + [shape((384, 128))] * 3, (along_x, slot, fetched),
        16, 10**9, 2 * 10**6, [pltpu.VMEM((384, 128), BF), pltpu.SemaphoreType.DMA((1,))], 1,
    )
    rows_in = exchange(pieces, "x")
    acts = pltpu.HBM((4, queries * size, width), BF)
    outs = call(
        step_kernel,
        [shape((queries, 128), F32), shape((queries, width), F32)]
        + [shape((384, 128))] * n_mp
        + [acts] * 2
        + [shape((32, 128), F32)],
        (
            along_x, core, *rows_in, query_vec, labels,
            query_weight, key_weight, value_weight, output_weight,
            gain_attn.reshape(1, -1), gain_score.reshape(1, -1), w_score.reshape(1, -1),
        ),
        32, 4 * 10**9, 10**7,
        [
            pltpu.VMEM((n_mp, 384, 128), BF),
            pltpu.VMEM((HEADS * queries // 2, 128, 256), F32),
            pltpu.VMEM((HEADS * queries // 2, 128, 256), F32),
        ]
        + [pltpu.VMEM((width, width), BF)] * 4
        + [pltpu.VMEM((4, queries * size, width), BF)] * 2
        + [pltpu.SemaphoreType.DMA((17,))],
        2, (2, 8, 9, 10, 11),
    )
    losses, query_grad, diff_base = outs[0], outs[1], outs[2:6]
    keep, send, vectors = outs[6:]

    column_grads = exchange(diff_base, "x")

    other = lax.ppermute(send, "c", [(0, 1), (1, 0)])
    block = shape((n_yz, 80, 128))
    *blocks, made = call(
        gradients_kernel, [pltpu.HBM(block.shape, BF)] * n_mp + [shape((8, 128), F32)], (along_x, keep, other, vectors), 32, 2 * 10**9, 10**7,
        [
            pltpu.VMEM((2, width, width), F32),
            pltpu.VMEM((n_mp, n_yz, 80, 128), BF),
            pltpu.VMEM((4, queries * size, width), BF),
            pltpu.SemaphoreType.DMA((12,)),
        ],
        1, (1,), column_grads[1:],
    )
    arrive = exchange(blocks, "x")

    outgoing = call(
        slots_kernel, pltpu.HBM((n_dp, 48, 128), BF), (along_x, slot, *column_grads), 16, 10**9, 2 * 10**6,
        [pltpu.VMEM((n_mp, 384, 128), BF), pltpu.VMEM((n_dp, 48, 128), BF), pltpu.SemaphoreType.DMA((4,))], 1, awaited=(made,),
    )
    arrived = swap(outgoing, ROWS)
    landed, token = call(
        landing_kernel,
        [pltpu.HBM((slab, stored), F32), shape((8, 128), F32)],
        (asked, arrived),
        20, 2 * 10**9, 4 * 10**6, [pltpu.VMEM((slab, stored), F32), pltpu.SemaphoreType.DMA((4,))],
    )
    table_grad = landed.T

    over_x = call(
        sum_kernel, pltpu.HBM(block.shape, BF), tuple(arrive), 8, 10**12, 10**7,
        [pltpu.VMEM(block.shape, BF), pltpu.VMEM(block.shape, BF), pltpu.SemaphoreType.DMA((8,))], 0, (0,),
    )
    parts = swap(after(over_x, arrived), ("y", "z"))
    copies = call(last_kernel, shape((2 * n_mp, 80, 128)), (parts,), 4, 10**6, 10**6, awaited=(token,))
    blocks = swap(copies, ("c", "x"))
    rows = width // n_dp
    finished = call(
        finish_kernel,
        [shape((rows, width), F32)] * 4 + [shape((width,), F32)] * 3,
        (core, blocks), 4, 10**6, 10**6, (), 1,
    )
    return (
        losses[:, 0],
        table_grad,
        query_grad,
        *finished,
    )


def solution(mesh):
    grid = Mesh(mesh.devices.reshape(4, 8, 2, 4), ("y", "z", "c", "x"))
    each = P(("y", "z", "c", "x"), None)
    placed = (each, P(), P(ROWS, "x"), each, each, P(), P(), P(), P(), P(), P(), P())
    return jax.shard_map(
        body,
        mesh=grid,
        in_specs=placed,
        out_specs=(
            P(("y", "z", "c", "x")),
            P(ROWS, "x"),
            each,
            P(ROWS, None),
            P(ROWS, None),
            P(ROWS, None),
            P(ROWS, None),
            P(),
            P(),
            P(),
        ),
        check_vma=False,
    )
```

```python
import jax
import jax.numpy as jnp
from jax import lax
from jax.experimental import pallas as pl
from jax.experimental.pallas import tpu as pltpu
from jax.sharding import Mesh
from jax.sharding import PartitionSpec as P

HEADS = 12
LIST_LEN = 256
EPSILON = 1e-06
SCORE_CAP = 20.0
RANK_CAP = 30.0

ROWS = ("y", "z", "c")
CAP = 32
SLAB = 192
BF = jnp.bfloat16
F32 = jnp.float32
MIB = 1024 * 1024


def dot(a, b, ca=1, cb=0):
    return lax.dot_general(a, b, (((ca,), (cb,)), ((), ())), preferred_element_type=F32)


def iota(shape, dim):
    return lax.broadcasted_iota(jnp.int32, shape, dim)


def whole(n):
    return [pl.BlockSpec(memory_space=pltpu.VMEM)] * n


def inside(x):
    return pltpu.with_memory_space_constraint(x, pltpu.VMEM)


def stays(x):
    return pltpu.with_memory_space_constraint(x, pltpu.HBM)


def call(kernel, out_shape, args, mib, flops, size, scratch=(), scalars=0, left=(), awaited=()):
    many = isinstance(out_shape, (list, tuple))
    outs = out_shape if many else [out_shape]
    specs = [
        pl.BlockSpec(memory_space=pltpu.HBM if getattr(o, "memory_space", None) == pltpu.HBM else pltpu.VMEM)
        for o in outs
    ]
    in_specs = [pl.BlockSpec(memory_space=pltpu.SMEM)] * scalars + whole(len(args) - scalars)
    args = list(args)
    for i in left:
        in_specs[i] = pl.BlockSpec(memory_space=pltpu.HBM)
        args[i] = stays(args[i])
    in_specs += [pl.BlockSpec(memory_space=pl.ANY)] * len(awaited)

    def run(*refs):
        kernel(*refs[: len(args)], *refs[len(args) + len(awaited) :])

    return pl.pallas_call(
        run,
        out_shape=out_shape,
        in_specs=in_specs,
        out_specs=specs if many else specs[0],
        scratch_shapes=list(scratch),
        compiler_params=pltpu.CompilerParams(vmem_limit_bytes=mib * MIB),
        cost_estimate=pl.CostEstimate(flops=flops, bytes_accessed=size, transcendentals=0),
    )(*args, *awaited)


def after(x, awaited):
    return pl.pallas_call(
        lambda *refs: None,
        out_shape=shape(x.shape, x.dtype),
        in_specs=[pl.BlockSpec(memory_space=pl.ANY)] * 2,
        out_specs=pl.BlockSpec(memory_space=pl.ANY),
        input_output_aliases={0: 0},
    )(x, awaited)


def shift(x, axis, by):
    return lax.ppermute(x, axis, [(i, (i + by) % 4) for i in range(4)])


def exchange(blocks, axis):
    far = shift(blocks[2], axis, 2)
    return [blocks[0], shift(blocks[1], axis, 1), far, shift(blocks[3], axis, 3)]


def collect(me, refs, held):
    for k, ref in enumerate(refs):
        held[(me - k) & 3] = ref[...]


def low_half(shape):
    return iota(shape, len(shape) - 1) < 64


def swap_halves(t):
    return jnp.concatenate([t[..., 64:], t[..., :64]], axis=-1)


def spread_tail(t):
    t = t.astype(F32)
    other = swap_halves(t)
    low = low_half(t.shape)
    return jnp.concatenate([jnp.where(low, t, other), jnp.where(low, other, t)], axis=1)


def unpack(block):
    b, rows, _ = block.shape
    n = rows // 3
    main = block[:, : 2 * n, :].reshape(b * 2 * n, 128)
    tail = spread_tail(block[:, 2 * n :, :]).astype(BF).reshape(b * 2 * n, 128)
    return jnp.concatenate([main, tail], axis=1)


def pack(full, n):
    tail = full[:, 128:]
    tail = jnp.where(low_half((n, 128)), tail[:n], tail[n:])
    return jnp.concatenate([full[:, :128], tail], axis=0).astype(BF)


def as_column(row):
    return jnp.transpose(jnp.broadcast_to(row, (128, 128)))


def lookup_kernel(place_hbm, ids_hbm, lookup_ref, ids_ref, place_ref, sem):
    copies = [
        pltpu.make_async_copy(place_hbm, place_ref, sem.at[0]),
        pltpu.make_async_copy(ids_hbm, ids_ref, sem.at[1]),
    ]
    for c in copies:
        c.start()
    for c in copies:
        c.wait()
    place = place_ref[...]
    lists = place.shape[1]
    owner_of_list = jnp.broadcast_to(place >> 3, (128, lists))
    row = iota((128, lists), 0)
    lookup = jnp.where(owner_of_list == row, 1.0, 0.0)
    lookup = jnp.where(row == 64, jnp.broadcast_to(place & 7, (128, lists)).astype(F32), lookup)
    lookup_ref[...] = lookup.astype(BF)


def routing_kernel(me_ref, a_ref, b_ref, c_ref, d_ref, lookup_ref, request_ref, slot_ref, held):
    collect(me_ref[0], (a_ref, b_ref, c_ref, d_ref), held)
    lookup = lookup_ref[...]
    lists = lookup.shape[1]
    lane = iota((128, 128), 1)
    before = (iota((128, 128), 1) < iota((128, 128), 0)).astype(F32).astype(BF)
    carry = jnp.zeros((1, 128), F32)
    request = jnp.zeros((128, 128), F32)
    for q in range(slot_ref.shape[0]):
        ids = as_column(held[q // 2, q % 2 : q % 2 + 1, :])
        list_id = ids >> 8
        chosen = jnp.concatenate(
            [(list_id == lane + 128 * t).astype(F32).astype(BF) for t in range(lists // 128)], axis=1
        )
        found = dot(chosen, lookup, 1, 1)
        sub = jnp.sum(jnp.where(lane == 64, found, 0.0), 1, keepdims=True)
        onehot = jnp.where(lane < 64, found, 0.0)
        onehot_low = onehot.astype(BF)
        ahead = dot(before, onehot_low) + carry
        carry = carry + jnp.sum(onehot, 0, keepdims=True)
        rank = jnp.sum(onehot * ahead, 1, keepdims=True)
        owner = jnp.sum(onehot * lane.astype(F32), 1, keepdims=True)
        slot = jnp.broadcast_to(owner * CAP + rank, (128, 128))
        slot_ref[q : q + 1, :] = jnp.transpose(slot)[0:1, :].astype(jnp.int32)
        rank = rank.astype(jnp.int32)
        place_in = (ids & 255).astype(F32)
        entry = jnp.where(rank == lane, sub + 1.0, jnp.where(rank == lane - CAP, place_in, 0.0))
        request = request + dot(onehot_low, entry.astype(BF), 0, 0)
    high = request[:64, :CAP]
    low = request[:64, CAP : 2 * CAP]
    asked = (high - 1.0) * LIST_LEN + low
    request_ref[...] = jnp.where(high > 0.5, asked, -1.0).astype(jnp.int32)


def four_groups(asked):
    part = asked.shape[0] // 4
    return jnp.concatenate([asked[part * k : part * (k + 1)] for k in range(4)], axis=1)


def load_kernel(table_hbm, table_ref, sem):
    copies = [
        pltpu.make_async_copy(table_hbm, table_ref.at[pl.ds(0, SLAB)], sem.at[0]),
        pltpu.make_async_copy(table_hbm.at[pl.ds(128, 64)], table_ref.at[pl.ds(SLAB, 64)], sem.at[1]),
    ]
    for c in copies:
        c.start()
    for c in copies:
        c.wait()


def owner_kernel(asked_ref, table_ref, out_ref, held):
    held[...] = four_groups(asked_ref[...])
    part = held.shape[0]
    stored = table_ref.shape[1]
    step = 4
    lane = iota((128 * step, 128), 1)

    def look(at, carry):
        r = step * at
        column = jnp.concatenate([as_column(held[pl.ds(r + i, 1), :]) for i in range(step)], axis=0)
        chosen = jnp.concatenate(
            [(column == lane + 128 * t).astype(F32).astype(BF) for t in range(stored // 128)], axis=1
        )
        rows = dot(chosen, table_ref[...], 1, 1)
        for i in range(step):
            for k in range(4):
                first = 128 * i + CAP * k
                out_ref[part * k + r + i] = pack(rows[first : first + CAP], CAP // 2)
        return carry

    lax.fori_loop(0, part // step, look, 0)


def pieces_kernel(me_ref, slot_ref, fetched_ref, own_hbm, *refs):
    out_refs, own_ref, sem = refs[:3], refs[3], refs[4]
    fetched = unpack(fetched_ref[...])
    slots = fetched.shape[0]
    copy = pltpu.make_async_copy(own_ref, own_hbm, sem.at[0])
    for k, out_ref in enumerate((own_ref, *out_refs)):
        m = (me_ref[0] + k) & 3
        column = jnp.concatenate([as_column(slot_ref[pl.ds(2 * m + i, 1), :]) for i in (0, 1)], axis=0)
        lane = iota((256, 128), 1)
        chosen = jnp.concatenate(
            [(column == lane + 128 * t).astype(F32).astype(BF) for t in range(slots // 128)], axis=1
        )
        out_ref[...] = pack(dot(chosen, fetched), 128)
        if k == 0:
            copy.start()
    copy.wait()


def slots_kernel(me_ref, slot_ref, a_ref, b_ref, c_ref, d_ref, out_hbm, held, out_ref, sem):
    collect(me_ref[0], (a_ref, b_ref, c_ref, d_ref), held)
    grads = unpack(held[...])
    groups = out_ref.shape[0]
    step = 16 * CAP

    def place(at, carry):
        row = iota((step, 128), 0) + step * at
        chosen = jnp.concatenate(
            [
                (jnp.broadcast_to(slot_ref[q : q + 1, :], (step, 128)) == row).astype(F32).astype(BF)
                for q in range(slot_ref.shape[0])
            ],
            axis=1,
        )
        rows = dot(chosen, grads)
        for i in range(16):
            out_ref[16 * at + i] = pack(rows[CAP * i : CAP * (i + 1)], CAP // 2)
        part = pl.ds(16 * at, 16)
        pltpu.make_async_copy(out_ref.at[part], out_hbm.at[part], sem.at[at]).start()
        return carry

    lax.fori_loop(0, groups // 16, place, 0)
    for at in range(groups // 16):
        part = pl.ds(16 * at, 16)
        pltpu.make_async_copy(out_ref.at[part], out_hbm.at[part], sem.at[at]).wait()


def landing_kernel(asked_ref, arrived_ref, out_hbm, token_ref, out_ref, sem):
    token_ref[...] = jnp.zeros_like(token_ref)
    arrived = unpack(arrived_ref[...])
    stored = out_ref.shape[1]
    slots = arrived.shape[0]
    asked = four_groups(asked_ref[...])
    part = asked.shape[0]
    columns = [as_column(asked[r : r + 1]) for r in range(part)]
    column = jnp.concatenate(
        [columns[g % part][CAP * (g // part) : CAP * (g // part + 1)] for g in range(4 * part)], axis=0
    )
    step = 512
    lane = iota((slots, 128), 1)

    def land(i, carry):
        r = pl.multiple_of(step * i, step)
        chosen = jnp.concatenate(
            [(column == lane + (r + 128 * t)).astype(F32).astype(BF) for t in range(step // 128)], axis=1
        )
        at = pl.ds(r, step)
        out_ref[:, at] = dot(arrived, chosen, 0, 0)[:SLAB]
        pltpu.make_async_copy(out_ref.at[:, at], out_hbm.at[:, at], sem.at[i]).start()
        return carry

    lax.fori_loop(0, stored // step, land, 0)
    for i in range(stored // step):
        at = pl.ds(step * i, step)
        pltpu.make_async_copy(out_ref.at[:, at], out_hbm.at[:, at], sem.at[i]).wait()


def lane_mean(x):
    return jnp.sum(x, 1, keepdims=True) * (1.0 / x.shape[1])


def step_kernel(
    me_ref,
    core_ref,
    a_hbm,
    b_ref,
    c_ref,
    d_ref,
    query_ref,
    labels_ref,
    wq_hbm,
    wk_hbm,
    wv_hbm,
    wo_hbm,
    gain_attn_ref,
    gain_score_ref,
    w_score_ref,
    losses_ref,
    query_grad_ref,
    base_0_ref,
    base_1_ref,
    base_2_ref,
    base_3_ref,
    keep_hbm,
    send_hbm,
    vectors_ref,
    held,
    scores_t,
    attend_t,
    wq_ref,
    wk_ref,
    wv_ref,
    wo_ref,
    keep_ref,
    send_ref,
    sem,
):
    me = me_ref[0]
    own = pltpu.make_async_copy(a_hbm, held.at[me], sem.at[8])
    own.start()
    sources = (wq_hbm, wk_hbm, wv_hbm, wo_hbm)
    weights = (wq_ref, wk_ref, wv_ref, wo_ref)
    half = wq_ref.shape[0] // 2
    copies = [
        pltpu.make_async_copy(a.at[pl.ds(half * h, half)], b.at[pl.ds(half * h, half)], sem.at[2 * i + h])
        for i, (a, b) in enumerate(zip(sources, weights))
        for h in (0, 1)
    ]
    for c in copies:
        c.start()
    for k, ref in ((1, b_ref), (2, c_ref), (3, d_ref)):
        held[(me - k) & 3] = ref[...]
    own.wait()
    queries, width = query_ref.shape
    size = 128
    head = width // HEADS
    pairs = HEADS // 2
    shrink = head ** (-0.5)
    low = low_half((size, 128))

    parts = []
    for m in range(4):
        main = held[m, :256, :].astype(F32)
        tail = held[m, 256:, :].astype(F32)
        parts += [main, jnp.concatenate([tail[:, :64], tail[:, 64:]], axis=0)]
    rows_in = jnp.concatenate(parts, axis=1)
    vecs = query_ref[...].astype(F32)
    vecs = jnp.concatenate([jnp.broadcast_to(vecs[q : q + 1], (size, width)) for q in range(queries)], axis=0)
    base = rows_in + vecs
    inv_one = 1.0 / jnp.sqrt(lane_mean(base * base) + EPSILON)
    normed_one = base * inv_one
    gain_attn = gain_attn_ref[...]
    first_input = (normed_one * gain_attn).astype(BF)
    for c in copies[0 : 2]:
        c.wait()
    q_all = dot(first_input, wq_ref[...]).astype(BF)
    for c in copies[2 : 4]:
        c.wait()
    k_all = dot(first_input, wk_ref[...]).astype(BF)
    for c in copies[4 : 6]:
        c.wait()
    v_all = dot(first_input, wv_ref[...]).astype(BF)

    def cut(x, q, p):
        return x[size * q : size * (q + 1), 128 * p : 128 * (p + 1)]

    zero = jnp.zeros((size, 128), BF)

    def heads_apart(x):
        return jnp.concatenate([jnp.where(low, x, zero), jnp.where(low, zero, x)], axis=0)

    def heads_joined(x):
        return jnp.where(low, x[:size], x[size:])

    context = []
    for q in range(queries):
        line = []
        for p in range(pairs):
            logits = dot(cut(k_all, q, p), heads_apart(cut(q_all, q, p)), 1, 1)
            th = jnp.tanh(logits * (shrink / SCORE_CAP))
            raised = jnp.exp(SCORE_CAP * th)
            attend = raised * (1.0 / jnp.sum(raised, 0, keepdims=True))
            scores_t[q * pairs + p] = th
            attend_t[q * pairs + p] = attend
            line.append(heads_joined(dot(attend.astype(BF), cut(v_all, q, p), 0, 0)))
        context.append(jnp.concatenate(line, axis=1))
    context = jnp.concatenate(context, axis=0).astype(BF)

    for c in copies[6 : 8]:
        c.wait()
    mixed = base + dot(context, wo_ref[...])
    inv_two = 1.0 / jnp.sqrt(lane_mean(mixed * mixed) + EPSILON)
    normed_two = mixed * inv_two
    gain_score = gain_score_ref[...]
    w_score = w_score_ref[...]
    scaled_two = normed_two * gain_score
    capped_scores = jnp.tanh(jnp.sum(scaled_two * w_score, 1, keepdims=True) * (1.0 / RANK_CAP))
    scores = RANK_CAP * capped_scores
    raised = jnp.exp(scores)
    relevance = jnp.exp(labels_ref[...].astype(F32))
    target = relevance / jnp.sum(relevance, 1, keepdims=True)
    diffs = []
    for q in range(queries):
        at = slice(size * q, size * (q + 1))
        total = jnp.sum(raised[at], 0, keepdims=True)
        wanted = as_column(target[q : q + 1])[:, 0:1]
        loss = jnp.log(total) - jnp.sum(wanted * scores[at], 0, keepdims=True)
        losses_ref[q : q + 1, :] = jnp.broadcast_to(loss, (1, 128))
        diffs.append(raised[at] / total - wanted)
    diff_raw = jnp.concatenate(diffs, axis=0) * (1.0 - capped_scores * capped_scores)
    grad_w_score = jnp.sum(scaled_two * diff_raw, 0, keepdims=True)
    diff_scaled = diff_raw * w_score
    grad_gain_score = jnp.sum(normed_two * diff_scaled, 0, keepdims=True)
    diff_normed = diff_scaled * gain_score
    diff_mixed = (diff_normed - normed_two * lane_mean(diff_normed * normed_two)) * inv_two
    diff_low = diff_mixed.astype(BF)
    diff_context = dot(diff_low, wo_ref[...], 1, 1).astype(BF)

    diff_q, diff_k, diff_v = [], [], []
    for q in range(queries):
        line_q, line_k, line_v = [], [], []
        for p in range(pairs):
            th = scores_t[q * pairs + p]
            attend = attend_t[q * pairs + p]
            split = heads_apart(cut(diff_context, q, p))
            diff_attend = dot(cut(v_all, q, p), split, 1, 1)
            line_v.append(dot(attend.astype(BF), split))
            inner = diff_attend - jnp.sum(attend * diff_attend, 0, keepdims=True)
            diff_logits = (attend * inner * (1.0 - th * th) * shrink).astype(BF)
            line_q.append(heads_joined(dot(diff_logits, cut(k_all, q, p), 0, 0)))
            line_k.append(dot(diff_logits, heads_apart(cut(q_all, q, p))))
        diff_q.append(jnp.concatenate(line_q, axis=1))
        diff_k.append(jnp.concatenate(line_k, axis=1))
        diff_v.append(jnp.concatenate(line_v, axis=1))
    diff_q = jnp.concatenate(diff_q, axis=0).astype(BF)
    diff_k = jnp.concatenate(diff_k, axis=0).astype(BF)
    diff_v = jnp.concatenate(diff_v, axis=0).astype(BF)

    first_core = core_ref[0] == 0
    first_pair = (first_input, first_input, diff_q, diff_k)
    second_pair = (first_input, context, diff_v, diff_low)
    for i in range(4):
        keep_ref[i] = jnp.where(first_core, first_pair[i], second_pair[i])
        send_ref[i] = jnp.where(first_core, second_pair[i], first_pair[i])
    sent = [
        pltpu.make_async_copy(a.at[i], b.at[i], sem.at[9 + 4 * j + i])
        for j, (a, b) in enumerate(((send_ref, send_hbm), (keep_ref, keep_hbm)))
        for i in range(4)
    ]
    for c in sent:
        c.start()

    diff_input = dot(diff_q, wq_ref[...], 1, 1) + dot(diff_k, wk_ref[...], 1, 1) + dot(diff_v, wv_ref[...], 1, 1)
    grad_gain_attn = jnp.sum(normed_one * diff_input, 0, keepdims=True)
    diff_first = diff_input * gain_attn
    diff_base = diff_mixed + (diff_first - normed_one * lane_mean(diff_first * normed_one)) * inv_one
    for q in range(queries):
        query_grad_ref[q : q + 1, :] = jnp.sum(diff_base[size * q : size * (q + 1)], 0, keepdims=True)
    for m in range(4):
        slab = diff_base[:, SLAB * m : SLAB * (m + 1)]
        held[m, :256, :] = slab[:, :128].astype(BF)
        held[m, 256:, :] = jnp.concatenate([slab[:128, 128:], slab[128:, 128:]], axis=1).astype(BF)
    for k, ref in enumerate((base_0_ref, base_1_ref, base_2_ref, base_3_ref)):
        ref[...] = held[(me + k) & 3]
    vectors = [
        v[:, 128 * t : 128 * (t + 1)]
        for v in (grad_gain_attn, grad_gain_score, grad_w_score)
        for t in range(width // 128)
    ]
    vectors_ref[...] = jnp.concatenate(vectors + [jnp.zeros((32 - len(vectors), 128), F32)], axis=0)
    for c in sent:
        c.wait()


FIRST = 48


def gradients_kernel(x_ref, y_ref, keep_hbm, other_ref, vectors_ref, *refs):
    x_refs, y_refs, (token_ref, grads, by_x, by_y, keep_ref, sem) = refs[:4], refs[4:8], refs[8:]
    token_ref[...] = jnp.zeros_like(token_ref)
    copies = [pltpu.make_async_copy(keep_hbm.at[i], keep_ref.at[i], sem.at[i]) for i in (0, 2, 1, 3)]
    for c in copies:
        c.start()
    for j in (0, 1):
        copies[2 * j].wait()
        copies[2 * j + 1].wait()
        left = jnp.concatenate([keep_ref[j], other_ref[j]], axis=0)
        right = jnp.concatenate([keep_ref[2 + j], other_ref[2 + j]], axis=0)
        grads[j] = dot(left, right, 0, 0)

    def assemble(at, carry):
        rows48 = jnp.concatenate([grads[j, pl.ds(pl.multiple_of(24 * at, 8), 24), :] for j in (0, 1)], axis=0)
        for m in range(4):
            tiles = []
            for h in range(9 * m, 9 * m + 9):
                rb, t = h // 6, h % 6
                tiles.append(rows48[8 * rb : 8 * rb + 8, 128 * t : 128 * (t + 1)])
            tiles.append(vectors_ref[8 * m : 8 * m + 8, :])
            block = jnp.concatenate(tiles, axis=0).astype(BF)
            by_x[m, at] = block[:FIRST]
            by_y[at >> 3, 8 * m + (at & 7)] = block[FIRST:]
        return carry

    lax.fori_loop(0, by_x.shape[1], assemble, 0)
    copies = []
    for j, (me, held, out_refs) in enumerate(((x_ref[0], by_x, x_refs), (y_ref[0], by_y, y_refs))):
        for k, ref in enumerate(out_refs):
            copies.append(pltpu.make_async_copy(held.at[(me + k) & 3], ref, sem.at[4 + 4 * j + k]))
            copies[-1].start()
    for c in copies:
        c.wait()


def plus(*refs):
    total = refs[0].astype(F32)
    for r in refs[1:]:
        total = total + r.astype(F32)
    return total.astype(BF)


def second_kernel(me_ref, own_hbm, b_ref, c_ref, d_ref, *refs):
    out_refs, (own_ref, total_ref, sem) = refs[:4], refs[4:]
    copy = pltpu.make_async_copy(own_hbm, own_ref, sem.at[0])
    copy.start()
    copy.wait()

    def add(i, carry):
        total_ref[i] = plus(own_ref[i], b_ref[i], c_ref[i], d_ref[i])
        return carry

    lax.fori_loop(0, total_ref.shape[0], add, 0)
    for k, ref in enumerate(out_refs):
        ref[...] = total_ref[(me_ref[0] + k) & 3]


def third_kernel(*refs):
    x_refs, y_refs, out_ref = refs[:4], refs[4:8], refs[8]
    out_ref[:, :FIRST, :] = plus(*[r[...] for r in x_refs])
    out_ref[:, FIRST:, :] = plus(*[r[...] for r in y_refs])


def last_kernel(parts_ref, out_ref):
    total = plus(*[parts_ref[i] for i in range(parts_ref.shape[0])])
    for i in range(out_ref.shape[0]):
        out_ref[i] = total


def finish_kernel(core_ref, blocks_ref, q_ref, k_ref, v_ref, o_ref, *vec_refs):
    blocks = blocks_ref[...].astype(F32)
    first_core = core_ref[0] == 0
    rows48, vectors = [], []
    for at in (0, 4):
        tiles = [blocks[at + m, 8 * i : 8 * i + 8] for m in range(4) for i in range(9)]
        rows48.append(
            jnp.concatenate([jnp.concatenate(tiles[6 * rb : 6 * rb + 6], axis=1) for rb in range(6)], axis=0)
        )
        vectors.append(jnp.concatenate([blocks[at + m, 72:] for m in range(4)], axis=0))
    for pair, refs in ((rows48[0], (q_ref, k_ref)), (rows48[1], (v_ref, o_ref))):
        for i, ref in enumerate(refs):
            ref[...] = jnp.where(first_core, pair[24 * i : 24 * i + 12], pair[24 * i + 12 : 24 * i + 24])
    vectors = vectors[0] + vectors[1]
    for i, ref in enumerate(vec_refs):
        for t in range(6):
            ref[pl.ds(128 * t, 128)] = vectors[6 * i + t]


def shape(dims, kind=BF):
    return jax.ShapeDtypeStruct(dims, kind)


def swap(x, axes):
    return lax.all_to_all(x, axes, split_axis=0, concat_axis=0, tiled=True)


def body(
    cand_item,
    list_place,
    item_table,
    query_vec,
    labels,
    query_weight,
    key_weight,
    value_weight,
    output_weight,
    gain_attn,
    gain_score,
    w_score,
):
    queries, size = cand_item.shape
    stored, slab = item_table.shape
    width = query_vec.shape[1]
    n_dp = lax.axis_size(ROWS)
    n_mp = lax.axis_size("x")
    n_yz = lax.axis_size(("y", "z"))
    slots = n_dp * CAP

    along_x = lax.axis_index("x").astype(jnp.int32).reshape(1)
    along_y = lax.axis_index("y").astype(jnp.int32).reshape(1)
    core = lax.axis_index("c").astype(jnp.int32).reshape(1)

    ids = exchange([cand_item] * 4, "x")
    lookup, own_ids = call(
        lookup_kernel,
        [pltpu.VMEM((128, list_place.shape[0]), BF), pltpu.VMEM((queries, size), jnp.int32)],
        (list_place.reshape(1, -1), cand_item), 4, 10**6, 10**6,
        [pltpu.VMEM((1, list_place.shape[0]), jnp.int32), pltpu.SemaphoreType.DMA((2,))], 0, (0, 1),
    )
    request, slot = call(
        routing_kernel,
        [shape((n_dp, CAP), jnp.int32), shape((n_mp * queries, size), jnp.int32)],
        (along_x, own_ids, *ids[1:], lookup),
        8, 3 * 10**8, 10**6, [pltpu.VMEM((n_mp, queries, size), jnp.int32)], 1,
    )
    asked = swap(request, ROWS)
    table = call(
        load_kernel, pltpu.VMEM((256, stored), BF), (item_table.T,), 4, 10**6, 2 * 10**6,
        [pltpu.SemaphoreType.DMA((2,))], 0, (0,), (request,),
    )
    found = call(
        owner_kernel, shape((n_dp, 48, 128)), (asked, inside(table)), 16, 2 * 10**9, 2 * 10**6,
        [pltpu.VMEM((n_dp // 4, 128), jnp.int32)],
    )
    fetched = swap(found, ROWS)
    pieces = call(
        pieces_kernel, [pltpu.HBM((384, 128), BF)] + [shape((384, 128))] * 3, (along_x, slot, fetched),
        16, 10**9, 2 * 10**6, [pltpu.VMEM((384, 128), BF), pltpu.SemaphoreType.DMA((1,))], 1,
    )
    rows_in = exchange(pieces, "x")
    acts = pltpu.HBM((4, queries * size, width), BF)
    outs = call(
        step_kernel,
        [shape((queries, 128), F32), shape((queries, width), F32)]
        + [shape((384, 128))] * n_mp
        + [acts] * 2
        + [shape((32, 128), F32)],
        (
            along_x, core, *rows_in, query_vec, labels,
            query_weight, key_weight, value_weight, output_weight,
            gain_attn.reshape(1, -1), gain_score.reshape(1, -1), w_score.reshape(1, -1),
        ),
        32, 4 * 10**9, 10**7,
        [
            pltpu.VMEM((n_mp, 384, 128), BF),
            pltpu.VMEM((HEADS * queries // 2, 128, 256), F32),
            pltpu.VMEM((HEADS * queries // 2, 128, 256), F32),
        ]
        + [pltpu.VMEM((width, width), BF)] * 4
        + [pltpu.VMEM((4, queries * size, width), BF)] * 2
        + [pltpu.SemaphoreType.DMA((17,))],
        2, (2, 8, 9, 10, 11),
    )
    losses, query_grad, diff_base = outs[0], outs[1], outs[2:6]
    keep, send, vectors = outs[6:]

    column_grads = exchange(diff_base, "x")

    other = lax.ppermute(send, "c", [(0, 1), (1, 0)])
    counts = (FIRST, 80 - FIRST)
    *blocks, made = call(
        gradients_kernel,
        [pltpu.HBM((n_yz, count, 128), BF) for count in counts for _ in range(4)] + [shape((8, 128), F32)],
        (along_x, along_y, keep, other, vectors), 32, 2 * 10**9, 10**7,
        [
            pltpu.VMEM((2, width, width), F32),
            pltpu.VMEM((4, n_yz, counts[0], 128), BF),
            pltpu.VMEM((4, n_yz, counts[1], 128), BF),
            pltpu.VMEM((4, queries * size, width), BF),
            pltpu.SemaphoreType.DMA((12,)),
        ],
        2, (2,), column_grads[1:],
    )
    over_first = [exchange(blocks[:4], "x"), exchange(blocks[4:], "y")]

    outgoing = call(
        slots_kernel, pltpu.HBM((n_dp, 48, 128), BF), (along_x, slot, *column_grads), 16, 10**9, 2 * 10**6,
        [pltpu.VMEM((n_mp, 384, 128), BF), pltpu.VMEM((n_dp, 48, 128), BF), pltpu.SemaphoreType.DMA((4,))], 1, awaited=(made,),
    )
    arrived = swap(outgoing, ROWS)
    landed, token = call(
        landing_kernel,
        [pltpu.HBM((slab, stored), F32), shape((8, 128), F32)],
        (asked, arrived),
        20, 2 * 10**9, 4 * 10**6, [pltpu.VMEM((slab, stored), F32), pltpu.SemaphoreType.DMA((4,))],
    )
    table_grad = landed.T

    over_second = []
    for axis, me, arrive, count in (("y", along_y, over_first[0], counts[0]), ("x", along_x, over_first[1], counts[1])):
        dims = (4, n_yz // 4, count, 128)
        blocks = call(
            second_kernel, [shape(dims[1:])] * 4, (me, *[a.reshape(dims) for a in arrive]), 8, (10**12 if axis == 'y' else 10**6), 10**7,
            [pltpu.VMEM(dims, BF), pltpu.VMEM(dims, BF), pltpu.SemaphoreType.DMA((1,))], 1, (1,),
        )
        over_second += exchange(blocks, axis)
    along = call(third_kernel, shape((n_yz // 4, 80, 128)), tuple(over_second), 8, 10**6, 10**6)
    parts = swap(after(along, arrived), "z")
    copies = call(last_kernel, shape((2 * n_mp, 80, 128)), (parts,), 4, 10**6, 10**6, awaited=(token,))
    blocks = swap(copies, ("c", "x"))
    rows = width // n_dp
    finished = call(
        finish_kernel,
        [shape((rows, width), F32)] * 4 + [shape((width,), F32)] * 3,
        (core, blocks), 4, 10**6, 10**6, (), 1,
    )
    return (
        losses[:, 0],
        table_grad,
        query_grad,
        *finished,
    )


def solution(mesh):
    grid = Mesh(mesh.devices.reshape(4, 8, 2, 4), ("y", "z", "c", "x"))
    each = P(("y", "z", "c", "x"), None)
    placed = (each, P(), P(ROWS, "x"), each, each, P(), P(), P(), P(), P(), P(), P())
    return jax.shard_map(
        body,
        mesh=grid,
        in_specs=placed,
        out_specs=(
            P(("y", "z", "c", "x")),
            P(ROWS, "x"),
            each,
            P(ROWS, None),
            P(ROWS, None),
            P(ROWS, None),
            P(ROWS, None),
            P(),
            P(),
            P(),
        ),
        check_vma=False,
    )
```

```python
import jax
import jax.numpy as jnp
from jax import lax
from jax.experimental import pallas as pl
from jax.experimental.pallas import tpu as pltpu
from jax.sharding import Mesh
from jax.sharding import PartitionSpec as P

HEADS = 12
LIST_LEN = 256
EPSILON = 1e-06
SCORE_CAP = 20.0
RANK_CAP = 30.0

ROWS = ("y", "z", "c")
CAP = 32
SLAB = 192
BF = jnp.bfloat16
F32 = jnp.float32
MIB = 1024 * 1024


def dot(a, b, ca=1, cb=0):
    return lax.dot_general(a, b, (((ca,), (cb,)), ((), ())), preferred_element_type=F32)


def iota(shape, dim):
    return lax.broadcasted_iota(jnp.int32, shape, dim)


def whole(n):
    return [pl.BlockSpec(memory_space=pltpu.VMEM)] * n


def inside(x):
    return pltpu.with_memory_space_constraint(x, pltpu.VMEM)


def stays(x):
    return pltpu.with_memory_space_constraint(x, pltpu.HBM)


def call(kernel, out_shape, args, mib, flops, size, scratch=(), scalars=0, left=(), awaited=()):
    many = isinstance(out_shape, (list, tuple))
    outs = out_shape if many else [out_shape]
    specs = [
        pl.BlockSpec(memory_space=pltpu.HBM if getattr(o, "memory_space", None) == pltpu.HBM else pltpu.VMEM)
        for o in outs
    ]
    in_specs = [pl.BlockSpec(memory_space=pltpu.SMEM)] * scalars + whole(len(args) - scalars)
    args = list(args)
    for i in left:
        in_specs[i] = pl.BlockSpec(memory_space=pltpu.HBM)
        args[i] = stays(args[i])
    in_specs += [pl.BlockSpec(memory_space=pl.ANY)] * len(awaited)

    def run(*refs):
        kernel(*refs[: len(args)], *refs[len(args) + len(awaited) :])

    return pl.pallas_call(
        run,
        out_shape=out_shape,
        in_specs=in_specs,
        out_specs=specs if many else specs[0],
        scratch_shapes=list(scratch),
        compiler_params=pltpu.CompilerParams(vmem_limit_bytes=mib * MIB),
        cost_estimate=pl.CostEstimate(flops=flops, bytes_accessed=size, transcendentals=0),
    )(*args, *awaited)


def after(x, awaited):
    return pl.pallas_call(
        lambda *refs: None,
        out_shape=shape(x.shape, x.dtype),
        in_specs=[pl.BlockSpec(memory_space=pl.ANY)] * 2,
        out_specs=pl.BlockSpec(memory_space=pl.ANY),
        input_output_aliases={0: 0},
    )(x, awaited)


def shift(x, axis, by):
    return lax.ppermute(x, axis, [(i, (i + by) % 4) for i in range(4)])


def exchange(blocks, axis):
    far = shift(blocks[2], axis, 2)
    return [blocks[0], shift(blocks[1], axis, 1), far, shift(blocks[3], axis, 3)]


def collect(me, refs, held):
    for k, ref in enumerate(refs):
        held[(me - k) & 3] = ref[...]


def low_half(shape):
    return iota(shape, len(shape) - 1) < 64


def swap_halves(t):
    return jnp.concatenate([t[..., 64:], t[..., :64]], axis=-1)


def spread_tail(t):
    t = t.astype(F32)
    other = swap_halves(t)
    low = low_half(t.shape)
    return jnp.concatenate([jnp.where(low, t, other), jnp.where(low, other, t)], axis=1)


def unpack(block):
    b, rows, _ = block.shape
    n = rows // 3
    main = block[:, : 2 * n, :].reshape(b * 2 * n, 128)
    tail = spread_tail(block[:, 2 * n :, :]).astype(BF).reshape(b * 2 * n, 128)
    return jnp.concatenate([main, tail], axis=1)


def pack(full, n):
    tail = full[:, 128:]
    tail = jnp.where(low_half((n, 128)), tail[:n], tail[n:])
    return jnp.concatenate([full[:, :128], tail], axis=0).astype(BF)


def as_column(row):
    return jnp.transpose(jnp.broadcast_to(row, (128, 128)))


def lookup_kernel(place_hbm, ids_hbm, lookup_ref, ids_ref, place_ref, sem):
    copies = [
        pltpu.make_async_copy(place_hbm, place_ref, sem.at[0]),
        pltpu.make_async_copy(ids_hbm, ids_ref, sem.at[1]),
    ]
    for c in copies:
        c.start()
    for c in copies:
        c.wait()
    place = place_ref[...]
    lists = place.shape[1]
    owner_of_list = jnp.broadcast_to(place >> 3, (128, lists))
    row = iota((128, lists), 0)
    lookup = jnp.where(owner_of_list == row, 1.0, 0.0)
    lookup = jnp.where(row == 64, jnp.broadcast_to(place & 7, (128, lists)).astype(F32), lookup)
    lookup_ref[...] = lookup.astype(BF)


def routing_kernel(me_ref, a_ref, b_ref, c_ref, d_ref, lookup_ref, request_ref, slot_ref, held):
    collect(me_ref[0], (a_ref, b_ref, c_ref, d_ref), held)
    lookup = lookup_ref[...]
    lists = lookup.shape[1]
    lane = iota((128, 128), 1)
    before = (iota((128, 128), 1) < iota((128, 128), 0)).astype(F32).astype(BF)
    carry = jnp.zeros((1, 128), F32)
    request = jnp.zeros((128, 128), F32)
    for q in range(slot_ref.shape[0]):
        ids = as_column(held[q // 2, q % 2 : q % 2 + 1, :])
        list_id = ids >> 8
        chosen = jnp.concatenate(
            [(list_id == lane + 128 * t).astype(F32).astype(BF) for t in range(lists // 128)], axis=1
        )
        found = dot(chosen, lookup, 1, 1)
        sub = jnp.sum(jnp.where(lane == 64, found, 0.0), 1, keepdims=True)
        onehot = jnp.where(lane < 64, found, 0.0)
        onehot_low = onehot.astype(BF)
        ahead = dot(before, onehot_low) + carry
        carry = carry + jnp.sum(onehot, 0, keepdims=True)
        rank = jnp.sum(onehot * ahead, 1, keepdims=True)
        owner = jnp.sum(onehot * lane.astype(F32), 1, keepdims=True)
        slot = jnp.broadcast_to(owner * CAP + rank, (128, 128))
        slot_ref[q : q + 1, :] = jnp.transpose(slot)[0:1, :].astype(jnp.int32)
        rank = rank.astype(jnp.int32)
        place_in = (ids & 255).astype(F32)
        entry = jnp.where(rank == lane, sub + 1.0, jnp.where(rank == lane - CAP, place_in, 0.0))
        request = request + dot(onehot_low, entry.astype(BF), 0, 0)
    high = request[:64, :CAP]
    low = request[:64, CAP : 2 * CAP]
    asked = (high - 1.0) * LIST_LEN + low
    request_ref[...] = jnp.where(high > 0.5, asked, -1.0).astype(jnp.int32)


def four_groups(asked):
    part = asked.shape[0] // 4
    return jnp.concatenate([asked[part * k : part * (k + 1)] for k in range(4)], axis=1)


def load_kernel(table_hbm, table_ref, sem):
    copies = [
        pltpu.make_async_copy(table_hbm, table_ref.at[pl.ds(0, SLAB)], sem.at[0]),
        pltpu.make_async_copy(table_hbm.at[pl.ds(128, 64)], table_ref.at[pl.ds(SLAB, 64)], sem.at[1]),
    ]
    for c in copies:
        c.start()
    for c in copies:
        c.wait()


def owner_kernel(asked_ref, table_ref, out_ref):
    asked = four_groups(asked_ref[...])
    part = asked.shape[0]
    stored = table_ref.shape[1]
    step = 4
    for r in range(0, part, step):
        column = jnp.concatenate([as_column(asked[r + i : r + i + 1]) for i in range(step)], axis=0)
        lane = iota((128 * step, 128), 1)
        chosen = jnp.concatenate(
            [(column == lane + 128 * t).astype(F32).astype(BF) for t in range(stored // 128)], axis=1
        )
        rows = dot(chosen, table_ref[...], 1, 1)
        for i in range(step):
            for k in range(4):
                at = 128 * i + CAP * k
                out_ref[part * k + r + i] = pack(rows[at : at + CAP], CAP // 2)


def pieces_kernel(me_ref, slot_ref, fetched_ref, own_hbm, *refs):
    out_refs, own_ref, sem = refs[:3], refs[3], refs[4]
    fetched = unpack(fetched_ref[...])
    slots = fetched.shape[0]
    copy = pltpu.make_async_copy(own_ref, own_hbm, sem.at[0])
    for k, out_ref in enumerate((own_ref, *out_refs)):
        m = (me_ref[0] + k) & 3
        column = jnp.concatenate([as_column(slot_ref[pl.ds(2 * m + i, 1), :]) for i in (0, 1)], axis=0)
        lane = iota((256, 128), 1)
        chosen = jnp.concatenate(
            [(column == lane + 128 * t).astype(F32).astype(BF) for t in range(slots // 128)], axis=1
        )
        out_ref[...] = pack(dot(chosen, fetched), 128)
        if k == 0:
            copy.start()
    copy.wait()


def slots_kernel(me_ref, slot_ref, a_ref, b_ref, c_ref, d_ref, out_hbm, held, out_ref, sem):
    collect(me_ref[0], (a_ref, b_ref, c_ref, d_ref), held)
    grads = unpack(held[...])
    groups = out_ref.shape[0]
    step = 16 * CAP
    copies = []
    for r in range(0, groups * CAP, step):
        row = iota((step, 128), 0) + r
        chosen = jnp.concatenate(
            [
                (jnp.broadcast_to(slot_ref[q : q + 1, :], (step, 128)) == row).astype(F32).astype(BF)
                for q in range(slot_ref.shape[0])
            ],
            axis=1,
        )
        rows = dot(chosen, grads)
        for i in range(16):
            out_ref[r // CAP + i] = pack(rows[CAP * i : CAP * (i + 1)], CAP // 2)
        at = pl.ds(r // CAP, 16)
        copies.append(pltpu.make_async_copy(out_ref.at[at], out_hbm.at[at], sem.at[r // step]))
        copies[-1].start()
    for c in copies:
        c.wait()


def landing_kernel(asked_ref, arrived_ref, out_hbm, token_ref, out_ref, sem):
    token_ref[...] = jnp.zeros_like(token_ref)
    arrived = unpack(arrived_ref[...])
    stored = out_ref.shape[1]
    slots = arrived.shape[0]
    asked = four_groups(asked_ref[...])
    part = asked.shape[0]
    columns = [as_column(asked[r : r + 1]) for r in range(part)]
    column = jnp.concatenate(
        [columns[g % part][CAP * (g // part) : CAP * (g // part + 1)] for g in range(4 * part)], axis=0
    )
    step = 512
    copies = []
    lane = iota((slots, 128), 1)
    for r in range(0, stored, step):
        chosen = jnp.concatenate(
            [(column == lane + (r + 128 * t)).astype(F32).astype(BF) for t in range(step // 128)], axis=1
        )
        out_ref[:, r : r + step] = dot(arrived, chosen, 0, 0)[:SLAB]
        at = pl.ds(r, step)
        copies.append(pltpu.make_async_copy(out_ref.at[:, at], out_hbm.at[:, at], sem.at[r // step]))
        copies[-1].start()
    for c in copies:
        c.wait()


def lane_mean(x):
    return jnp.sum(x, 1, keepdims=True) * (1.0 / x.shape[1])


def step_kernel(
    me_ref,
    core_ref,
    a_hbm,
    b_ref,
    c_ref,
    d_ref,
    query_ref,
    labels_ref,
    wq_ref,
    wk_hbm,
    wv_hbm,
    wo_hbm,
    gain_attn_ref,
    gain_score_ref,
    w_score_ref,
    losses_ref,
    query_grad_ref,
    base_0_ref,
    base_1_ref,
    base_2_ref,
    base_3_ref,
    keep_hbm,
    send_hbm,
    vectors_ref,
    held,
    scores_t,
    attend_t,
    wk_ref,
    wv_ref,
    wo_ref,
    keep_ref,
    send_ref,
    sem,
):
    me = me_ref[0]
    own = pltpu.make_async_copy(a_hbm, held.at[me], sem.at[8])
    own.start()
    sources = (wk_hbm, wv_hbm, wo_hbm)
    weights = (wk_ref, wv_ref, wo_ref)
    half = wq_ref.shape[0] // 2
    copies = [
        pltpu.make_async_copy(a.at[pl.ds(half * h, half)], b.at[pl.ds(half * h, half)], sem.at[2 * i + h])
        for i, (a, b) in enumerate(zip(sources, weights))
        for h in (0, 1)
    ]
    for c in copies:
        c.start()
    for k, ref in ((1, b_ref), (2, c_ref), (3, d_ref)):
        held[(me - k) & 3] = ref[...]
    own.wait()
    queries, width = query_ref.shape
    size = 128
    head = width // HEADS
    pairs = HEADS // 2
    shrink = head ** (-0.5)
    low = low_half((size, 128))

    parts = []
    for m in range(4):
        main = held[m, :256, :].astype(F32)
        tail = held[m, 256:, :].astype(F32)
        parts += [main, jnp.concatenate([tail[:, :64], tail[:, 64:]], axis=0)]
    rows_in = jnp.concatenate(parts, axis=1)
    vecs = query_ref[...].astype(F32)
    vecs = jnp.concatenate([jnp.broadcast_to(vecs[q : q + 1], (size, width)) for q in range(queries)], axis=0)
    base = rows_in + vecs
    inv_one = 1.0 / jnp.sqrt(lane_mean(base * base) + EPSILON)
    normed_one = base * inv_one
    gain_attn = gain_attn_ref[...]
    first_input = (normed_one * gain_attn).astype(BF)
    q_all = dot(first_input, wq_ref[...]).astype(BF)
    for c in copies[0 : 2]:
        c.wait()
    k_all = dot(first_input, wk_ref[...]).astype(BF)
    for c in copies[2 : 4]:
        c.wait()
    v_all = dot(first_input, wv_ref[...]).astype(BF)

    def cut(x, q, p):
        return x[size * q : size * (q + 1), 128 * p : 128 * (p + 1)]

    zero = jnp.zeros((size, 128), BF)

    def heads_apart(x):
        return jnp.concatenate([jnp.where(low, x, zero), jnp.where(low, zero, x)], axis=0)

    def heads_joined(x):
        return jnp.where(low, x[:size], x[size:])

    context = []
    for q in range(queries):
        line = []
        for p in range(pairs):
            logits = dot(cut(k_all, q, p), heads_apart(cut(q_all, q, p)), 1, 1)
            th = jnp.tanh(logits * (shrink / SCORE_CAP))
            raised = jnp.exp(SCORE_CAP * th)
            attend = raised * (1.0 / jnp.sum(raised, 0, keepdims=True))
            scores_t[q * pairs + p] = th
            attend_t[q * pairs + p] = attend
            line.append(heads_joined(dot(attend.astype(BF), cut(v_all, q, p), 0, 0)))
        context.append(jnp.concatenate(line, axis=1))
    context = jnp.concatenate(context, axis=0).astype(BF)

    for c in copies[4 : 6]:
        c.wait()
    mixed = base + dot(context, wo_ref[...])
    inv_two = 1.0 / jnp.sqrt(lane_mean(mixed * mixed) + EPSILON)
    normed_two = mixed * inv_two
    gain_score = gain_score_ref[...]
    w_score = w_score_ref[...]
    scaled_two = normed_two * gain_score
    capped_scores = jnp.tanh(jnp.sum(scaled_two * w_score, 1, keepdims=True) * (1.0 / RANK_CAP))
    scores = RANK_CAP * capped_scores
    raised = jnp.exp(scores)
    relevance = jnp.exp(labels_ref[...].astype(F32))
    target = relevance / jnp.sum(relevance, 1, keepdims=True)
    diffs = []
    for q in range(queries):
        at = slice(size * q, size * (q + 1))
        total = jnp.sum(raised[at], 0, keepdims=True)
        wanted = as_column(target[q : q + 1])[:, 0:1]
        loss = jnp.log(total) - jnp.sum(wanted * scores[at], 0, keepdims=True)
        losses_ref[q : q + 1, :] = jnp.broadcast_to(loss, (1, 128))
        diffs.append(raised[at] / total - wanted)
    diff_raw = jnp.concatenate(diffs, axis=0) * (1.0 - capped_scores * capped_scores)
    grad_w_score = jnp.sum(scaled_two * diff_raw, 0, keepdims=True)
    diff_scaled = diff_raw * w_score
    grad_gain_score = jnp.sum(normed_two * diff_scaled, 0, keepdims=True)
    diff_normed = diff_scaled * gain_score
    diff_mixed = (diff_normed - normed_two * lane_mean(diff_normed * normed_two)) * inv_two
    diff_low = diff_mixed.astype(BF)
    diff_context = dot(diff_low, wo_ref[...], 1, 1).astype(BF)

    diff_q, diff_k, diff_v = [], [], []
    for q in range(queries):
        line_q, line_k, line_v = [], [], []
        for p in range(pairs):
            th = scores_t[q * pairs + p]
            attend = attend_t[q * pairs + p]
            split = heads_apart(cut(diff_context, q, p))
            diff_attend = dot(cut(v_all, q, p), split, 1, 1)
            line_v.append(dot(attend.astype(BF), split))
            inner = diff_attend - jnp.sum(attend * diff_attend, 0, keepdims=True)
            diff_logits = (attend * inner * (1.0 - th * th) * shrink).astype(BF)
            line_q.append(heads_joined(dot(diff_logits, cut(k_all, q, p), 0, 0)))
            line_k.append(dot(diff_logits, heads_apart(cut(q_all, q, p))))
        diff_q.append(jnp.concatenate(line_q, axis=1))
        diff_k.append(jnp.concatenate(line_k, axis=1))
        diff_v.append(jnp.concatenate(line_v, axis=1))
    diff_q = jnp.concatenate(diff_q, axis=0).astype(BF)
    diff_k = jnp.concatenate(diff_k, axis=0).astype(BF)
    diff_v = jnp.concatenate(diff_v, axis=0).astype(BF)

    first_core = core_ref[0] == 0
    first_pair = (first_input, first_input, diff_q, diff_k)
    second_pair = (first_input, context, diff_v, diff_low)
    for i in range(4):
        keep_ref[i] = jnp.where(first_core, first_pair[i], second_pair[i])
        send_ref[i] = jnp.where(first_core, second_pair[i], first_pair[i])
    sent = [
        pltpu.make_async_copy(a.at[i], b.at[i], sem.at[9 + 4 * j + i])
        for j, (a, b) in enumerate(((send_ref, send_hbm), (keep_ref, keep_hbm)))
        for i in range(4)
    ]
    for c in sent:
        c.start()

    diff_input = dot(diff_q, wq_ref[...], 1, 1) + dot(diff_k, wk_ref[...], 1, 1) + dot(diff_v, wv_ref[...], 1, 1)
    grad_gain_attn = jnp.sum(normed_one * diff_input, 0, keepdims=True)
    diff_first = diff_input * gain_attn
    diff_base = diff_mixed + (diff_first - normed_one * lane_mean(diff_first * normed_one)) * inv_one
    for q in range(queries):
        query_grad_ref[q : q + 1, :] = jnp.sum(diff_base[size * q : size * (q + 1)], 0, keepdims=True)
    for m in range(4):
        slab = diff_base[:, SLAB * m : SLAB * (m + 1)]
        held[m, :256, :] = slab[:, :128].astype(BF)
        held[m, 256:, :] = jnp.concatenate([slab[:128, 128:], slab[128:, 128:]], axis=1).astype(BF)
    for k, ref in enumerate((base_0_ref, base_1_ref, base_2_ref, base_3_ref)):
        ref[...] = held[(me + k) & 3]
    vectors = [
        v[:, 128 * t : 128 * (t + 1)]
        for v in (grad_gain_attn, grad_gain_score, grad_w_score)
        for t in range(width // 128)
    ]
    vectors_ref[...] = jnp.concatenate(vectors + [jnp.zeros((32 - len(vectors), 128), F32)], axis=0)
    for c in sent:
        c.wait()


def gradients_kernel(me_ref, keep_hbm, other_ref, vectors_ref, *refs):
    out_refs, (token_ref, grads, held, keep_ref, sem) = refs[:4], refs[4:]
    token_ref[...] = jnp.zeros_like(token_ref)
    loads = [pltpu.make_async_copy(keep_hbm.at[i], keep_ref.at[i], sem.at[i]) for i in (0, 2, 1, 3)]
    for c in loads:
        c.start()
    grads[0] = dot(other_ref[0], other_ref[2], 0, 0)
    for c in loads:
        c.wait()
    grads[0] = grads[0] + dot(keep_ref[0], keep_ref[2], 0, 0)
    left = jnp.concatenate([keep_ref[1], other_ref[1]], axis=0)
    right = jnp.concatenate([keep_ref[3], other_ref[3]], axis=0)
    grads[1] = dot(left, right, 0, 0)

    def assemble(at, carry):
        rows48 = jnp.concatenate([grads[j, pl.ds(pl.multiple_of(24 * at, 8), 24), :] for j in (0, 1)], axis=0)
        for m in range(4):
            tiles = []
            for h in range(9 * m, 9 * m + 9):
                rb, t = h // 6, h % 6
                tiles.append(rows48[8 * rb : 8 * rb + 8, 128 * t : 128 * (t + 1)])
            tiles.append(vectors_ref[8 * m : 8 * m + 8, :])
            held[m, at] = jnp.concatenate(tiles, axis=0).astype(BF)
        return carry

    lax.fori_loop(0, held.shape[1], assemble, 0)
    own = pltpu.make_async_copy(held.at[me_ref[0]], out_refs[0], sem.at[4])
    own.start()
    for k in (1, 2, 3):
        out_refs[k][...] = held[(me_ref[0] + k) & 3]
    own.wait()


def plus(*refs):
    total = refs[0].astype(F32)
    for r in refs[1:]:
        total = total + r.astype(F32)
    return total.astype(BF)


def sum_kernel(own_hbm, b_ref, c_ref, d_ref, out_hbm, own_ref, out_ref, sem):
    n = own_ref.shape[0] // 4
    loads = [
        pltpu.make_async_copy(own_hbm.at[pl.ds(n * i, n)], own_ref.at[pl.ds(n * i, n)], sem.at[i]) for i in range(4)
    ]
    for c in loads:
        c.start()
    copies = []
    for i in range(4):
        at = pl.ds(n * i, n)
        loads[i].wait()
        out_ref[n * i : n * (i + 1)] = plus(*[r[n * i : n * (i + 1)] for r in (own_ref, b_ref, c_ref, d_ref)])
        copies.append(pltpu.make_async_copy(out_ref.at[at], out_hbm.at[at], sem.at[4 + i]))
        copies[-1].start()
    for c in copies:
        c.wait()


def last_kernel(parts_ref, out_ref):
    total = plus(*[parts_ref[i] for i in range(parts_ref.shape[0])])
    for i in range(out_ref.shape[0]):
        out_ref[i] = total


def finish_kernel(core_ref, blocks_ref, q_ref, k_ref, v_ref, o_ref, *vec_refs):
    blocks = blocks_ref[...].astype(F32)
    first_core = core_ref[0] == 0
    rows48, vectors = [], []
    for at in (0, 4):
        tiles = [blocks[at + m, 8 * i : 8 * i + 8] for m in range(4) for i in range(9)]
        rows48.append(
            jnp.concatenate([jnp.concatenate(tiles[6 * rb : 6 * rb + 6], axis=1) for rb in range(6)], axis=0)
        )
        vectors.append(jnp.concatenate([blocks[at + m, 72:] for m in range(4)], axis=0))
    for pair, refs in ((rows48[0], (q_ref, k_ref)), (rows48[1], (v_ref, o_ref))):
        for i, ref in enumerate(refs):
            ref[...] = jnp.where(first_core, pair[24 * i : 24 * i + 12], pair[24 * i + 12 : 24 * i + 24])
    vectors = vectors[0] + vectors[1]
    for i, ref in enumerate(vec_refs):
        for t in range(6):
            ref[pl.ds(128 * t, 128)] = vectors[6 * i + t]


def shape(dims, kind=BF):
    return jax.ShapeDtypeStruct(dims, kind)


def swap(x, axes):
    return lax.all_to_all(x, axes, split_axis=0, concat_axis=0, tiled=True)


def body(
    cand_item,
    list_place,
    item_table,
    query_vec,
    labels,
    query_weight,
    key_weight,
    value_weight,
    output_weight,
    gain_attn,
    gain_score,
    w_score,
):
    queries, size = cand_item.shape
    stored, slab = item_table.shape
    width = query_vec.shape[1]
    n_dp = lax.axis_size(ROWS)
    n_mp = lax.axis_size("x")
    n_yz = lax.axis_size(("y", "z"))
    slots = n_dp * CAP

    along_x = lax.axis_index("x").astype(jnp.int32).reshape(1)
    core = lax.axis_index("c").astype(jnp.int32).reshape(1)

    ids = exchange([cand_item] * 4, "x")
    lookup, own_ids = call(
        lookup_kernel,
        [pltpu.VMEM((128, list_place.shape[0]), BF), pltpu.VMEM((queries, size), jnp.int32)],
        (list_place.reshape(1, -1), cand_item), 4, 10**6, 10**6,
        [pltpu.VMEM((1, list_place.shape[0]), jnp.int32), pltpu.SemaphoreType.DMA((2,))], 0, (0, 1),
    )
    request, slot = call(
        routing_kernel,
        [shape((n_dp, CAP), jnp.int32), shape((n_mp * queries, size), jnp.int32)],
        (along_x, own_ids, *ids[1:], lookup),
        8, 3 * 10**8, 10**6, [pltpu.VMEM((n_mp, queries, size), jnp.int32)], 1,
    )
    asked = swap(request, ROWS)
    table = call(
        load_kernel, pltpu.VMEM((256, stored), BF), (item_table.T,), 4, 10**6, 2 * 10**6,
        [pltpu.SemaphoreType.DMA((2,))], 0, (0,), (request,),
    )
    found = call(
        owner_kernel, shape((n_dp, 48, 128)), (asked, inside(table)), 16, 2 * 10**9, 2 * 10**6
    )
    fetched = swap(found, ROWS)
    pieces = call(
        pieces_kernel, [pltpu.HBM((384, 128), BF)] + [shape((384, 128))] * 3, (along_x, slot, fetched),
        16, 10**9, 2 * 10**6, [pltpu.VMEM((384, 128), BF), pltpu.SemaphoreType.DMA((1,))], 1,
    )
    rows_in = exchange(pieces, "x")
    acts = pltpu.HBM((4, queries * size, width), BF)
    outs = call(
        step_kernel,
        [shape((queries, 128), F32), shape((queries, width), F32)]
        + [shape((384, 128))] * n_mp
        + [acts] * 2
        + [shape((32, 128), F32)],
        (
            along_x, core, *rows_in, query_vec, labels,
            query_weight, key_weight, value_weight, output_weight,
            gain_attn.reshape(1, -1), gain_score.reshape(1, -1), w_score.reshape(1, -1),
        ),
        32, 4 * 10**9, 10**7,
        [
            pltpu.VMEM((n_mp, 384, 128), BF),
            pltpu.VMEM((HEADS * queries // 2, 128, 256), F32),
            pltpu.VMEM((HEADS * queries // 2, 128, 256), F32),
        ]
        + [pltpu.VMEM((width, width), BF)] * 3
        + [pltpu.VMEM((4, queries * size, width), BF)] * 2
        + [pltpu.SemaphoreType.DMA((17,))],
        2, (2, 9, 10, 11),
    )
    losses, query_grad, diff_base = outs[0], outs[1], outs[2:6]
    keep, send, vectors = outs[6:]

    column_grads = exchange(diff_base, "x")

    other = lax.ppermute(send, "c", [(0, 1), (1, 0)])
    block = shape((n_yz, 80, 128))
    *blocks, made = call(
        gradients_kernel, [pltpu.HBM(block.shape, BF)] + [block] * 3 + [shape((8, 128), F32)], (along_x, keep, other, vectors), 32, 2 * 10**9, 10**7,
        [
            pltpu.VMEM((2, width, width), F32),
            pltpu.VMEM((n_mp, n_yz, 80, 128), BF),
            pltpu.VMEM((4, queries * size, width), BF),
            pltpu.SemaphoreType.DMA((5,)),
        ],
        1, (1,), column_grads[1:],
    )
    arrive = exchange(blocks, "x")

    outgoing = call(
        slots_kernel, pltpu.HBM((n_dp, 48, 128), BF), (along_x, slot, *column_grads), 16, 10**9, 2 * 10**6,
        [pltpu.VMEM((n_mp, 384, 128), BF), pltpu.VMEM((n_dp, 48, 128), BF), pltpu.SemaphoreType.DMA((4,))], 1, awaited=(made,),
    )
    arrived = swap(outgoing, ROWS)
    landed, token = call(
        landing_kernel,
        [pltpu.HBM((slab, stored), F32), shape((8, 128), F32)],
        (asked, arrived),
        20, 2 * 10**9, 4 * 10**6, [pltpu.VMEM((slab, stored), F32), pltpu.SemaphoreType.DMA((4,))],
    )
    table_grad = landed.T

    over_x = call(
        sum_kernel, pltpu.HBM(block.shape, BF), tuple(arrive), 8, 10**12, 10**7,
        [pltpu.VMEM(block.shape, BF), pltpu.VMEM(block.shape, BF), pltpu.SemaphoreType.DMA((8,))], 0, (0,),
    )
    parts = swap(after(over_x, arrived), ("y", "z"))
    copies = call(last_kernel, shape((2 * n_mp, 80, 128)), (parts,), 4, 10**6, 10**6, awaited=(token,))
    blocks = swap(copies, ("c", "x"))
    rows = width // n_dp
    finished = call(
        finish_kernel,
        [shape((rows, width), F32)] * 4 + [shape((width,), F32)] * 3,
        (core, blocks), 4, 10**6, 10**6, (), 1,
    )
    return (
        losses[:, 0],
        table_grad,
        query_grad,
        *finished,
    )


def solution(mesh):
    grid = Mesh(mesh.devices.reshape(4, 8, 2, 4), ("y", "z", "c", "x"))
    each = P(("y", "z", "c", "x"), None)
    placed = (each, P(), P(ROWS, "x"), each, each, P(), P(), P(), P(), P(), P(), P())
    return jax.shard_map(
        body,
        mesh=grid,
        in_specs=placed,
        out_specs=(
            P(("y", "z", "c", "x")),
            P(ROWS, "x"),
            each,
            P(ROWS, None),
            P(ROWS, None),
            P(ROWS, None),
            P(ROWS, None),
            P(),
            P(),
            P(),
        ),
        check_vma=False,
    )
```
